32 devices in a mesh: graph: 4 (over z), config: 8 (over y, x, core).
Axes of the slice: x: 2, y: 2, z: 4, core: 2. Of those that a mesh axis runs over, the one named last changes fastest.
Arguments:
- features: bfloat16 [16, 2048, 128], P('config', 'graph'), may hold values from -6 to 6
- cotangent: bfloat16 [16, 2048, 128], P(None, ('graph', 'config')), may hold values from -6 to 6
- sage_weight: bfloat16 [2, 128, 128], replicated, may hold values from -0.5 to 0.5
- attn_weight: bfloat16 [4, 128, 128], replicated, may hold values from -0.5 to 0.5
- tile_vals: bfloat16 [48, 128, 128], P('graph'), may hold values from -0.375 to 0.375
- tile_dst: int32 [48], P('graph'), may hold values from 0 to 3
- tile_src: int32 [48], P('graph'), may hold values from 0 to 3
- tile_count: int32 [4], P('graph'), may hold values from 3 to 12, as said below
- hub_ids: int32 [32], P('graph'), may hold values from 0 to 2047, as said below
- hub_weight: bfloat16 [2048, 32], P('graph'), may hold values from -1 to 1
Outputs:
- layer_out: bfloat16 [16, 2048, 128], P(None, ('graph', 'config'))
- grad_features: bfloat16 [16, 2048, 128], P('config', 'graph')
- grad_weights: float32 [4, 6, 128, 128], P('graph')
The draws below stay inside these ranges and needn't reach their ends.
Inputs may be any that keep to these rules, and one draw needn't show every extreme that they name: Slot t of slab g (t counted within the slab) is live when t < tile_count[g]; some slab has all 12 slots live. `hub_ids`: entries g * 8 to (g+1) * 8 - 1 are distinct nodes of slab g.
All inputs are finite; a program needn't handle non-finite values.
Results may differ from the reference program's by a relative error of at most 0.024.
Values may be sent and summed in bfloat16 or wider, within the bound.
No kernel may reach another device: no remote copies, remote signals or barrier semaphores. Data moves between devices by JAX's collectives and lax.ppermute only.
A program may use at most 64 MiB of HBM per device.

```python
import math
import jax
import jax.numpy as jnp
from jax import lax

F = 128
HEADS = 4
TILE = 128
NODE_DEV = 512
HUB_DEV = 8
TILES_DEV = 12
NODES = 2048
LAYOUTS = 16
TILES = 48
HUB = 32
SHARE = 64
N_GRAPH = 4
N_CONFIG = 8


def draw_tile_count(key, part):
    first_key, second_key = jax.random.split(key)
    counts = jax.random.randint(first_key, (N_GRAPH,), TILES_DEV // 4, TILES_DEV + 1)
    busiest = jax.random.randint(second_key, (), 0, N_GRAPH)
    filled = jnp.where(jnp.arange(N_GRAPH) == busiest, TILES_DEV, counts)
    return filled.astype(jnp.int32)


def draw_hub_ids(key, part):
    slab_keys = jax.random.split(key, N_GRAPH)
    picks = jax.vmap(lambda slab_key: jax.random.permutation(slab_key, NODE_DEV)[:HUB_DEV])(slab_keys)
    offsets = jnp.arange(N_GRAPH, dtype=jnp.int32)[:, None] * NODE_DEV
    return (picks.astype(jnp.int32) + offsets).reshape(-1).astype(jnp.int32)


def with_ends(entries, own_key, least, largest):
    longest = entries.shape.index(max(entries.shape))
    spots = []
    for shift in (0, 1):
        where = [jax.random.randint(jax.random.fold_in(own_key, axis), (), 0, length) for axis, length in enumerate(entries.shape)]
        where[longest] = (where[longest] + shift) % entries.shape[longest]
        spots.append(tuple(where))
    return entries.at[spots[0]].set(least).at[spots[1]].set(largest)


def level_of(stream_key, dims, cuts, least, largest):
    def one(dim, shards_of):
        heights = jax.random.uniform(jax.random.fold_in(jax.random.fold_in(stream_key, 6), dim), (shards_of,), jnp.float32, least / len(cuts), largest / len(cuts))
        return jnp.repeat(jnp.exp(heights), dims[dim] // shards_of).reshape((-1,) + (1,) * (len(dims) - dim - 1))

    gain = one(*cuts[0])
    for cut in cuts[1:]:
        gain = gain * one(*cut)
    return gain


def normal_values(own_key, dims, deviation, bound, cuts=(), kind=jnp.bfloat16):
    gain = level_of(own_key, dims, cuts, -0.22, 0.18) if cuts else 1.0
    drawn = jax.random.normal(own_key, dims, jnp.float32) * deviation * gain
    return jnp.minimum(jnp.maximum(drawn, -bound), bound).astype(kind)


def setup_inputs(seed: int = 0) -> dict:
    key_of = jax.random.split(jax.random.key(seed), 11)
    return {
        "features": normal_values(key_of[0], (LAYOUTS, NODES, F), 1.0, 6.0, ((0, 8), (1, 4))),
        "cotangent": normal_values(key_of[1], (LAYOUTS, NODES, F), 1.0, 6.0, ((1, 32),)),
        "sage_weight": normal_values(key_of[2], (2, F, F), F ** -0.5, 0.5),
        "attn_weight": normal_values(key_of[3], (4, F, F), F ** -0.5, 0.5),
        "tile_vals": normal_values(key_of[4], (TILES, TILE, TILE), (2 * TILE) ** -0.5, 0.375, ((0, 4),)),
        "tile_dst": with_ends(jax.random.randint(key_of[5], (TILES,), 0, NODE_DEV // TILE), jax.random.fold_in(key_of[5], 1), 0, (NODE_DEV // TILE) - 1).astype(jnp.int32),
        "tile_src": with_ends(jax.random.randint(key_of[6], (TILES,), 0, NODE_DEV // TILE), jax.random.fold_in(key_of[6], 1), 0, (NODE_DEV // TILE) - 1).astype(jnp.int32),
        "tile_count": draw_tile_count(jax.random.fold_in(key_of[10], 71), 0),
        "hub_ids": draw_hub_ids(jax.random.fold_in(key_of[10], 71), 0),
        "hub_weight": normal_values(key_of[9], (NODES, HUB), HUB ** -0.5, 1.0, ((0, 4),)),
    }


CAP = 20.0

def attend(queries, key_rows, value_rows):
    layout_count, node_count, feature_width = queries.shape
    head_size = feature_width // HEADS
    split = (layout_count, node_count, HEADS, head_size)
    query_b = queries.reshape(split)
    key_b = key_rows.reshape(split)
    value_b = value_rows.reshape(split)
    scores = jnp.einsum('lkhd,mkhd->khlm', query_b, key_b, preferred_element_type=jnp.float32) / math.sqrt(head_size)
    capped = CAP * jnp.tanh(scores / CAP)
    weights = jnp.exp(capped)
    attention = weights / lax.optimization_barrier(jnp.sum(weights, axis=-1, keepdims=True))
    attention = attention.astype(value_b.dtype)
    mixture = jnp.einsum('khlm,mkhd->lkhd', attention, value_b, preferred_element_type=jnp.float32)
    return mixture.reshape(layout_count, node_count, feature_width).astype(queries.dtype)

def project(flat_rows, weight):
    return jnp.dot(flat_rows, weight, preferred_element_type=jnp.float32)

def project_back(flat_rows, weight):
    return jnp.dot(flat_rows, weight.T, preferred_element_type=jnp.float32)

def outer_sum(left_rows, right_rows):
    return jnp.dot(left_rows.T, right_rows, preferred_element_type=jnp.float32)

def sage_forward(feats, aggregate, sage_weight):
    shaped = feats.shape
    width_f = shaped[-1]
    pre_acts = project(feats.reshape(-1, width_f), sage_weight[0]) + project(aggregate.reshape(-1, width_f), sage_weight[1])
    hidden = jax.nn.silu(pre_acts).astype(jnp.bfloat16)
    return (pre_acts.reshape(shaped), hidden.reshape(shaped))

def node_forward(hidden, attn_weight):
    shaped = hidden.shape
    width_f = shaped[-1]
    three = (shaped[0], -1, width_f)
    flat_hidden = hidden.reshape(-1, width_f)
    queries = project(flat_hidden, attn_weight[0]).astype(jnp.bfloat16)
    key_rows = project(flat_hidden, attn_weight[1]).astype(jnp.bfloat16)
    value_rows = project(flat_hidden, attn_weight[2]).astype(jnp.bfloat16)
    mixture = attend(queries.reshape(three), key_rows.reshape(three), value_rows.reshape(three))
    output = (flat_hidden.astype(jnp.float32) + project(mixture.reshape(-1, width_f), attn_weight[3])).astype(jnp.bfloat16)
    return (output.reshape(shaped), queries.reshape(shaped), key_rows.reshape(shaped), value_rows.reshape(shaped), mixture.reshape(shaped))

def node_backward(cot_rows, hidden, queries, key_rows, value_rows, mixture, attn_weight):
    shaped = hidden.shape
    width_f = shaped[-1]
    three = (shaped[0], -1, width_f)
    flat_cot = cot_rows.reshape(-1, width_f)
    grad_mix = project_back(flat_cot, attn_weight[3]).astype(jnp.bfloat16)
    grad_wo = outer_sum(mixture.reshape(-1, width_f), flat_cot)
    unused, pullback = jax.vjp(attend, queries.reshape(three), key_rows.reshape(three), value_rows.reshape(three))
    grad_q, grad_k, grad_v = pullback(grad_mix.reshape(three))
    flat_q = grad_q.reshape(-1, width_f)
    flat_k = grad_k.reshape(-1, width_f)
    flat_v = grad_v.reshape(-1, width_f)
    grad_hidden = (flat_cot.astype(jnp.float32) + project_back(flat_q, attn_weight[0]) + project_back(flat_k, attn_weight[1]) + project_back(flat_v, attn_weight[2])).astype(jnp.bfloat16)
    flat_hidden = hidden.reshape(-1, width_f)
    grads = jnp.stack([outer_sum(flat_hidden, flat_q), outer_sum(flat_hidden, flat_k), outer_sum(flat_hidden, flat_v), grad_wo])
    return (grad_hidden.reshape(shaped), grads)

def sage_backward(grad_hidden, pre_acts, feats, aggregate, sage_weight):
    shaped = feats.shape
    width_f = shaped[-1]
    flat_pre = pre_acts.reshape(-1, width_f)
    sigmoid_pre = jax.nn.sigmoid(flat_pre)
    grad_pre = (grad_hidden.reshape(-1, width_f).astype(jnp.float32) * sigmoid_pre * (1.0 + flat_pre * (1.0 - sigmoid_pre))).astype(jnp.bfloat16)
    grads = jnp.stack([outer_sum(feats.reshape(-1, width_f), grad_pre), outer_sum(aggregate.reshape(-1, width_f), grad_pre)])
    grad_self = project_back(grad_pre, sage_weight[0]).astype(jnp.bfloat16).reshape(shaped)
    grad_agg = project_back(grad_pre, sage_weight[1]).astype(jnp.bfloat16).reshape(shaped)
    return (grad_self, grad_agg, grads)

def reference(features, cotangent, sage_weight, attn_weight, tile_vals, tile_dst, tile_src, tile_count, hub_ids, hub_weight):
    slab_count = N_GRAPH
    span_count = N_GRAPH * N_CONFIG
    hub_rows = features[:, hub_ids]
    by_slab = features.reshape(LAYOUTS, slab_count, NODE_DEV, F).transpose(1, 0, 2, 3)
    tiles_slab = tile_vals.reshape(slab_count, TILES_DEV, TILE, TILE)
    dst_slab = tile_dst.reshape(slab_count, TILES_DEV)
    src_slab = tile_src.reshape(slab_count, TILES_DEV)
    hubw_slab = hub_weight.reshape(slab_count, NODE_DEV, HUB)
    block_ids = jnp.arange(NODE_DEV // TILE, dtype=jnp.int32)[:, None]

    def placement(targets, count):
        live = (jnp.arange(TILES_DEV, dtype=jnp.int32) < count).astype(jnp.float32)
        return (targets[None, :] == block_ids).astype(jnp.float32) * live[None, :]

    def forward_slab(packed):
        feats, tiles, dst, src, count, hubw = packed
        gathered = feats.reshape(LAYOUTS, -1, TILE, F)[:, src]
        products = jnp.einsum('tij,ltjf->ltif', tiles.astype(jnp.float32), gathered.astype(jnp.float32), precision=lax.Precision.HIGHEST)
        tile_sum = jnp.einsum('bt,ltif->lbif', placement(dst, count), products, precision=lax.Precision.HIGHEST).reshape(LAYOUTS, NODE_DEV, F)
        hub_sum = jnp.einsum('nj,ljf->lnf', hubw.astype(jnp.float32), hub_rows.astype(jnp.float32), precision=lax.Precision.HIGHEST)
        aggregate = (tile_sum + hub_sum).astype(jnp.bfloat16)
        pre_acts, hidden = sage_forward(feats, aggregate, sage_weight)
        return (aggregate, hidden)
    aggregates, hiddens = lax.map(forward_slab, (by_slab, tiles_slab, dst_slab, src_slab, tile_count, hubw_slab))
    hidden_all = hiddens.transpose(1, 0, 2, 3).reshape(LAYOUTS, span_count, SHARE, F).transpose(1, 0, 2, 3)
    cot_all = cotangent.reshape(LAYOUTS, span_count, SHARE, F).transpose(1, 0, 2, 3)

    def node_span(packed):
        hidden, cot_rows = packed
        output, queries, key_rows, value_rows, mixture = node_forward(hidden, attn_weight)
        grad_hidden, grads = node_backward(cot_rows, hidden, queries, key_rows, value_rows, mixture, attn_weight)
        return (output, grad_hidden, grads)
    outputs, grad_hiddens, attn_parts = lax.map(node_span, (hidden_all, cot_all))
    layer_out = outputs.transpose(1, 0, 2, 3).reshape(LAYOUTS, NODES, F)
    grad_slab = grad_hiddens.transpose(1, 0, 2, 3).reshape(LAYOUTS, slab_count, NODE_DEV, F).transpose(1, 0, 2, 3)

    def backward_slab(packed):
        feats, aggregate, grad_hidden, hubw = packed
        pre_acts, unused = sage_forward(feats, aggregate, sage_weight)
        grad_self, grad_agg, grads = sage_backward(grad_hidden, pre_acts, feats, aggregate, sage_weight)
        hub_part = jnp.einsum('nj,lnf->ljf', hubw.astype(jnp.float32), grad_agg.astype(jnp.float32), precision=lax.Precision.HIGHEST)
        return (grad_self, grad_agg, grads, hub_part)
    grad_selfs, grad_aggs, sage_parts, hub_parts = lax.map(backward_slab, (by_slab, aggregates, grad_slab, hubw_slab))
    hub_total = lax.optimization_barrier(jnp.sum(hub_parts, axis=0))

    def finish_slab(packed):
        index, grad_self, grad_agg, tiles, dst, src, count = packed
        gathered = grad_agg.reshape(LAYOUTS, -1, TILE, F)[:, dst]
        products = jnp.einsum('tij,ltif->ltjf', tiles.astype(jnp.float32), gathered.astype(jnp.float32), precision=lax.Precision.HIGHEST)
        back_rows = jnp.einsum('bt,ltjf->lbjf', placement(src, count), products, precision=lax.Precision.HIGHEST).reshape(LAYOUTS, NODE_DEV, F)
        local_ids = lax.dynamic_slice_in_dim(hub_ids, (index * HUB_DEV).astype(jnp.int32), HUB_DEV) - (index * NODE_DEV).astype(jnp.int32)
        hub_piece = lax.dynamic_slice_in_dim(hub_total, (index * HUB_DEV).astype(jnp.int32), HUB_DEV, 1)
        totals = grad_self.astype(jnp.float32) + back_rows
        totals = totals.at[:, local_ids].add(hub_piece)
        return totals.astype(jnp.bfloat16)
    slab_ids = jnp.arange(slab_count, dtype=jnp.int32)
    grads_x = lax.map(finish_slab, (slab_ids, grad_selfs, grad_aggs, tiles_slab, dst_slab, src_slab, tile_count))
    grad_features = grads_x.transpose(1, 0, 2, 3).reshape(LAYOUTS, NODES, F)
    attn_slab = lax.optimization_barrier(jnp.sum(attn_parts.reshape(slab_count, N_CONFIG, 4, F, F), axis=1))
    grad_weights = jnp.concatenate([sage_parts, attn_slab], axis=1)
    grad_weights = grad_weights / math.sqrt(LAYOUTS * NODE_DEV)
    return (layer_out, grad_features, grad_weights)
```

```python
import functools
import math

import jax
import jax.numpy as jnp
from jax import lax
from jax.experimental import pallas as pl
from jax.experimental.pallas import tpu as pltpu
from jax.sharding import PartitionSpec as P

HEADS = 4
CAP = 20.0
SUB = 8

BF = jnp.bfloat16
F32 = jnp.float32
VMEM = pl.BlockSpec(memory_space=pltpu.VMEM)
SMEM = pl.BlockSpec(memory_space=pltpu.SMEM)
LIMIT = 48 * 1024 * 1024


def dot(a, b):
    return jnp.dot(a, b, preferred_element_type=F32)


def dot_nt(a, b):
    return lax.dot_general(a, b, (((1,), (1,)), ((), ())), preferred_element_type=F32)


def call(kernel, outs, operands, specs, scratch=(), flops=0, size=0, name=None):
    return pl.pallas_call(
        kernel,
        out_shape=outs,
        in_specs=specs,
        out_specs=jax.tree.map(lambda _: VMEM, outs),
        scratch_shapes=list(scratch),
        compiler_params=pltpu.CompilerParams(vmem_limit_bytes=LIMIT),
        cost_estimate=pl.CostEstimate(flops=flops, bytes_accessed=size, transcendentals=0),
        name=name,
    )(*operands)


def hub_pick(ids, feats, out):
    layouts, nodes, _ = feats.shape
    hubs = out.shape[1]
    row = lax.broadcasted_iota(jnp.int32, (hubs, nodes), 0)
    col = lax.broadcasted_iota(jnp.int32, (hubs, nodes), 1)
    want = jnp.zeros((hubs, nodes), jnp.int32)
    for j in range(hubs):
        want = jnp.where(row == j, lax.rem(ids[j], nodes), want)
    hot = jnp.where(col == want, 1.0, 0.0).astype(BF)
    for l in range(layouts):
        out[l] = dot(hot, feats[l]).astype(BF)


def adjacency(src, dst, count, tiles, feats, weight, adj, adj_t, summed, pre_self):
    slots, tile, _ = tiles.shape
    layouts, nodes, _ = feats.shape
    adj[...] = jnp.zeros(adj.shape, F32)
    for t in range(slots):

        @pl.when(t < count[0])
        def _():
            at = pl.ds(pl.multiple_of(dst[t] * tile, tile), tile)
            block = tiles[t].astype(F32)
            col = src[t]
            for s in range(nodes // tile):

                @pl.when(col == s)
                def _():
                    adj[at, pl.ds(s * tile, tile)] += block

    dense = adj[...].astype(BF)
    adj_t[...] = adj[...].T.astype(BF)
    wide = jnp.concatenate([feats[l] for l in range(layouts)], axis=1)
    summed[...] = dot(dense, wide)
    for l in range(layouts):
        pre_self[l] = dot(feats[l], weight[0])


def sage_out(ranks, pieces, summed, pre_self, hub_weight, weight, hidden, agg, pre, hub_all):
    layouts, nodes, width = pre_self.shape
    shares, groups, _, _ = hidden.shape
    hubs = pieces[0].shape[1]
    me = lax.axis_index("graph")
    for s, piece in enumerate(pieces):
        at = pl.ds(pl.multiple_of(lax.rem(me + ranks - s, ranks) * hubs, hubs), hubs)
        for l in range(layouts):
            hub_all[at, l * width : (l + 1) * width] = piece[l].astype(F32)
    total = summed[...] + dot(hub_weight[...], hub_all[...].astype(BF))
    acts = []
    for l in range(layouts):
        mine = total[:, l * width : (l + 1) * width].astype(BF)
        agg[l] = mine
        value = pre_self[l] + dot(mine, weight[1])
        pre[l] = value
        act = value / (1.0 + jnp.exp(-value))
        acts.append(act.reshape(shares, groups, SUB, width))
    both = jnp.concatenate(acts, axis=2)
    hidden[...] = both.astype(BF)


def prepare(cot, attn, weight, feats, agg, pre, hub_weight, cot_g, gmix, slope, rows_t, w_back, hub_t):
    layouts, nodes, width = cot.shape
    groups = cot_g.shape[0]
    for p in range(groups // 2):
        block = cot[:, 2 * SUB * p : 2 * SUB * (p + 1), :].astype(F32)
        for h in range(2):
            rows = block[:, SUB * h : SUB * (h + 1), :].reshape(layouts * SUB, width).astype(BF)
            cot_g[2 * p + h] = rows
            gmix[2 * p + h] = dot_nt(rows, attn[3]).astype(BF)
    for l in range(feats.shape[0]):
        value = pre[l]
        sig = 1.0 / (1.0 + jnp.exp(-value))
        slope[l] = sig * (1.0 + value * (1.0 - sig))
        at = slice(l * feats.shape[1], (l + 1) * feats.shape[1])
        rows_t[0:width, at] = feats[l].T
        rows_t[width : 2 * width, at] = agg[l].T
    w_back[:, 0:width] = weight[0].T
    w_back[:, width : 2 * width] = weight[1].T
    hub_t[...] = hub_weight[...].T


def attend(hidden, cot_g, gmix, attn, grad_hidden, mixed, grads):
    shares, groups, depth, width = hidden.shape
    rows = shares * depth
    head = width // HEADS
    scale = 1.0 / math.sqrt(head)
    w_all = jnp.concatenate([attn[0], attn[1], attn[2]], axis=1)
    lane = lax.broadcasted_iota(jnp.int32, (rows, width), 1) // head
    r = lax.broadcasted_iota(jnp.int32, (rows, rows), 0)
    c = lax.broadcasted_iota(jnp.int32, (rows, rows), 1)
    same = (r % SUB) == (c % SUB)
    zero = jnp.zeros((rows, width), BF)

    def by_head(x):
        return [jnp.where(lane == e, x, zero) for e in range(HEADS)]

    total_w = jnp.zeros((width, 3 * width), F32)
    total_o = jnp.zeros((width, width), F32)
    for g in range(groups):
        hid = hidden[:, g].reshape(rows, width)
        qkv = dot(hid, w_all).astype(BF)
        q, k, v = (qkv[:, i * width : (i + 1) * width] for i in range(3))
        gm = gmix[g]
        k_t, v_t = k.T, v.T
        scores = dot_nt(jnp.concatenate(by_head(k), axis=0), q)
        d_probs = dot_nt(jnp.concatenate(by_head(v), axis=0), gm)
        probs, d_scores, mix_t, dq_t = [], [], [], []
        for e in range(HEADS):
            t = jnp.tanh(scores[e * rows : (e + 1) * rows] * (scale / CAP))
            w = jnp.where(same, jnp.exp(CAP * t), 0.0)
            a = w * (1.0 / jnp.sum(w, axis=0, keepdims=True))
            z = a * d_probs[e * rows : (e + 1) * rows]
            zs = jnp.sum(z, axis=0, keepdims=True)
            ds = ((z - a * zs) * (scale - scale * (t * t))).astype(BF)
            p = a.astype(BF)
            at = slice(e * head, (e + 1) * head)
            mix_t.append(dot(v_t[at], p))
            dq_t.append(dot(k_t[at], ds))
            probs.append(p)
            d_scores.append(ds)
        mix_t = jnp.concatenate(mix_t, axis=0).astype(BF)
        dq = jnp.concatenate(dq_t, axis=0).astype(BF).T
        dk = dot(jnp.concatenate(d_scores, axis=1), jnp.concatenate(by_head(q), axis=0)).astype(BF)
        dv = dot(jnp.concatenate(probs, axis=1), jnp.concatenate(by_head(gm), axis=0)).astype(BF)
        d_all = jnp.concatenate([dq, dk, dv], axis=1)
        back = cot_g[g].astype(F32) + dot_nt(d_all, w_all)
        grad_hidden[:, g] = back.astype(BF).reshape(shares, depth, width)
        mixed[g] = mix_t.T
        total_w += dot(hid.T, d_all)
        total_o += dot(mix_t, cot_g[g])
    for i in range(3):
        grads[i] = total_w[:, i * width : (i + 1) * width].astype(BF)
    grads[3] = total_o.astype(BF)


def outputs(hidden, mixed, attn, out):
    shares, groups, depth, width = hidden.shape
    rows = shares * depth
    layouts = rows // SUB
    for p in range(groups // 2):
        pair = []
        for g in (2 * p, 2 * p + 1):
            both = hidden[:, g].reshape(rows, width).astype(F32) + dot(mixed[g], attn[3])
            pair.append(both.reshape(layouts, SUB, width))
        out[:, 2 * SUB * p : 2 * SUB * (p + 1), :] = jnp.concatenate(pair, axis=1).astype(BF)


def sage_back(grad_hidden, slope, rows_t, w_back, hub_t, adj_t, totals, hub_part, grads):
    shares, groups, depth, width = grad_hidden.shape
    layouts, nodes, _ = slope.shape
    parts = grad_hidden[...].astype(F32).reshape(shares, groups, layouts, SUB, width)
    grad_pre, grad_agg, grad_self = [], [], []
    for l in range(layouts):
        gpre = (parts[:, :, l].reshape(nodes, width) * slope[l]).astype(BF)
        both = dot(gpre, w_back[...])
        grad_pre.append(gpre)
        grad_self.append(both[:, 0:width].astype(BF).astype(F32))
        grad_agg.append(both[:, width : 2 * width].astype(BF))
    wide = jnp.concatenate(grad_agg, axis=1)
    part = dot(hub_t[...], wide).astype(BF)
    for l in range(layouts):
        hub_part[:, l] = part[:, l * width : (l + 1) * width].reshape(
            hub_part.shape[0], hub_part.shape[2], width
        )
    back = dot(adj_t[...], wide)
    for l in range(layouts):
        totals[l] = grad_self[l] + back[:, l * width : (l + 1) * width]
    both = dot(rows_t[...], jnp.concatenate(grad_pre, axis=0))
    grads[0] = both[0:width].astype(BF)
    grads[1] = both[width : 2 * width].astype(BF)


def finish(ids, totals, hub_parts, out, work):
    layouts, nodes, width = totals.shape
    hubs = hub_parts.shape[2]
    work[...] = totals[...]
    summed = jnp.sum(hub_parts[...].astype(F32), axis=0)
    for l in range(layouts):
        for j in range(hubs):
            at = pl.ds(lax.rem(ids[j], nodes), 1)
            work[l, at, :] += summed[l, j : j + 1, :]
    out[...] = work[...].astype(BF)


def add_parts(parts, out):
    out[...] = jnp.sum(parts[...].astype(F32), axis=0).astype(BF)


def scaled(gathered, out, *, scale):
    out[...] = gathered[...].astype(F32) * scale


def local(
    features,
    cotangent,
    sage_weight,
    attn_weight,
    tile_vals,
    tile_dst,
    tile_src,
    tile_count,
    hub_ids,
    hub_weight,
):
    layout_dev, node_dev, width = features.shape
    ranks = lax.axis_size("graph")
    shares = lax.axis_size("config")
    share = node_dev // shares
    groups = share // SUB
    layouts = layout_dev * shares
    rows = layouts * SUB
    depth = layout_dev * SUB
    hub_dev = hub_ids.shape[0]
    hubs = hub_weight.shape[1]

    def shape(dims, kind=BF):
        return jax.ShapeDtypeStruct(dims, kind)

    mine = call(hub_pick, shape((layout_dev, hub_dev, width)), (hub_ids, features), [SMEM, VMEM], name="hub_pick")
    pieces = [mine]
    for s in range(1, ranks):
        pieces.append(lax.ppermute(mine, "graph", [(i, (i + s) % ranks) for i in range(ranks)]))

    adj_t, summed, pre_self = call(
        lambda src, dst, count, tiles, feats, weight, adj_t, summed, pre_self, adj: adjacency(
            src, dst, count, tiles, feats, weight, adj, adj_t, summed, pre_self
        ),
        (
            shape((node_dev, node_dev)),
            shape((node_dev, layout_dev * width), F32),
            shape((layout_dev, node_dev, width), F32),
        ),
        (tile_src, tile_dst, tile_count, tile_vals, features, sage_weight),
        [SMEM, SMEM, SMEM, VMEM, VMEM, VMEM],
        [pltpu.VMEM((node_dev, node_dev), F32)],
        flops=10**9,
        size=2**21,
        name="adjacency",
    )

    def sage_kernel(*refs):
        sage_out(ranks, refs[:ranks], *refs[ranks:])

    hidden, agg, pre = call(
        sage_kernel,
        (
            shape((shares, groups, depth, width)),
            shape((layout_dev, node_dev, width)),
            shape((layout_dev, node_dev, width), F32),
        ),
        (*pieces, summed, pre_self, hub_weight, sage_weight),
        [VMEM] * (ranks + 4),
        [pltpu.VMEM((hubs, layout_dev * width), F32)],
        name="sage_out",
    )
    hidden_in = lax.all_to_all(hidden, "config", split_axis=0, concat_axis=0, tiled=True)

    cot_g, gmix, slope, rows_t, w_back, hub_t = call(
        prepare,
        (
            shape((groups, rows, width)),
            shape((groups, rows, width)),
            shape((layout_dev, node_dev, width), F32),
            shape((2 * width, layout_dev * node_dev)),
            shape((width, 2 * width)),
            shape((hubs, node_dev)),
        ),
        (cotangent, attn_weight, sage_weight, features, agg, pre, hub_weight),
        [VMEM] * 7,
        flops=10**9,
        size=2**21,
        name="prepare",
    )

    grad_hidden, mixed, attn_grads = call(
        attend,
        (
            shape((shares, groups, depth, width)),
            shape((groups, rows, width)),
            shape((4, width, width)),
        ),
        (hidden_in, cot_g, gmix, attn_weight),
        [VMEM] * 4,
        name="attend",
    )
    grad_in = lax.all_to_all(grad_hidden, "config", split_axis=0, concat_axis=0, tiled=True)

    output = call(
        outputs,
        shape((layouts, share, width)),
        (hidden_in, mixed, attn_weight),
        [VMEM] * 3,
        flops=10**9,
        size=2**21,
        name="outputs",
    )

    totals, hub_part, sage_grads = call(
        sage_back,
        (
            shape((layout_dev, node_dev, width), F32),
            shape((ranks, layout_dev, hub_dev, width)),
            shape((2, width, width)),
        ),
        (grad_in, slope, rows_t, w_back, hub_t, adj_t),
        [VMEM] * 6,
        name="sage_back",
    )

    hub_parts = lax.all_to_all(hub_part, "graph", split_axis=0, concat_axis=0, tiled=True)
    partial_grads = jnp.concatenate([sage_grads, attn_grads], axis=0)
    count = partial_grads.shape[0]
    slices = partial_grads.reshape(shares, count * width // shares, width)
    received = lax.all_to_all(slices, "config", split_axis=0, concat_axis=0, tiled=True)
    own = call(add_parts, shape(received.shape[1:]), (received,), [VMEM], name="add_parts")
    gathered = lax.all_to_all(
        jnp.broadcast_to(own[None], received.shape), "config", split_axis=0, concat_axis=0, tiled=True
    )
    grad_features = call(
        finish,
        shape((layout_dev, node_dev, width)),
        (hub_ids, totals, hub_parts),
        [SMEM, VMEM, VMEM],
        [pltpu.VMEM((layout_dev, node_dev, width), F32)],
        name="finish",
    )
    scale = 1.0 / math.sqrt(layouts * node_dev)
    weights = call(
        functools.partial(scaled, scale=scale),
        shape((count, width, width), F32),
        (gathered.reshape(count, width, width),),
        [VMEM],
        name="scaled",
    )
    return (output, grad_features, weights[None])


def solution(mesh):
    return jax.shard_map(
        local,
        mesh=mesh,
        in_specs=(
            P("config", "graph", None),
            P(None, ("graph", "config"), None),
            P(),
            P(),
            P("graph", None, None),
            P("graph"),
            P("graph"),
            P("graph"),
            P("graph"),
            P("graph", None),
        ),
        out_specs=(
            P(None, ("graph", "config"), None),
            P("config", "graph", None),
            P("graph", None, None, None),
        ),
        check_vma=False,
    )
```

```python
import functools
import math

import jax
import jax.numpy as jnp
from jax import lax
from jax.experimental import pallas as pl
from jax.experimental.pallas import tpu as pltpu
from jax.sharding import PartitionSpec as P

HEADS = 4
CAP = 20.0
SUB = 8

BF = jnp.bfloat16
F32 = jnp.float32
VMEM = pl.BlockSpec(memory_space=pltpu.VMEM)
HBM = pl.BlockSpec(memory_space=pltpu.HBM)
LIMIT = 24 * 1024 * 1024


def dot(a, b):
    return jnp.dot(a, b, preferred_element_type=F32)


def dot_nt(a, b):
    return lax.dot_general(a, b, (((1,), (1,)), ((), ())), preferred_element_type=F32)


def dot_tn(a, b):
    return lax.dot_general(a, b, (((0,), (0,)), ((), ())), preferred_element_type=F32)


def shape(dims, kind=BF):
    return jax.ShapeDtypeStruct(dims, kind)


def call(kernel, outs, operands, specs, scratch=(), hidden=False, name=None):
    cost = {}
    if hidden:
        cost["cost_estimate"] = pl.CostEstimate(flops=10**9, bytes_accessed=2**21, transcendentals=0)
    return pl.pallas_call(
        kernel,
        out_shape=outs,
        in_specs=specs,
        out_specs=jax.tree.map(lambda _: VMEM, outs),
        scratch_shapes=list(scratch),
        compiler_params=pltpu.CompilerParams(vmem_limit_bytes=LIMIT),
        name=name,
        **cost,
    )(*operands)


def fetch(pairs, sems):
    copies = [pltpu.make_async_copy(a, b, sems.at[i]) for i, (a, b) in enumerate(pairs)]
    for copy in copies:
        copy.start()
    return copies


def swapped(x, axis, mask):
    count = lax.axis_size(axis)
    return lax.ppermute(x, axis, [(i, i ^ mask) for i in range(count)])


def hub_pick(ids, feats, out, kept, ids_s, sems):
    copies = fetch([(ids, ids_s)] + [(feats.at[l], kept.at[l]) for l in range(feats.shape[0])], sems)
    layouts, nodes, _ = feats.shape
    hubs = out.shape[1]
    row = lax.broadcasted_iota(jnp.int32, (hubs, nodes), 0)
    col = lax.broadcasted_iota(jnp.int32, (hubs, nodes), 1)
    want = jnp.zeros((hubs, nodes), jnp.int32)
    copies[0].wait()
    for j in range(hubs):
        want = jnp.where(row == j, lax.rem(ids_s[j], nodes), want)
    hot = jnp.where(col == want, 1.0, 0.0).astype(BF)
    for l in range(layouts):
        copies[1 + l].wait()
        out[l] = dot(hot, kept[l]).astype(BF)


def adjacency(src, dst, count, tiles, weight, hub_t, feats, adj_t, summed, pre_self, weight_v, hub_v, *scratch):
    src_s, dst_s, count_s, tiles_v, adj, sems = scratch
    copies = fetch(
        [(src, src_s), (dst, dst_s), (count, count_s), (weight, weight_v), (tiles, tiles_v), (hub_t, hub_v)], sems
    )
    slots, tile, _ = tiles.shape
    layouts, nodes, _ = feats.shape
    adj[...] = jnp.zeros(adj.shape, F32)
    for i in range(4):
        copies[i].wait()
    for l in range(layouts):
        pre_self[l] = dot(feats[l], weight_v[0])
    copies[4].wait()
    for t in range(slots):

        @pl.when(t < count_s[0])
        def _():
            at = pl.ds(pl.multiple_of(dst_s[t] * tile, tile), tile)
            block = tiles_v[t].astype(F32)
            col = src_s[t]
            for s in range(nodes // tile):

                @pl.when(col == s)
                def _():
                    adj[at, pl.ds(s * tile, tile)] += block

    dense = adj[...].astype(BF)
    wide = jnp.concatenate([feats[l] for l in range(layouts)], axis=1)
    summed[...] = dot(dense, wide)
    adj_t[...] = dense.T
    copies[5].wait()


def sage_out(*refs):
    pieces, (summed, pre_self, hub_t, weight, own, other, agg, pre, hub_all, ready) = refs[:-10], refs[-10:]
    layouts, nodes, width = pre_self.shape
    shares, groups, _, _ = ready.shape
    hubs = pieces[0].shape[1]
    slab = lax.axis_index("graph")
    for s, piece in enumerate(pieces):
        at = pl.ds(pl.multiple_of(lax.bitwise_xor(slab, s) * hubs, hubs), hubs)
        for l in range(layouts):
            hub_all[at, l * width : (l + 1) * width] = piece[l].astype(F32)
    total = summed[...] + dot_tn(hub_t[...], hub_all[...].astype(BF))
    acts = []
    for l in range(layouts):
        mine = total[:, l * width : (l + 1) * width].astype(BF)
        agg[l] = mine
        value = pre_self[l] + dot(mine, weight[1])
        pre[l] = value
        act = value / (1.0 + jnp.exp(-value))
        acts.append(act.reshape(shares, groups, SUB, width))
    ready[...] = jnp.concatenate(acts, axis=2).astype(BF)
    hand_out(ready, own, other)


def hand_out(ready, own, other):
    me = lax.axis_index("config")
    for s in range(own.shape[0]):
        own[s] = ready[lax.bitwise_xor(me, 2 * s)]
        other[s] = ready[lax.bitwise_xor(me, 2 * s + 1)]


def arrivals(own, other, received):
    found = [(0, own[0]), (1, other[0])]
    for s, both in enumerate(received):
        found.append((2 * s + 2, both[0]))
        found.append((2 * s + 3, both[1]))
    return found


def prepare(cot, attn, weight, feats, agg, pre, cot_g, gmix, slope, rows_t, w_back, attn_v, cot_v, sems):
    copies = fetch([(attn, attn_v), (cot, cot_v)], sems)
    width = cot.shape[2]
    layouts = cot.shape[0]
    groups = cot_g.shape[0]
    for l in range(feats.shape[0]):
        value = pre[l]
        sig = 1.0 / (1.0 + jnp.exp(-value))
        slope[l] = sig * (1.0 + value * (1.0 - sig))
        at = slice(l * feats.shape[1], (l + 1) * feats.shape[1])
        rows_t[0:width, at] = feats[l].T
        rows_t[width : 2 * width, at] = agg[l].T
    w_back[:, 0:width] = weight[0].T
    w_back[:, width : 2 * width] = weight[1].T
    copies[0].wait()
    copies[1].wait()
    for p in range(groups // 2):
        block = cot_v[:, 2 * SUB * p : 2 * SUB * (p + 1), :].astype(F32)
        for h in range(2):
            rows = block[:, SUB * h : SUB * (h + 1), :].reshape(layouts * SUB, width).astype(BF)
            cot_g[2 * p + h] = rows
            gmix[2 * p + h] = dot_nt(rows, attn_v[3]).astype(BF)


def attend(*refs):
    (own, other), received = refs[:2], refs[2:-13]
    cot_g, gmix, attn, own_out, other_out, hid_out, mixed, grads_own, grads_other = refs[-13:-4]
    hidden, ready, grads, _ = refs[-4:]
    me = lax.axis_index("config")
    groups, shares, depth, width = hidden.shape
    rows = shares * depth
    head = width // HEADS
    scale = 1.0 / math.sqrt(head)
    for mask, block in arrivals(own, other, received):
        hidden[:, lax.bitwise_xor(me, mask)] = block
    w_all = jnp.concatenate([attn[0], attn[1], attn[2]], axis=1)
    lane = lax.broadcasted_iota(jnp.int32, (rows, width), 1) // head
    r = lax.broadcasted_iota(jnp.int32, (rows, rows), 0)
    c = lax.broadcasted_iota(jnp.int32, (rows, rows), 1)
    same = (r % SUB) == (c % SUB)
    zero = jnp.zeros((rows, width), BF)

    def by_head(x):
        return [jnp.where(lane == e, x, zero) for e in range(HEADS)]

    total_w = jnp.zeros((width, 3 * width), F32)
    total_o = jnp.zeros((width, width), F32)
    for g in range(groups):
        hid = hidden[g].reshape(rows, width)
        hid_out[g] = hid
        qkv = dot(hid, w_all).astype(BF)
        q, k, v = (qkv[:, i * width : (i + 1) * width] for i in range(3))
        gm = gmix[g]
        k_t, v_t = k.T, v.T
        scores = dot_nt(jnp.concatenate(by_head(k), axis=0), q)
        d_probs = dot_nt(jnp.concatenate(by_head(v), axis=0), gm)
        probs, d_scores, mix_t, dq_t = [], [], [], []
        for e in range(HEADS):
            t = jnp.tanh(scores[e * rows : (e + 1) * rows] * (scale / CAP))
            w = jnp.where(same, jnp.exp(CAP * t), 0.0)
            a = w * (1.0 / jnp.sum(w, axis=0, keepdims=True))
            z = a * d_probs[e * rows : (e + 1) * rows]
            zs = jnp.sum(z, axis=0, keepdims=True)
            ds = ((z - a * zs) * (scale - scale * (t * t))).astype(BF)
            p = a.astype(BF)
            at = slice(e * head, (e + 1) * head)
            mix_t.append(dot(v_t[at], p))
            dq_t.append(dot(k_t[at], ds))
            probs.append(p)
            d_scores.append(ds)
        mix_t = jnp.concatenate(mix_t, axis=0).astype(BF)
        dq = jnp.concatenate(dq_t, axis=0).astype(BF).T
        dk = dot(jnp.concatenate(d_scores, axis=1), jnp.concatenate(by_head(q), axis=0)).astype(BF)
        dv = dot(jnp.concatenate(probs, axis=1), jnp.concatenate(by_head(gm), axis=0)).astype(BF)
        d_all = jnp.concatenate([dq, dk, dv], axis=1)
        back = cot_g[g].astype(F32) + dot_nt(d_all, w_all)
        ready[:, g] = back.astype(BF).reshape(shares, depth, width)
        mixed[g] = mix_t.T
        total_w += dot(hid.T, d_all)
        total_o += dot(mix_t, cot_g[g])
    hand_out(ready, own_out, other_out)
    for i in range(3):
        grads[i] = total_w[:, i * width : (i + 1) * width].astype(BF)
    grads[3] = total_o.astype(BF)
    core = lax.rem(me, 2)
    half = grads_own.shape[0]
    grads_own[...] = grads[pl.ds(core * half, half)]
    grads_other[...] = grads[pl.ds((1 - core) * half, half)]


def outputs(hidden, mixed, attn, out):
    groups, rows, width = hidden.shape
    layouts = rows // SUB
    for p in range(groups // 2):
        pair = []
        for g in (2 * p, 2 * p + 1):
            both = hidden[g].astype(F32) + dot(mixed[g], attn[3])
            pair.append(both.reshape(layouts, SUB, width))
        out[:, 2 * SUB * p : 2 * SUB * (p + 1), :] = jnp.concatenate(pair, axis=1).astype(BF)


def sage_back(ranks, *refs):
    (own, other), received = refs[:2], refs[2 : -9 - ranks]
    slope, rows_t, w_back, hub_t, wide, self_out, grads = refs[-9 - ranks : -2 - ranks]
    hub_out, (parts, hub_sum) = refs[-2 - ranks : -2], refs[-2:]
    me = lax.axis_index("config")
    shares, groups, layouts, _, width = parts.shape
    nodes = slope.shape[1]
    for mask, block in arrivals(own, other, received):
        parts[lax.bitwise_xor(me, mask)] = block.astype(F32).reshape(parts.shape[1:])
    grad_pre, grad_agg = [], []
    for l in range(layouts):
        gpre = (parts[:, :, l].reshape(nodes, width) * slope[l]).astype(BF)
        both = dot(gpre, w_back[...]).astype(BF)
        grad_pre.append(gpre)
        self_out[l] = both[:, 0:width]
        grad_agg.append(both[:, width : 2 * width])
    spread = jnp.concatenate(grad_agg, axis=1)
    wide[...] = spread
    hub_sum[...] = dot(hub_t[...], spread)
    slab = lax.axis_index("graph")
    hubs = hub_out[0].shape[1]
    for s in range(ranks):
        at = pl.ds(pl.multiple_of(lax.bitwise_xor(slab, s) * hubs, hubs), hubs)
        for l in range(layouts):
            hub_out[s][l] = hub_sum[at, l * width : (l + 1) * width].astype(BF)
    both = dot(rows_t[...], jnp.concatenate(grad_pre, axis=0))
    grads[0] = both[0:width].astype(BF)
    grads[1] = both[width : 2 * width].astype(BF)


def chip_order(chip, parts, work):
    for s, part in enumerate(parts):
        work[lax.bitwise_xor(chip, s)] = part[...].astype(F32)
    total = work[0]
    for s in range(1, len(parts)):
        total = total + work[s]
    return total


def tile_back(adj_t, wide, grad_self, *refs):
    parts, (totals, half, work) = refs[:-3], refs[-3:]
    layouts, _, width = totals.shape
    back = dot(adj_t[...], wide[...])
    for l in range(layouts):
        totals[l] = grad_self[l].astype(F32) + back[:, l * width : (l + 1) * width]
    half[...] = chip_order(lax.axis_index("config") // 2, parts, work).astype(BF)


def finish(ranks, scale, ids, totals, half, half_other, *refs):
    hub_parts, chips = refs[:ranks], refs[ranks:-6]
    out, weights, ids_s, rows, work, sems = refs[-6:]
    copies = fetch([(ids, ids_s)], sems)
    me = lax.axis_index("config")
    layouts, nodes, width = totals.shape
    weights[0:2] = chip_order(me // 2, chips, work) * scale
    count = half.shape[0]
    core = lax.rem(me, 2)
    weights[pl.ds(2 + core * count, count)] = half[...].astype(F32) * scale
    weights[pl.ds(2 + (1 - core) * count, count)] = half_other[...].astype(F32) * scale
    summed = hub_parts[0][...].astype(F32)
    for part in hub_parts[1:]:
        summed = summed + part[...].astype(F32)
    rows[...] = totals[...]
    copies[0].wait()
    for l in range(layouts):
        for j in range(ids.shape[0]):
            at = pl.ds(lax.rem(ids_s[j], nodes), 1)
            rows[l, at, :] += summed[l, j : j + 1, :]
    out[...] = rows[...].astype(BF)


def exchange(own, other):
    other = swapped(other, "config", 1)
    received = [
        swapped(jnp.stack([own[s], other[s]]), "config", 2 * s) for s in range(1, own.shape[0])
    ]
    return (own, other, *received)


def chips_of(x):
    return [x] + [swapped(x, "config", mask) for mask in range(2, lax.axis_size("config"), 2)]


def local(
    features,
    cotangent,
    sage_weight,
    attn_weight,
    tile_vals,
    tile_dst,
    tile_src,
    tile_count,
    hub_ids,
    hub_weight,
):
    layout_dev, node_dev, width = features.shape
    ranks = lax.axis_size("graph")
    shares = lax.axis_size("config")
    chips = shares // 2
    share = node_dev // shares
    groups = share // SUB
    layouts = layout_dev * shares
    rows = layouts * SUB
    depth = layout_dev * SUB
    hub_dev = hub_ids.shape[0]
    hubs = hub_weight.shape[1]
    slots = tile_vals.shape[0]
    slab = (layout_dev, node_dev, width)
    spread = (node_dev, layout_dev * width)
    dma = pltpu.SemaphoreType.DMA

    mine, feats = call(
        hub_pick,
        (shape((layout_dev, hub_dev, width)), shape(slab)),
        (hub_ids, features),
        [HBM, HBM],
        [pltpu.SMEM((hub_dev,), jnp.int32), dma((1 + layout_dev,))],
        name="hub_pick",
    )
    pieces = [mine] + [swapped(mine, "graph", s) for s in range(1, ranks)]

    adj_t, summed, pre_self, sage_w, hub_t = call(
        adjacency,
        (
            shape((node_dev, node_dev)),
            shape(spread, F32),
            shape(slab, F32),
            shape(sage_weight.shape),
            shape((hubs, node_dev)),
        ),
        (tile_src, tile_dst, tile_count, tile_vals, sage_weight, hub_weight.T, feats),
        [HBM] * 6 + [VMEM],
        [
            pltpu.SMEM((slots,), jnp.int32),
            pltpu.SMEM((slots,), jnp.int32),
            pltpu.SMEM((1,), jnp.int32),
            pltpu.VMEM(tile_vals.shape, BF),
            pltpu.VMEM((node_dev, node_dev), F32),
            dma((6,)),
        ],
        hidden=True,
        name="adjacency",
    )

    own, other, agg, pre = call(
        sage_out,
        (
            shape((chips, groups, depth, width)),
            shape((chips, groups, depth, width)),
            shape(slab),
            shape(slab, F32),
        ),
        (*pieces, summed, pre_self, hub_t, sage_w),
        [VMEM] * (ranks + 4),
        [pltpu.VMEM((hubs, layout_dev * width), F32), pltpu.VMEM((shares, groups, depth, width), BF)],
        name="sage_out",
    )
    hidden_in = exchange(own, other)

    cot_g, gmix, slope, rows_t, w_back, attn = call(
        prepare,
        (
            shape((groups, rows, width)),
            shape((groups, rows, width)),
            shape(slab, F32),
            shape((2 * width, layout_dev * node_dev)),
            shape((width, 2 * width)),
            shape(attn_weight.shape),
        ),
        (cotangent, attn_weight, sage_w, feats, agg, pre),
        [HBM] * 2 + [VMEM] * 4,
        [pltpu.VMEM((layouts, share, width), BF), dma((2,))],
        hidden=True,
        name="prepare",
    )

    half = (attn_weight.shape[0] // 2, width, width)
    own, other, hidden, mixed, grads_own, grads_other = call(
        attend,
        (
            shape((chips, groups, depth, width)),
            shape((chips, groups, depth, width)),
            shape((groups, rows, width)),
            shape((groups, rows, width)),
            shape(half),
            shape(half),
        ),
        (*hidden_in, cot_g, gmix, attn),
        [VMEM] * (len(hidden_in) + 3),
        [
            pltpu.VMEM((groups, shares, depth, width), BF),
            pltpu.VMEM((shares, groups, depth, width), BF),
            pltpu.VMEM(attn_weight.shape, BF),
            pltpu.VMEM((8, width), F32),
        ],
        name="attend",
    )
    grad_in = exchange(own, other)
    half_parts = chips_of(grads_own + swapped(grads_other, "config", 1))

    output = call(
        outputs,
        shape((layouts, share, width)),
        (hidden, mixed, attn),
        [VMEM] * 3,
        hidden=True,
        name="outputs",
    )

    wide, grad_self, sage_grads, *hub_parts = call(
        functools.partial(sage_back, ranks),
        (
            shape(spread),
            shape(slab),
            shape(sage_weight.shape),
            *[shape((layout_dev, hub_dev, width)) for _ in range(ranks)],
        ),
        (*grad_in, slope, rows_t, w_back, hub_t),
        [VMEM] * (len(grad_in) + 4),
        [
            pltpu.VMEM((shares, groups, layout_dev, SUB, width), F32),
            pltpu.VMEM((hubs, layout_dev * width), F32),
        ],
        name="sage_back",
    )
    hub_parts = [swapped(part, "graph", s) if s else part for s, part in enumerate(hub_parts)]
    sage_parts = chips_of(sage_grads + swapped(sage_grads, "config", 1))

    totals, half_own = call(
        tile_back,
        (shape(slab, F32), shape(half)),
        (adj_t, wide, grad_self, *half_parts),
        [VMEM] * (3 + chips),
        [pltpu.VMEM((chips, *half), F32)],
        hidden=True,
        name="tile_back",
    )
    half_other = swapped(half_own, "config", 1)

    grad_features, weights = call(
        functools.partial(finish, ranks, 1.0 / math.sqrt(layouts * node_dev)),
        (shape(slab), shape((6, width, width), F32)),
        (hub_ids, totals, half_own, half_other, *hub_parts, *sage_parts),
        [HBM] + [VMEM] * (3 + ranks + chips),
        [
            pltpu.SMEM((hub_dev,), jnp.int32),
            pltpu.VMEM(slab, F32),
            pltpu.VMEM((chips, *sage_weight.shape), F32),
            dma((1,)),
        ],
        name="finish",
    )
    return (output, grad_features, weights[None])


def solution(mesh):
    return jax.shard_map(
        local,
        mesh=mesh,
        in_specs=(
            P("config", "graph", None),
            P(None, ("graph", "config"), None),
            P(),
            P(),
            P("graph", None, None),
            P("graph"),
            P("graph"),
            P("graph"),
            P("graph"),
            P("graph", None),
        ),
        out_specs=(
            P(None, ("graph", "config"), None),
            P("config", "graph", None),
            P("graph", None, None, None),
        ),
        check_vma=False,
    )
```

```python
import functools
import math

import jax
import jax.numpy as jnp
from jax import lax
from jax.experimental import pallas as pl
from jax.experimental.pallas import tpu as pltpu
from jax.sharding import PartitionSpec as P

HEADS = 4
CAP = 20.0
SUB = 8

BF = jnp.bfloat16
F32 = jnp.float32
VMEM = pl.BlockSpec(memory_space=pltpu.VMEM)
HBM = pl.BlockSpec(memory_space=pltpu.HBM)
LIMIT = 24 * 1024 * 1024


def dot(a, b):
    return jnp.dot(a, b, preferred_element_type=F32)


def dot_nt(a, b):
    return lax.dot_general(a, b, (((1,), (1,)), ((), ())), preferred_element_type=F32)


def dot_tn(a, b):
    return lax.dot_general(a, b, (((0,), (0,)), ((), ())), preferred_element_type=F32)


def shape(dims, kind=BF):
    return jax.ShapeDtypeStruct(dims, kind)


def call(kernel, outs, operands, specs, scratch=(), micros=1.0, name=None):
    return pl.pallas_call(
        kernel,
        out_shape=outs,
        in_specs=specs,
        out_specs=jax.tree.map(lambda _: VMEM, outs),
        scratch_shapes=list(scratch),
        compiler_params=pltpu.CompilerParams(vmem_limit_bytes=LIMIT),
        cost_estimate=pl.CostEstimate(
            flops=int(micros * 10**9), bytes_accessed=int(micros * 2**21), transcendentals=0
        ),
        name=name,
    )(*operands)


def fetch(pairs, sems):
    copies = [pltpu.make_async_copy(a, b, sems.at[i]) for i, (a, b) in enumerate(pairs)]
    for copy in copies:
        copy.start()
    return copies


def swapped(x, axis, mask):
    count = lax.axis_size(axis)
    return lax.ppermute(x, axis, [(i, i ^ mask) for i in range(count)])


def hub_pick(ints, feats, out, ints_s, sems):
    copies = fetch([(ints, ints_s)], sems)
    layouts, nodes, _ = feats.shape
    hubs = out.shape[1]
    row = lax.broadcasted_iota(jnp.int32, (hubs, nodes), 0)
    col = lax.broadcasted_iota(jnp.int32, (hubs, nodes), 1)
    want = jnp.zeros((hubs, nodes), jnp.int32)
    copies[0].wait()
    for j in range(hubs):
        want = jnp.where(row == j, lax.rem(ints_s[j], nodes), want)
    hot = jnp.where(col == want, 1.0, 0.0).astype(BF)
    for l in range(layouts):
        out[l] = dot(hot, feats[l]).astype(BF)


def adjacency(first, ints, tiles, weight, feats, adj_t, summed, pre_self, ints_s, adj, sems):
    copies = fetch([(ints, ints_s)], sems)
    slots, tile, _ = tiles.shape
    layouts, nodes, _ = feats.shape
    adj[...] = jnp.zeros(adj.shape, F32)
    for l in range(layouts):
        pre_self[l] = dot(feats[l], weight[0])
    copies[0].wait()
    for t in range(slots):

        @pl.when(t < ints_s[first + 2 * slots])
        def _():
            at = pl.ds(pl.multiple_of(ints_s[first + t] * tile, tile), tile)
            block = tiles[t].astype(F32)
            col = ints_s[first + slots + t]
            for s in range(nodes // tile):

                @pl.when(col == s)
                def _():
                    adj[at, pl.ds(s * tile, tile)] += block

    dense = adj[...].astype(BF)
    wide = jnp.concatenate([feats[l] for l in range(layouts)], axis=1)
    summed[...] = dot(dense, wide)
    adj_t[...] = dense.T


def sage_out(*refs):
    pieces, (summed, pre_self, hub_t, weight, own, other, agg, pre, hub_all, ready) = refs[:-10], refs[-10:]
    layouts, nodes, width = pre_self.shape
    shares, groups, _, _ = ready.shape
    hubs = pieces[0].shape[1]
    slab = lax.axis_index("graph")
    for s, piece in enumerate(pieces):
        at = pl.ds(pl.multiple_of(lax.bitwise_xor(slab, s) * hubs, hubs), hubs)
        for l in range(layouts):
            hub_all[at, l * width : (l + 1) * width] = piece[l].astype(F32)
    total = summed[...] + dot_tn(hub_t[...], hub_all[...].astype(BF))
    acts = []
    for l in range(layouts):
        mine = total[:, l * width : (l + 1) * width].astype(BF)
        agg[l] = mine
        value = pre_self[l] + dot(mine, weight[1])
        pre[l] = value
        act = value / (1.0 + jnp.exp(-value))
        acts.append(act.reshape(shares, groups, SUB, width))
    ready[...] = jnp.concatenate(acts, axis=2).astype(BF)
    hand_out(ready, own, other)


def hand_out(ready, own, other):
    me = lax.axis_index("config")
    for s in range(own.shape[0]):
        own[s] = ready[lax.bitwise_xor(me, 2 * s)]
        other[s] = ready[lax.bitwise_xor(me, 2 * s + 1)]


def arrivals(own, other, received):
    found = [(0, own[0]), (1, other[0])]
    for s, both in enumerate(received):
        found.append((2 * s + 2, both[0]))
        found.append((2 * s + 3, both[1]))
    return found


def prepare(cot, attn, weight, feats, agg, pre, cot_g, gmix, slope, rows_t, w_back):
    layouts, _, width = cot.shape
    groups = cot_g.shape[0]
    for l in range(feats.shape[0]):
        value = pre[l]
        sig = 1.0 / (1.0 + jnp.exp(-value))
        slope[l] = sig * (1.0 + value * (1.0 - sig))
        at = slice(l * feats.shape[1], (l + 1) * feats.shape[1])
        rows_t[0:width, at] = feats[l].T
        rows_t[width : 2 * width, at] = agg[l].T
    w_back[:, 0:width] = weight[0].T
    w_back[:, width : 2 * width] = weight[1].T
    for p in range(groups // 2):
        block = cot[:, 2 * SUB * p : 2 * SUB * (p + 1), :].astype(F32)
        for h in range(2):
            rows = block[:, SUB * h : SUB * (h + 1), :].reshape(layouts * SUB, width).astype(BF)
            cot_g[2 * p + h] = rows
            gmix[2 * p + h] = dot_nt(rows, attn[3]).astype(BF)


def attend(*refs):
    (own, other), received = refs[:2], refs[2:-12]
    cot_g, gmix, attn, own_out, other_out, hid_out, mixed_t, grads_own, grads_other = refs[-12:-3]
    hidden, ready, grads = refs[-3:]
    me = lax.axis_index("config")
    groups, shares, depth, width = hidden.shape
    rows = shares * depth
    head = width // HEADS
    scale = 1.0 / math.sqrt(head)
    for mask, block in arrivals(own, other, received):
        hidden[:, lax.bitwise_xor(me, mask)] = block
    w_all = jnp.concatenate([attn[0], attn[1], attn[2]], axis=1)
    lane = lax.broadcasted_iota(jnp.int32, (rows, width), 1) // head
    r = lax.broadcasted_iota(jnp.int32, (rows, HEADS * rows), 0)
    c = lax.broadcasted_iota(jnp.int32, (rows, HEADS * rows), 1)
    same = (r % SUB) == (c % SUB)
    zero = jnp.zeros((rows, width), BF)
    gap = jnp.zeros((head, rows), BF)

    def by_head(x):
        return jnp.concatenate([jnp.where(lane == e, x, zero) for e in range(HEADS)], axis=0)

    flat = hidden[...].reshape(groups * rows, width)
    hid_out[...] = flat.reshape(groups, rows, width)
    qkv = dot(flat, w_all).astype(BF)
    inputs = []
    for g in range(groups):
        q, k, v = (qkv[g * rows : (g + 1) * rows, i * width : (i + 1) * width] for i in range(3))
        inputs.append((k, v, k.T, v.T, by_head(q), by_head(gmix[g])))
    products = [(dot_nt(k, qm), dot_nt(v, gm)) for k, v, _, _, qm, gm in inputs]
    weighted = []
    for scores, d_probs in products:
        t = jnp.tanh(scores * (scale / CAP))
        w = jnp.where(same, jnp.exp2(t * (CAP * math.log2(math.e))), 0.0)
        a = w * (1.0 / jnp.sum(w, axis=0, keepdims=True))
        z = a * d_probs
        zs = jnp.sum(z, axis=0, keepdims=True)
        weighted.append((a.astype(BF), ((z - a * zs) * (scale - scale * (t * t))).astype(BF)))
    d_all, mix_t = [], []
    for (k, v, k_t, v_t, qm, gm), (p, ds) in zip(inputs, weighted):
        mix, dq = [], []
        for e in range(HEADS):
            at, span = slice(e * head, (e + 1) * head), slice(e * rows, (e + 1) * rows)
            left = jnp.concatenate(
                [jnp.concatenate([v_t[at], gap], axis=1), jnp.concatenate([gap, k_t[at]], axis=1)], axis=0
            )
            both = dot(left, jnp.concatenate([p[:, span], ds[:, span]], axis=0))
            mix.append(both[:head])
            dq.append(both[head:])
        mix_t.append(jnp.concatenate(mix, axis=0).astype(BF))
        dq = jnp.concatenate(dq, axis=0).astype(BF).T
        d_all.append(jnp.concatenate([dq, dot(ds, qm).astype(BF), dot(p, gm).astype(BF)], axis=1))
    d_all = jnp.concatenate(d_all, axis=0)
    mix_t = jnp.concatenate(mix_t, axis=1)
    mixed_t[...] = mix_t
    cots = cot_g[...].reshape(groups * rows, width)
    back = (cots.astype(F32) + dot_nt(d_all, w_all)).astype(BF).reshape(groups, shares, depth, width)
    for g in range(groups):
        ready[:, g] = back[g]
    hand_out(ready, own_out, other_out)
    total = dot(flat.T, d_all)
    for i in range(3):
        grads[i] = total[:, i * width : (i + 1) * width].astype(BF)
    grads[3] = dot(mix_t, cots).astype(BF)
    core = lax.rem(me, 2)
    half = grads_own.shape[0]
    grads_own[...] = grads[pl.ds(core * half, half)]
    grads_other[...] = grads[pl.ds((1 - core) * half, half)]


def outputs(hidden, mixed_t, attn, out):
    groups, rows, width = hidden.shape
    layouts = rows // SUB
    projected = dot_tn(mixed_t[...], attn[3])
    for p in range(groups // 2):
        pair = []
        for g in (2 * p, 2 * p + 1):
            both = hidden[g].astype(F32) + projected[g * rows : (g + 1) * rows]
            pair.append(both.reshape(layouts, SUB, width))
        out[:, 2 * SUB * p : 2 * SUB * (p + 1), :] = jnp.concatenate(pair, axis=1).astype(BF)


def sage_back(*refs):
    (own, other), received = refs[:2], refs[2:-10]
    slope, rows_t, w_back, hub_t, wide, self_out, grads, hub_out, parts, hub_sum = refs[-10:]
    me = lax.axis_index("config")
    layouts, width = parts.shape[2], parts.shape[4]
    nodes = slope.shape[1]
    for mask, block in arrivals(own, other, received):
        parts[lax.bitwise_xor(me, mask)] = block[...].astype(F32).reshape(parts.shape[1:])
    grad_pre, grad_agg = [], []
    for l in range(layouts):
        gpre = (parts[:, :, l].reshape(nodes, width) * slope[l]).astype(BF)
        both = dot(gpre, w_back[...]).astype(BF)
        grad_pre.append(gpre)
        self_out[l] = both[:, 0:width]
        grad_agg.append(both[:, width : 2 * width])
    spread = jnp.concatenate(grad_agg, axis=1)
    wide[...] = spread
    hub_sum[...] = dot(hub_t[...], spread)
    slab = lax.axis_index("graph")
    ranks, _, hubs, _ = hub_out.shape
    for s in range(ranks):
        at = pl.ds(pl.multiple_of(lax.bitwise_xor(slab, s) * hubs, hubs), hubs)
        for l in range(layouts):
            hub_out[s, l] = hub_sum[at, l * width : (l + 1) * width].astype(BF)
    both = dot(rows_t[...], jnp.concatenate(grad_pre, axis=0))
    grads[0] = both[0:width].astype(BF)
    grads[1] = both[width : 2 * width].astype(BF)


def tile_back(adj_t, wide, grad_self, totals):
    back = dot(adj_t[...], wide[...])
    layouts, _, width = totals.shape
    for l in range(layouts):
        totals[l] = grad_self[l].astype(F32) + back[:, l * width : (l + 1) * width]


def finish(ints, totals, hub_own, hub_in, out, ints_s, rows, sems):
    copies = fetch([(ints, ints_s)], sems)
    layouts, nodes, _ = totals.shape
    hubs = hub_own.shape[-2]
    summed = [hub_own[0, l].astype(F32) + hub_in[0, l].astype(F32) for l in range(layouts)]
    rows[...] = totals[...]
    copies[0].wait()
    for l in range(layouts):
        for j in range(hubs):
            at = pl.ds(lax.rem(ints_s[j], nodes), 1)
            rows[l, at, :] += summed[l][j : j + 1, :]
    out[...] = rows[...].astype(BF)


def weights_out(scale, sage, sage_in, half, half_in, out):
    first = sage.shape[0]
    count = half.shape[0]
    core = lax.rem(lax.axis_index("config"), 2)
    out[0:first] = (sage[...].astype(F32) + sage_in[...].astype(F32)) * scale
    out[pl.ds(first + core * count, count)] = half[...].astype(F32) * scale
    out[pl.ds(first + (1 - core) * count, count)] = half_in[...].astype(F32) * scale


def exchange(own, other):
    other = swapped(other, "config", 1)
    received = [
        swapped(jnp.stack([own[s], other[s]]), "config", 2 * s) for s in range(1, own.shape[0])
    ]
    return (own, other, *received)


def local(
    features,
    cotangent,
    sage_weight,
    attn_weight,
    tile_vals,
    tile_dst,
    tile_src,
    tile_count,
    hub_ids,
    hub_weight,
):
    layout_dev, node_dev, width = features.shape
    ranks = lax.axis_size("graph")
    shares = lax.axis_size("config")
    chips = shares // 2
    share = node_dev // shares
    groups = share // SUB
    layouts = layout_dev * shares
    rows = layouts * SUB
    depth = layout_dev * SUB
    hub_dev = hub_ids.shape[0]
    hubs = hub_weight.shape[1]
    slab = (layout_dev, node_dev, width)
    spread = (node_dev, layout_dev * width)
    dma = pltpu.SemaphoreType.DMA
    ints = jnp.concatenate([hub_ids, tile_dst, tile_src, tile_count])
    ints_s = pltpu.SMEM(ints.shape, jnp.int32)
    hub_t = hub_weight.T

    mine = call(
        hub_pick,
        shape((layout_dev, hub_dev, width)),
        (ints, features),
        [VMEM] * 2,
        [ints_s, dma((1,))],
        name="hub_pick",
    )
    pieces = [mine] + [swapped(mine, "graph", s) for s in range(1, ranks)]

    adj_t, summed, pre_self = call(
        functools.partial(adjacency, hub_dev),
        (shape((node_dev, node_dev)), shape(spread, F32), shape(slab, F32)),
        (ints, tile_vals, sage_weight, features),
        [VMEM] * 4,
        [ints_s, pltpu.VMEM((node_dev, node_dev), F32), dma((1,))],
        name="adjacency",
    )

    own, other, agg, pre = call(
        sage_out,
        (
            shape((chips, groups, depth, width)),
            shape((chips, groups, depth, width)),
            shape(slab),
            shape(slab, F32),
        ),
        (*pieces, summed, pre_self, hub_t, sage_weight),
        [VMEM] * (ranks + 4),
        [pltpu.VMEM((hubs, layout_dev * width), F32), pltpu.VMEM((shares, groups, depth, width), BF)],
        name="sage_out",
    )
    hidden_in = exchange(own, other)

    cot_g, gmix, slope, rows_t, w_back = call(
        prepare,
        (
            shape((groups, rows, width)),
            shape((groups, rows, width)),
            shape(slab, F32),
            shape((2 * width, layout_dev * node_dev)),
            shape((width, 2 * width)),
        ),
        (cotangent, attn_weight, sage_weight, features, agg, pre),
        [VMEM] * 6,
        name="prepare",
    )

    half = (attn_weight.shape[0] // 2, width, width)
    own, other, hidden, mixed_t, grads_own, grads_other = call(
        attend,
        (
            shape((chips, groups, depth, width)),
            shape((chips, groups, depth, width)),
            shape((groups, rows, width)),
            shape((width, groups * rows)),
            shape(half),
            shape(half),
        ),
        (*hidden_in, cot_g, gmix, attn_weight),
        [VMEM] * (len(hidden_in) + 3),
        [
            pltpu.VMEM((groups, shares, depth, width), BF),
            pltpu.VMEM((shares, groups, depth, width), BF),
            pltpu.VMEM(attn_weight.shape, BF),
        ],
        micros=4.0,
        name="attend",
    )
    grad_in = exchange(own, other)
    masks = [1 << i for i in range(1, shares.bit_length() - 1)]
    half_sum = grads_own + swapped(grads_other, "config", 1)
    for mask in masks[:-1]:
        half_sum = half_sum + swapped(half_sum, "config", mask)

    output = call(
        outputs,
        shape((layouts, share, width)),
        (hidden, mixed_t, attn_weight),
        [VMEM] * 3,
        name="outputs",
    )

    wide, grad_self, sage_sum, hub_sum = call(
        sage_back,
        (
            shape(spread),
            shape(slab),
            shape(sage_weight.shape),
            shape((ranks, layout_dev, hub_dev, width)),
        ),
        (*grad_in, slope, rows_t, w_back, hub_t),
        [VMEM] * (len(grad_in) + 4),
        [
            pltpu.VMEM((shares, groups, layout_dev, SUB, width), F32),
            pltpu.VMEM((hubs, layout_dev * width), F32),
        ],
        name="sage_back",
    )
    while hub_sum.shape[0] > 2:
        keep = hub_sum.shape[0] // 2
        hub_sum = hub_sum[:keep] + swapped(hub_sum[keep:], "graph", keep)
    hub_in = swapped(hub_sum[1:], "graph", 1)

    sage_sum = sage_sum + swapped(sage_sum, "config", 1)
    first = sage_sum.shape[0]
    both = jnp.concatenate([sage_sum, half_sum], axis=0)
    both = both + swapped(both, "config", masks[-1])
    sage_sum, half_sum = both[:first], both[first:]
    half_in = swapped(half_sum, "config", 1)
    for mask in masks[:-2]:
        sage_sum = sage_sum + swapped(sage_sum, "config", mask)
    sage_in = swapped(sage_sum, "config", masks[-2])

    totals = call(
        tile_back,
        shape(slab, F32),
        (adj_t, wide, grad_self),
        [VMEM] * 3,
        name="tile_back",
    )
    grad_features = call(
        finish,
        shape(slab),
        (ints, totals, hub_sum, hub_in),
        [VMEM] * 4,
        [ints_s, pltpu.VMEM(slab, F32), dma((1,))],
        name="finish",
    )
    weights = call(
        functools.partial(weights_out, 1.0 / math.sqrt(layouts * node_dev)),
        shape((first + attn_weight.shape[0], width, width), F32),
        (sage_sum, sage_in, half_sum, half_in),
        [VMEM] * 4,
        name="weights_out",
    )
    return (output, grad_features, weights[None])


def solution(mesh):
    return jax.shard_map(
        local,
        mesh=mesh,
        in_specs=(
            P("config", "graph", None),
            P(None, ("graph", "config"), None),
            P(),
            P(),
            P("graph", None, None),
            P("graph"),
            P("graph"),
            P("graph"),
            P("graph"),
            P("graph", None),
        ),
        out_specs=(
            P(None, ("graph", "config"), None),
            P("config", "graph", None),
            P("graph", None, None, None),
        ),
        check_vma=False,
    )
```

```python
import functools
import math

import jax
import jax.numpy as jnp
from jax import lax
from jax.experimental import pallas as pl
from jax.experimental.pallas import tpu as pltpu
from jax.sharding import PartitionSpec as P

HEADS = 4
CAP = 20.0
SUB = 8

BF = jnp.bfloat16
F32 = jnp.float32
VMEM = pl.BlockSpec(memory_space=pltpu.VMEM)
HBM = pl.BlockSpec(memory_space=pltpu.HBM)
LIMIT = 24 * 1024 * 1024
WHOLE = 56 * 1024 * 1024


def dot(a, b):
    return jnp.dot(a, b, preferred_element_type=F32)


def dot_nt(a, b):
    return lax.dot_general(a, b, (((1,), (1,)), ((), ())), preferred_element_type=F32)


def dot_tn(a, b):
    return lax.dot_general(a, b, (((0,), (0,)), ((), ())), preferred_element_type=F32)


def shape(dims, kind=BF):
    return jax.ShapeDtypeStruct(dims, kind)


def call(kernel, outs, operands, specs, scratch=(), micros=1.0, limit=LIMIT, name=None):
    return pl.pallas_call(
        kernel,
        out_shape=outs,
        in_specs=specs,
        out_specs=jax.tree.map(lambda _: VMEM, outs),
        scratch_shapes=list(scratch),
        compiler_params=pltpu.CompilerParams(vmem_limit_bytes=limit),
        cost_estimate=pl.CostEstimate(
            flops=int(micros * 10**9), bytes_accessed=int(micros * 2**21), transcendentals=0
        ),
        name=name,
    )(*operands)


def fetch(pairs, sems):
    copies = [pltpu.make_async_copy(a, b, sems.at[i]) for i, (a, b) in enumerate(pairs)]
    for copy in copies:
        copy.start()
    return copies


def swapped(x, axis, mask):
    count = lax.axis_size(axis)
    return lax.ppermute(x, axis, [(i, i ^ mask) for i in range(count)])


def hub_pick(ids, feats, out, ids_s, feats_v, sems):
    layouts, nodes, _ = feats.shape
    copies = fetch([(ids, ids_s)] + [(feats.at[l], feats_v.at[l]) for l in range(layouts)], sems)
    hubs = out.shape[1]
    row = lax.broadcasted_iota(jnp.int32, (hubs, nodes), 0)
    col = lax.broadcasted_iota(jnp.int32, (hubs, nodes), 1)
    want = jnp.zeros((hubs, nodes), jnp.int32)
    copies[0].wait()
    for j in range(hubs):
        want = jnp.where(row == j, lax.rem(ids_s[j], nodes), want)
    hot = jnp.where(col == want, 1.0, 0.0).astype(BF)
    for l in range(layouts):
        copies[1 + l].wait()
        out[l] = dot(hot, feats_v[l]).astype(BF)


def adjacency(first, ints, tiles, weight, feats, adj_t, summed, pre_self, ints_s, adj, sems):
    copies = fetch([(ints, ints_s)], sems)
    slots, tile, _ = tiles.shape
    layouts, nodes, _ = feats.shape
    adj[...] = jnp.zeros(adj.shape, F32)
    for l in range(layouts):
        pre_self[l] = dot(feats[l], weight[0])
    copies[0].wait()
    for t in range(slots):

        @pl.when(t < ints_s[first + 2 * slots])
        def _():
            at = pl.ds(pl.multiple_of(ints_s[first + t] * tile, tile), tile)
            block = tiles[t].astype(F32)
            col = ints_s[first + slots + t]
            for s in range(nodes // tile):

                @pl.when(col == s)
                def _():
                    adj[at, pl.ds(s * tile, tile)] += block

    dense = adj[...].astype(BF)
    wide = jnp.concatenate([feats[l] for l in range(layouts)], axis=1)
    summed[...] = dot(dense, wide)
    adj_t[...] = dense.T


def sage_out(*refs):
    pieces, (summed, pre_self, hub_t, weight, own, other, agg, pre, hub_all, ready) = refs[:-10], refs[-10:]
    layouts, nodes, width = pre_self.shape
    shares, groups, _, _ = ready.shape
    hubs = pieces[0].shape[1]
    slab = lax.axis_index("graph")
    for s, piece in enumerate(pieces):
        at = pl.ds(pl.multiple_of(lax.bitwise_xor(slab, s) * hubs, hubs), hubs)
        for l in range(layouts):
            hub_all[at, l * width : (l + 1) * width] = piece[l].astype(F32)
    total = summed[...] + dot_tn(hub_t[...], hub_all[...].astype(BF))
    acts = []
    for l in range(layouts):
        mine = total[:, l * width : (l + 1) * width].astype(BF)
        agg[l] = mine
        value = pre_self[l] + dot(mine, weight[1])
        pre[l] = value
        act = value / (1.0 + jnp.exp(-value))
        acts.append(act.reshape(shares, groups, SUB, width))
    ready[...] = jnp.concatenate(acts, axis=2).astype(BF)
    hand_out(ready, own, other)


def hand_out(ready, own, other):
    me = lax.axis_index("config")
    for s in range(own.shape[0]):
        own[s] = ready[lax.bitwise_xor(me, 2 * s)]
        other[s] = ready[lax.bitwise_xor(me, 2 * s + 1)]


def arrivals(own, other, received):
    found = [(0, own[0]), (1, other[0])]
    for s, both in enumerate(received):
        found.append((2 * s + 2, both[0]))
        found.append((2 * s + 3, both[1]))
    return found


def prepare(cot, attn, weight, feats, agg, pre, cot_g, gmix, slope, rows_t, w_back):
    layouts, _, width = cot.shape
    groups = cot_g.shape[0]
    for l in range(feats.shape[0]):
        value = pre[l]
        sig = 1.0 / (1.0 + jnp.exp(-value))
        slope[l] = sig * (1.0 + value * (1.0 - sig))
        at = slice(l * feats.shape[1], (l + 1) * feats.shape[1])
        rows_t[0:width, at] = feats[l].T
        rows_t[width : 2 * width, at] = agg[l].T
    w_back[:, 0:width] = weight[0].T
    w_back[:, width : 2 * width] = weight[1].T
    for p in range(groups // 2):
        block = cot[:, 2 * SUB * p : 2 * SUB * (p + 1), :].astype(F32)
        for h in range(2):
            rows = block[:, SUB * h : SUB * (h + 1), :].reshape(layouts * SUB, width).astype(BF)
            cot_g[2 * p + h] = rows
            gmix[2 * p + h] = dot_nt(rows, attn[3]).astype(BF)


def attend(*refs):
    (own, other), received = refs[:2], refs[2:-12]
    cot_g, gmix, attn, own_out, other_out, hid_out, mixed_t, grads_own, grads_other = refs[-12:-3]
    hidden, ready, grads = refs[-3:]
    me = lax.axis_index("config")
    groups, shares, depth, width = hidden.shape
    rows = shares * depth
    head = width // HEADS
    scale = 1.0 / math.sqrt(head)
    for mask, block in arrivals(own, other, received):
        hidden[:, lax.bitwise_xor(me, mask)] = block
    w_all = jnp.concatenate([attn[0], attn[1], attn[2]], axis=1)
    lane = lax.broadcasted_iota(jnp.int32, (rows, width), 1) // head
    r = lax.broadcasted_iota(jnp.int32, (rows, HEADS * rows), 0)
    c = lax.broadcasted_iota(jnp.int32, (rows, HEADS * rows), 1)
    same = (r % SUB) == (c % SUB)
    zero = jnp.zeros((rows, width), BF)
    gap = jnp.zeros((head, rows), BF)

    def by_head(x):
        return jnp.concatenate([jnp.where(lane == e, x, zero) for e in range(HEADS)], axis=0)

    flat = hidden[...].reshape(groups * rows, width)
    hid_out[...] = flat.reshape(groups, rows, width)
    qkv = dot(flat, w_all).astype(BF)
    inputs = []
    for g in range(groups):
        q, k, v = (qkv[g * rows : (g + 1) * rows, i * width : (i + 1) * width] for i in range(3))
        inputs.append((k, v, k.T, v.T, by_head(q), by_head(gmix[g])))
    products = [(dot_nt(k, qm), dot_nt(v, gm)) for k, v, _, _, qm, gm in inputs]
    weighted = []
    for scores, d_probs in products:
        t = jnp.tanh(scores * (scale / CAP))
        w = jnp.where(same, jnp.exp2(t * (CAP * math.log2(math.e))), 0.0)
        a = w * (1.0 / jnp.sum(w, axis=0, keepdims=True))
        z = a * d_probs
        zs = jnp.sum(z, axis=0, keepdims=True)
        weighted.append((a.astype(BF), ((z - a * zs) * (scale - scale * (t * t))).astype(BF)))
    d_all, mix_t = [], []
    for (k, v, k_t, v_t, qm, gm), (p, ds) in zip(inputs, weighted):
        mix, dq = [], []
        for e in range(HEADS):
            at, span = slice(e * head, (e + 1) * head), slice(e * rows, (e + 1) * rows)
            left = jnp.concatenate(
                [jnp.concatenate([v_t[at], gap], axis=1), jnp.concatenate([gap, k_t[at]], axis=1)], axis=0
            )
            both = dot(left, jnp.concatenate([p[:, span], ds[:, span]], axis=0))
            mix.append(both[:head])
            dq.append(both[head:])
        mix_t.append(jnp.concatenate(mix, axis=0).astype(BF))
        dq = jnp.concatenate(dq, axis=0).astype(BF).T
        d_all.append(jnp.concatenate([dq, dot(ds, qm).astype(BF), dot(p, gm).astype(BF)], axis=1))
    d_all = jnp.concatenate(d_all, axis=0)
    mix_t = jnp.concatenate(mix_t, axis=1)
    mixed_t[...] = mix_t
    cots = cot_g[...].reshape(groups * rows, width)
    back = (cots.astype(F32) + dot_nt(d_all, w_all)).astype(BF).reshape(groups, shares, depth, width)
    for g in range(groups):
        ready[:, g] = back[g]
    hand_out(ready, own_out, other_out)
    total = dot(flat.T, d_all)
    for i in range(3):
        grads[i] = total[:, i * width : (i + 1) * width].astype(BF)
    grads[3] = dot(mix_t, cots).astype(BF)
    core = lax.rem(me, 2)
    half = grads_own.shape[0]
    grads_own[...] = grads[pl.ds(core * half, half)]
    grads_other[...] = grads[pl.ds((1 - core) * half, half)]


def outputs(hidden, mixed_t, attn, mine, theirs, out, half):
    half[...] = add(mine, theirs)
    groups, rows, width = hidden.shape
    layouts = rows // SUB
    projected = dot_tn(mixed_t[...], attn[3])
    for p in range(groups // 2):
        pair = []
        for g in (2 * p, 2 * p + 1):
            both = hidden[g].astype(F32) + projected[g * rows : (g + 1) * rows]
            pair.append(both.reshape(layouts, SUB, width))
        out[:, 2 * SUB * p : 2 * SUB * (p + 1), :] = jnp.concatenate(pair, axis=1).astype(BF)


def sage_back(*refs):
    (own, other), received = refs[:2], refs[2:-10]
    slope, rows_t, w_back, hub_t, wide, self_out, grads, hub_out, parts, hub_sum = refs[-10:]
    me = lax.axis_index("config")
    layouts, width = parts.shape[2], parts.shape[4]
    nodes = slope.shape[1]
    for mask, block in arrivals(own, other, received):
        parts[lax.bitwise_xor(me, mask)] = block[...].astype(F32).reshape(parts.shape[1:])
    grad_pre, grad_agg = [], []
    for l in range(layouts):
        gpre = (parts[:, :, l].reshape(nodes, width) * slope[l]).astype(BF)
        both = dot(gpre, w_back[...]).astype(BF)
        grad_pre.append(gpre)
        self_out[l] = both[:, 0:width]
        grad_agg.append(both[:, width : 2 * width])
    spread = jnp.concatenate(grad_agg, axis=1)
    wide[...] = spread
    hub_sum[...] = dot(hub_t[...], spread)
    slab = lax.axis_index("graph")
    ranks, _, hubs, _ = hub_out.shape
    for s in range(ranks):
        at = pl.ds(pl.multiple_of(lax.bitwise_xor(slab, s) * hubs, hubs), hubs)
        for l in range(layouts):
            hub_out[s, l] = hub_sum[at, l * width : (l + 1) * width].astype(BF)
    both = dot(rows_t[...], jnp.concatenate(grad_pre, axis=0))
    grads[0] = both[0:width].astype(BF)
    grads[1] = both[width : 2 * width].astype(BF)


def tile_back(adj_t, wide, grad_self, totals):
    back = dot(adj_t[...], wide[...])
    layouts, _, width = totals.shape
    for l in range(layouts):
        totals[l] = grad_self[l].astype(F32) + back[:, l * width : (l + 1) * width]


def add(a, b):
    return (a[...].astype(F32) + b[...].astype(F32)).astype(BF)


def join(sage, sage_in, half, half_in, sage_sum, half_sum):
    sage_sum[...] = add(sage, sage_in)
    half_sum[...] = add(half, half_in)


def finish(ints, totals, hub_own, hub_in, out, ints_s, rows, sems):
    copies = fetch([(ints, ints_s)], sems)
    layouts, nodes, _ = totals.shape
    hubs = hub_own.shape[-2]
    summed = [hub_own[0, l].astype(F32) + hub_in[0, l].astype(F32) for l in range(layouts)]
    rows[...] = totals[...]
    copies[0].wait()
    for l in range(layouts):
        for j in range(hubs):
            at = pl.ds(lax.rem(ints_s[j], nodes), 1)
            rows[l, at, :] += summed[l][j : j + 1, :]
    out[...] = rows[...].astype(BF)


def weights_out(scale, sage, sage_in, half, half_in, out):
    first = sage.shape[0]
    count = half.shape[0]
    core = lax.rem(lax.axis_index("config"), 2)
    out[0:first] = (sage[...].astype(F32) + sage_in[...].astype(F32)) * scale
    out[pl.ds(first + core * count, count)] = half[...].astype(F32) * scale
    out[pl.ds(first + (1 - core) * count, count)] = half_in[...].astype(F32) * scale


def exchange(own, other):
    other = swapped(other, "config", 1)
    received = [
        swapped(jnp.stack([own[s], other[s]]), "config", 2 * s) for s in range(1, own.shape[0])
    ]
    return (own, other, *received)


def local(
    features,
    cotangent,
    sage_weight,
    attn_weight,
    tile_vals,
    tile_dst,
    tile_src,
    tile_count,
    hub_ids,
    hub_weight,
):
    layout_dev, node_dev, width = features.shape
    ranks = lax.axis_size("graph")
    shares = lax.axis_size("config")
    chips = shares // 2
    share = node_dev // shares
    groups = share // SUB
    layouts = layout_dev * shares
    rows = layouts * SUB
    depth = layout_dev * SUB
    hub_dev = hub_ids.shape[0]
    hubs = hub_weight.shape[1]
    slab = (layout_dev, node_dev, width)
    spread = (node_dev, layout_dev * width)
    dma = pltpu.SemaphoreType.DMA
    ints = jnp.concatenate([hub_ids, tile_dst, tile_src, tile_count])
    ints_s = pltpu.SMEM(ints.shape, jnp.int32)
    hub_t = hub_weight.T

    mine = call(
        hub_pick,
        shape((layout_dev, hub_dev, width)),
        (hub_ids, features),
        [HBM] * 2,
        [pltpu.SMEM((hub_dev,), jnp.int32), pltpu.VMEM(slab, BF), dma((1 + layout_dev,))],
        limit=WHOLE,
        name="hub_pick",
    )
    pieces = [mine] + [swapped(mine, "graph", s) for s in range(1, ranks)]

    adj_t, summed, pre_self = call(
        functools.partial(adjacency, hub_dev),
        (shape((node_dev, node_dev)), shape(spread, F32), shape(slab, F32)),
        (ints, tile_vals, sage_weight, features),
        [VMEM] * 4,
        [ints_s, pltpu.VMEM((node_dev, node_dev), F32), dma((1,))],
        name="adjacency",
    )

    own, other, agg, pre = call(
        sage_out,
        (
            shape((chips, groups, depth, width)),
            shape((chips, groups, depth, width)),
            shape(slab),
            shape(slab, F32),
        ),
        (*pieces, summed, pre_self, hub_t, sage_weight),
        [VMEM] * (ranks + 4),
        [pltpu.VMEM((hubs, layout_dev * width), F32), pltpu.VMEM((shares, groups, depth, width), BF)],
        name="sage_out",
    )
    hidden_in = exchange(own, other)

    cot_g, gmix, slope, rows_t, w_back = call(
        prepare,
        (
            shape((groups, rows, width)),
            shape((groups, rows, width)),
            shape(slab, F32),
            shape((2 * width, layout_dev * node_dev)),
            shape((width, 2 * width)),
        ),
        (cotangent, attn_weight, sage_weight, features, agg, pre),
        [VMEM] * 6,
        name="prepare",
    )

    half = (attn_weight.shape[0] // 2, width, width)
    own, other, hidden, mixed_t, grads_own, grads_other = call(
        attend,
        (
            shape((chips, groups, depth, width)),
            shape((chips, groups, depth, width)),
            shape((groups, rows, width)),
            shape((width, groups * rows)),
            shape(half),
            shape(half),
        ),
        (*hidden_in, cot_g, gmix, attn_weight),
        [VMEM] * (len(hidden_in) + 3),
        [
            pltpu.VMEM((groups, shares, depth, width), BF),
            pltpu.VMEM((shares, groups, depth, width), BF),
            pltpu.VMEM(attn_weight.shape, BF),
        ],
        micros=4.0,
        name="attend",
    )
    grad_in = exchange(own, other)
    output, half_sum = call(
        outputs,
        (shape((layouts, share, width)), shape(half)),
        (hidden, mixed_t, attn_weight, grads_own, swapped(grads_other, "config", 1)),
        [VMEM] * 5,
        name="outputs",
    )

    wide, grad_self, sage_sum, hub_sum = call(
        sage_back,
        (
            shape(spread),
            shape(slab),
            shape(sage_weight.shape),
            shape((ranks, layout_dev, hub_dev, width)),
        ),
        (*grad_in, slope, rows_t, w_back, hub_t),
        [VMEM] * (len(grad_in) + 4),
        [
            pltpu.VMEM((shares, groups, layout_dev, SUB, width), F32),
            pltpu.VMEM((hubs, layout_dev * width), F32),
        ],
        name="sage_back",
    )
    while hub_sum.shape[0] > 2:
        keep = hub_sum.shape[0] // 2
        hub_sum = hub_sum[:keep] + swapped(hub_sum[keep:], "graph", keep)
    hub_in = swapped(hub_sum[1:], "graph", 1)

    masks = [1 << i for i in range(1, shares.bit_length() - 1)]
    half_in = swapped(half_sum, "config", masks[0])
    sage_in = swapped(sage_sum, "config", 1)
    for mask, later in zip(masks, masks[1:] + [1]):
        sage_sum, half_sum = call(
            join,
            (shape(sage_weight.shape), shape(half)),
            (sage_sum, sage_in, half_sum, half_in),
            [VMEM] * 4,
            micros=0.1,
            name="join",
        )
        sage_in = swapped(sage_sum, "config", mask)
        half_in = swapped(half_sum, "config", later)

    totals = call(
        tile_back,
        shape(slab, F32),
        (adj_t, wide, grad_self),
        [VMEM] * 3,
        name="tile_back",
    )
    grad_features = call(
        finish,
        shape(slab),
        (ints, totals, hub_sum, hub_in),
        [VMEM] * 4,
        [ints_s, pltpu.VMEM(slab, F32), dma((1,))],
        name="finish",
    )
    weights = call(
        functools.partial(weights_out, 1.0 / math.sqrt(layouts * node_dev)),
        shape((sage_weight.shape[0] + attn_weight.shape[0], width, width), F32),
        (sage_sum, sage_in, half_sum, half_in),
        [VMEM] * 4,
        name="weights_out",
    )
    return (output, grad_features, weights[None])


def solution(mesh):
    return jax.shard_map(
        local,
        mesh=mesh,
        in_specs=(
            P("config", "graph", None),
            P(None, ("graph", "config"), None),
            P(),
            P(),
            P("graph", None, None),
            P("graph"),
            P("graph"),
            P("graph"),
            P("graph"),
            P("graph", None),
        ),
        out_specs=(
            P(None, ("graph", "config"), None),
            P("config", "graph", None),
            P("graph", None, None, None),
        ),
        check_vma=False,
    )
```

```python
import functools
import math

import jax
import jax.numpy as jnp
from jax import lax
from jax.experimental import pallas as pl
from jax.experimental.pallas import tpu as pltpu
from jax.sharding import PartitionSpec as P

HEADS = 4
CAP = 20.0
SUB = 8

BF = jnp.bfloat16
F32 = jnp.float32
VMEM = pl.BlockSpec(memory_space=pltpu.VMEM)
ANY = pl.BlockSpec(memory_space=pl.ANY)
HBM = pl.BlockSpec(memory_space=pltpu.HBM)
LIMIT = 24 * 1024 * 1024
WHOLE = 56 * 1024 * 1024


def dot(a, b):
    return jnp.dot(a, b, preferred_element_type=F32)


def dot_nt(a, b):
    return lax.dot_general(a, b, (((1,), (1,)), ((), ())), preferred_element_type=F32)


def dot_tn(a, b):
    return lax.dot_general(a, b, (((0,), (0,)), ((), ())), preferred_element_type=F32)


def shape(dims, kind=BF):
    return jax.ShapeDtypeStruct(dims, kind)


def call(kernel, outs, operands, specs, scratch=(), micros=1.0, limit=LIMIT, outs_at=VMEM, name=None):
    return pl.pallas_call(
        kernel,
        out_shape=outs,
        in_specs=specs,
        out_specs=jax.tree.map(lambda _: outs_at, outs),
        scratch_shapes=list(scratch),
        compiler_params=pltpu.CompilerParams(vmem_limit_bytes=limit),
        cost_estimate=pl.CostEstimate(
            flops=int(micros * 10**9), bytes_accessed=int(micros * 2**21), transcendentals=0
        ),
        name=name,
    )(*operands)


def fetch(pairs, sems):
    copies = [pltpu.make_async_copy(a, b, sems.at[i]) for i, (a, b) in enumerate(pairs)]
    for copy in copies:
        copy.start()
    return copies


def swapped(x, axis, mask):
    count = lax.axis_size(axis)
    return lax.ppermute(x, axis, [(i, i ^ mask) for i in range(count)])


def one_hot(ids, hubs, nodes):
    row = lax.broadcasted_iota(jnp.int32, (hubs, nodes), 0)
    col = lax.broadcasted_iota(jnp.int32, (hubs, nodes), 1)
    want = jnp.zeros((hubs, nodes), jnp.int32)
    for j in range(hubs):
        want = jnp.where(row == j, lax.rem(ids[j], nodes), want)
    return jnp.where(col == want, 1.0, 0.0).astype(BF)


def hub_pick(ids, feats, out, ids_s, feats_v, sems):
    layouts, nodes, _ = feats.shape
    copies = fetch([(ids, ids_s)] + [(feats.at[l], feats_v.at[l]) for l in range(layouts)], sems)
    copies[0].wait()
    hot = one_hot(ids_s, out.shape[1], nodes)
    for l in range(layouts):
        copies[1 + l].wait()
        out[l] = dot(hot, feats_v[l]).astype(BF)


def core_rows(ref, lead, core):
    block = ref[lead + (slice(None), pl.ds(core, 1))]
    return block.reshape(block.shape[0] * block.shape[2], block.shape[3])


def adjacency(first, ints, tiles, weight, feats, other, whole, summed, pre_self, chosen, mine, hot, ints_s, adj, dense, sems):
    copies = fetch([(ints, ints_s)], sems)
    slots, tile, _ = tiles.shape
    layouts, chips, cores, share, width = feats.shape
    nodes = chips * cores * share
    core = lax.rem(lax.axis_index("config"), 2)
    adj[...] = jnp.zeros(adj.shape, F32)
    for l in range(2 * layouts):
        chosen[l] = core_rows((feats, other)[l // layouts], (l % layouts,), core)
        pre_self[l] = dot(chosen[l], weight[0])
    copies[0].wait()
    for t in range(slots):

        @pl.when(t < ints_s[first + 2 * slots])
        def _():
            at = pl.ds(pl.multiple_of(ints_s[first + t] * tile, tile), tile)
            block = tiles[t].astype(F32)
            col = ints_s[first + slots + t]
            for s in range(nodes // tile):

                @pl.when(col == s)
                def _():
                    adj[at, pl.ds(s * tile, tile)] += block

    whole[...] = adj[...].astype(BF)
    dense[...] = whole[...].reshape(dense.shape)
    wide = [x[l].reshape(nodes, width) for x in (feats, other) for l in range(layouts)]
    summed[...] = dot(core_rows(dense, (), core), jnp.concatenate(wide, axis=1))
    hot[...] = one_hot(ints_s, mine.shape[1], nodes)
    for l in range(layouts):
        mine[l] = dot(hot[...], wide[l]).astype(BF)


def sage_out(*refs):
    hub_rows, (summed, pre_self, hub_weight, weight) = refs[:2], refs[2:6]
    blocks, (agg, pre, ready) = refs[6:-3], refs[-3:]
    layouts, nodes, width = pre_self.shape
    chips, groups, _, _ = ready.shape
    me = lax.axis_index("config")
    hub_all = jnp.concatenate([x[...] for x in hub_rows], axis=1)
    total = summed[...] + dot(core_rows(hub_weight, (), lax.rem(me, 2)), hub_all)
    acts = []
    for l in range(layouts):
        mine = total[:, l * width : (l + 1) * width].astype(BF)
        agg[l] = mine
        value = pre_self[l] + dot(mine, weight[1])
        pre[l] = value
        act = value / (1.0 + jnp.exp(-value))
        acts.append(act.reshape(chips, groups, SUB, width))
    ready[...] = jnp.concatenate(acts, axis=2).astype(BF)
    for s, block in enumerate(blocks):
        block[...] = ready[lax.bitwise_xor(me // 2, s)]


def prepare(cot, attn, weight, feats, agg, pre, adj, cot_g, gmix, slope, rows_t, w_back, adj_t):
    layouts, _, width = cot.shape
    groups = cot_g.shape[0]
    adj_t[...] = adj[...].T
    for l in range(feats.shape[0]):
        value = pre[l]
        sig = 1.0 / (1.0 + jnp.exp(-value))
        slope[l] = sig * (1.0 + value * (1.0 - sig))
        at = slice(l * feats.shape[1], (l + 1) * feats.shape[1])
        rows_t[0:width, at] = feats[l].T
        rows_t[width : 2 * width, at] = agg[l].T
    w_back[:, 0:width] = weight[0].T
    w_back[:, width : 2 * width] = weight[1].T
    for p in range(groups // 2):
        block = cot[:, 2 * SUB * p : 2 * SUB * (p + 1), :].astype(F32)
        for h in range(2):
            rows = block[:, SUB * h : SUB * (h + 1), :].reshape(layouts * SUB, width).astype(BF)
            cot_g[2 * p + h] = rows
            gmix[2 * p + h] = dot_nt(rows, attn[3]).astype(BF)


def attend(*refs):
    hidden, ready, grads, pieces = refs[-4:]
    groups, shares, depth, width = hidden.shape
    chips = shares // 2
    blocks, (cot_g, gmix, attn) = refs[:chips], refs[chips : chips + 3]
    outs, (hid_out, mixed_t) = refs[chips + 3 : -6], refs[-6:-4]
    me = lax.axis_index("config")
    rows = shares * depth
    head = width // HEADS
    scale = 1.0 / math.sqrt(head)
    for s, block in enumerate(blocks):
        for core in range(2):
            hidden[:, lax.bitwise_xor(me, 2 * s + core)] = block[:, core * depth : (core + 1) * depth]
    w_all = jnp.concatenate([attn[0], attn[1], attn[2]], axis=1)
    lane = lax.broadcasted_iota(jnp.int32, (rows, width), 1) // head
    r = lax.broadcasted_iota(jnp.int32, (rows, HEADS * rows), 0)
    c = lax.broadcasted_iota(jnp.int32, (rows, HEADS * rows), 1)
    same = (r % SUB) == (c % SUB)
    zero = jnp.zeros((rows, width), BF)
    gap = jnp.zeros((head, rows), BF)

    def by_head(x):
        return jnp.concatenate([jnp.where(lane == e, x, zero) for e in range(HEADS)], axis=0)

    flat = hidden[...].reshape(groups * rows, width)
    hid_out[...] = flat.reshape(groups, rows, width)
    qkv = dot(flat, w_all).astype(BF)
    inputs = []
    for g in range(groups):
        q, k, v = (qkv[g * rows : (g + 1) * rows, i * width : (i + 1) * width] for i in range(3))
        inputs.append((k, v, k.T, v.T, by_head(q), by_head(gmix[g])))
    products = [(dot_nt(k, qm), dot_nt(v, gm)) for k, v, _, _, qm, gm in inputs]
    weighted = []
    for scores, d_probs in products:
        t = jnp.tanh(scores * (scale / CAP))
        w = jnp.where(same, jnp.exp2(t * (CAP * math.log2(math.e))), 0.0)
        a = w * (1.0 / jnp.sum(w, axis=0, keepdims=True))
        z = a * d_probs
        zs = jnp.sum(z, axis=0, keepdims=True)
        weighted.append((a.astype(BF), ((z - a * zs) * (scale - scale * (t * t))).astype(BF)))
    d_all, mix_t = [], []
    for (k, v, k_t, v_t, qm, gm), (p, ds) in zip(inputs, weighted):
        mix, dq = [], []
        for e in range(HEADS):
            at, span = slice(e * head, (e + 1) * head), slice(e * rows, (e + 1) * rows)
            left = jnp.concatenate(
                [jnp.concatenate([v_t[at], gap], axis=1), jnp.concatenate([gap, k_t[at]], axis=1)], axis=0
            )
            both = dot(left, jnp.concatenate([p[:, span], ds[:, span]], axis=0))
            mix.append(both[:head])
            dq.append(both[head:])
        mix_t.append(jnp.concatenate(mix, axis=0).astype(BF))
        dq = jnp.concatenate(dq, axis=0).astype(BF).T
        d_all.append(jnp.concatenate([dq, dot(ds, qm).astype(BF), dot(p, gm).astype(BF)], axis=1))
    d_all = jnp.concatenate(d_all, axis=0)
    mix_t = jnp.concatenate(mix_t, axis=1)
    mixed_t[...] = mix_t
    cots = cot_g[...].reshape(groups * rows, width)
    back = (cots.astype(F32) + dot_nt(d_all, w_all)).astype(BF).reshape(groups, shares, depth, width)
    for g in range(groups):
        ready[:, g] = back[g]
    total = dot(flat.T, d_all)
    for i in range(3):
        grads[i] = total[:, i * width : (i + 1) * width].astype(BF)
    grads[3] = dot(mix_t, cots).astype(BF)
    shared = grads[...].reshape(chips, -1, width)
    pieces[...] = shared
    count = groups * 2 * depth
    for s, block in enumerate(outs):
        pair = [ready[lax.bitwise_xor(me, 2 * s + core)] for core in range(2)]
        block[0:count] = jnp.concatenate(pair, axis=1).reshape(count, width)
        block[count:] = pieces[lax.bitwise_xor(me // 2, s)]


def outputs(hidden, mixed_t, attn, _, out, done):
    done[...] = jnp.zeros(done.shape, F32)
    groups, rows, width = hidden.shape
    layouts = rows // SUB
    projected = dot_tn(mixed_t[...], attn[3])
    for p in range(groups // 2):
        pair = []
        for g in (2 * p, 2 * p + 1):
            both = hidden[g].astype(F32) + projected[g * rows : (g + 1) * rows]
            pair.append(both.reshape(layouts, SUB, width))
        out[:, 2 * SUB * p : 2 * SUB * (p + 1), :] = jnp.concatenate(pair, axis=1).astype(BF)


def sage_back(*refs):
    parts, hub_sum = refs[-2:]
    chips, _, layouts, _, width = parts.shape
    blocks, (slope, rows_t, w_back, hub_weight) = refs[:chips], refs[chips : chips + 4]
    mine, theirs, sums, hub_mine, hub_theirs = refs[chips + 5 : -2]
    me = lax.axis_index("config")
    nodes = slope.shape[1]
    count = parts.shape[1] * layouts * SUB
    for s, block in enumerate(blocks):
        parts[lax.bitwise_xor(me // 2, s)] = block[0:count].astype(F32).reshape(parts.shape[1:])
    sums[2 * width :] = sum(block[count:].astype(F32) for block in blocks).astype(BF)
    half = layouts // 2
    grad_pre, grad_agg = [], []
    for l in range(layouts):
        gpre = (parts[:, :, l].reshape(nodes, width) * slope[l]).astype(BF)
        (mine, theirs)[l // half][l % half] = gpre
        grad_pre.append(gpre)
        grad_agg.append(dot(gpre, w_back[:, width : 2 * width]).astype(BF))
    both = dot(rows_t[...], jnp.concatenate(grad_pre, axis=0))
    sums[0 : 2 * width] = both.astype(BF)
    hub_sum[...] = dot_tn(core_rows(hub_weight, (), lax.rem(me, 2)), jnp.concatenate(grad_agg, axis=1))
    slab = lax.axis_index("graph")
    ranks, _, hubs, _ = hub_mine.shape
    for s in range(ranks):
        at = pl.ds(pl.multiple_of(lax.bitwise_xor(slab, s) * hubs, hubs), hubs)
        for l in range(layouts):
            (hub_mine, hub_theirs)[l // half][s, l % half] = hub_sum[at, l * width : (l + 1) * width].astype(BF)


def tile_back(adj_t, w_back, mine, theirs, totals, whole):
    layouts, nodes, width = totals.shape
    core = lax.rem(lax.axis_index("config"), 2)
    for l in range(layouts):
        for part, at in ((mine, core), (theirs, 1 - core)):
            whole[l, :, pl.ds(at, 1)] = part[l].reshape(whole.shape[1], 1, whole.shape[3], width)
    grad_self, grad_agg = [], []
    for l in range(layouts):
        both = dot(whole[l].reshape(nodes, width), w_back[...]).astype(BF)
        grad_self.append(both[:, 0:width])
        grad_agg.append(both[:, width : 2 * width])
    back = dot(adj_t[...], jnp.concatenate(grad_agg, axis=1))
    for l in range(layouts):
        totals[l] = grad_self[l].astype(F32) + back[:, l * width : (l + 1) * width]


def add(a, b):
    return (a[...].astype(F32) + b[...].astype(F32)).astype(BF)


def join(*refs):
    pairs = len(refs) // 3
    for i in range(pairs):
        refs[2 * pairs + i][...] = add(refs[2 * i], refs[2 * i + 1])


def joined(*operands):
    return call(
        join,
        [shape(x.shape) for x in operands[::2]],
        operands,
        [VMEM] * len(operands),
        micros=0.1,
        name="join",
    )


def by_slab(*refs):
    pieces, (rows, work) = refs[:-2], refs[-2:]
    layouts, hubs, width = pieces[0].shape
    slab = lax.axis_index("graph")
    for s, piece in enumerate(pieces):
        at = pl.ds(pl.multiple_of(lax.bitwise_xor(slab, s) * hubs, hubs), hubs)
        for l in range(layouts):
            work[at, l * width : (l + 1) * width] = piece[l].astype(F32)
    rows[...] = work[...].astype(BF)


def finish(hot, totals, hub_own, hub_in, _, out, work, sems):
    layouts, nodes, width = totals.shape
    summed = [hub_own[0, l].astype(F32) + hub_in[0, l].astype(F32) for l in range(layouts)]
    upper = [x.astype(BF) for x in summed]
    lower = [(x - y.astype(F32)).astype(BF) for x, y in zip(summed, upper)]
    twice = jnp.concatenate([hot[...], hot[...]], axis=0)
    copies = []
    for l in range(layouts):
        added = dot_tn(twice, jnp.concatenate([upper[l], lower[l]], axis=0))
        work[l] = (totals[l] + added).astype(BF)
        copies.append(pltpu.make_async_copy(work.at[l], out.at[l], sems.at[l]))
        copies[l].start()
    for copy in copies:
        copy.wait()


def weights_out(scale, *refs):
    sums, (out, done, work) = refs[:-3], refs[-3:]
    done[...] = jnp.zeros(done.shape, F32)
    width = out.shape[1]
    first = 2 * width
    share = sums[0].shape[0] - first
    chip = lax.axis_index("config") // 2
    for s, part in enumerate(sums):
        at = lax.bitwise_xor(chip, s)
        work[at] = part[0:first].astype(F32)
        out[pl.ds(pl.multiple_of(first + at * share, share), share)] = part[first:].astype(F32) * scale
    total = work[0]
    for s in range(1, len(sums)):
        total = total + work[s]
    out[0:first] = total * scale


def exchange(blocks):
    return [swapped(block, "config", 2 * s) if s else block for s, block in enumerate(blocks)]


def local(
    features,
    cotangent,
    sage_weight,
    attn_weight,
    tile_vals,
    tile_dst,
    tile_src,
    tile_count,
    hub_ids,
    hub_weight,
):
    layout_dev, node_dev, width = features.shape
    ranks = lax.axis_size("graph")
    shares = lax.axis_size("config")
    chips = shares // 2
    share = node_dev // shares
    groups = share // SUB
    layouts = layout_dev * shares
    rows = layouts * SUB
    depth = 2 * layout_dev * SUB
    hub_dev = hub_ids.shape[0]
    hubs = hub_weight.shape[1]
    slab = (layout_dev, node_dev, width)
    part = (2 * layout_dev, node_dev // 2, width)
    block = (groups, depth, width)
    dma = pltpu.SemaphoreType.DMA
    ints = jnp.concatenate([hub_ids, tile_dst, tile_src, tile_count])
    ints_s = pltpu.SMEM(ints.shape, jnp.int32)
    hub_weight = hub_weight.reshape(chips, 2, share, hubs)
    by_core = (layout_dev, chips, 2, share, width)

    mine = call(
        hub_pick,
        shape((layout_dev, hub_dev, width)),
        (hub_ids, features),
        [HBM] * 2,
        [pltpu.SMEM((hub_dev,), jnp.int32), pltpu.VMEM(slab, BF), dma((1 + layout_dev,))],
        limit=WHOLE,
        name="hub_pick",
    )
    pieces = [swapped(mine, "graph", s) for s in range(1, ranks)]
    other = swapped(features, "config", 1)

    adj, summed, pre_self, feats, mine, hot = call(
        functools.partial(adjacency, hub_dev),
        (
            shape((node_dev, node_dev)),
            shape((part[1], part[0] * width), F32),
            shape(part, F32),
            shape(part),
            shape(mine.shape),
            shape((hub_dev, node_dev)),
        ),
        (ints, tile_vals, sage_weight, features.reshape(by_core), other.reshape(by_core)),
        [VMEM] * 5,
        [
            ints_s,
            pltpu.VMEM((node_dev, node_dev), F32),
            pltpu.VMEM((chips, 2, share, node_dev), BF),
            dma((1,)),
        ],
        name="adjacency",
    )

    hub_rows = call(
        by_slab,
        shape((hubs, layout_dev * width)),
        (mine, *pieces),
        [VMEM] * ranks,
        [pltpu.VMEM((hubs, layout_dev * width), F32)],
        micros=0.1,
        name="by_slab",
    )
    hub_rows = (hub_rows, swapped(hub_rows, "config", 1))

    *blocks, agg, pre = call(
        sage_out,
        (*[shape(block)] * chips, shape(part), shape(part, F32)),
        (*hub_rows, summed, pre_self, hub_weight, sage_weight),
        [VMEM] * 6,
        [pltpu.VMEM((chips, *block), BF)],
        name="sage_out",
    )
    hidden_in = exchange(blocks)

    cot_g, gmix, slope, rows_t, w_back, adj_t = call(
        prepare,
        (
            shape((groups, rows, width)),
            shape((groups, rows, width)),
            shape(part, F32),
            shape((2 * width, part[0] * part[1])),
            shape((width, 2 * width)),
            shape((node_dev, node_dev)),
        ),
        (cotangent, attn_weight, sage_weight, feats, agg, pre, adj),
        [VMEM] * 7,
        name="prepare",
    )

    share_rows = attn_weight.shape[0] * width // chips
    back = (groups * depth + share_rows, width)
    *blocks, hidden, mixed_t = call(
        attend,
        (
            *[shape(back)] * chips,
            shape((groups, rows, width)),
            shape((width, groups * rows)),
        ),
        (*hidden_in, cot_g, gmix, attn_weight),
        [VMEM] * (len(hidden_in) + 3),
        [
            pltpu.VMEM((groups, shares, depth // 2, width), BF),
            pltpu.VMEM((shares, groups, depth // 2, width), BF),
            pltpu.VMEM(attn_weight.shape, BF),
            pltpu.VMEM((chips, share_rows, width), BF),
        ],
        micros=4.0,
        name="attend",
    )
    grad_in = exchange(blocks)
    token = shape((SUB, width), F32)
    output, shown = call(
        outputs,
        (shape((layouts, share, width)), token),
        (hidden, mixed_t, attn_weight, grad_in[1]),
        [VMEM] * 3 + [ANY],
        name="outputs",
    )

    hub_shape = (ranks, layout_dev, hub_dev, width)
    mine = (layout_dev, node_dev // 2, width)
    mine, theirs, sums, hub_sum, hub_theirs = call(
        sage_back,
        (shape(mine), shape(mine), shape((2 * width + share_rows, width)), shape(hub_shape), shape(hub_shape)),
        (*grad_in, slope, rows_t, w_back, hub_weight, shown),
        [VMEM] * (chips + 4) + [ANY],
        [
            pltpu.VMEM((chips, groups, 2 * layout_dev, SUB, width), F32),
            pltpu.VMEM((hubs, part[0] * width), F32),
        ],
        name="sage_back",
    )
    hub_in = swapped(hub_theirs, "config", 1)
    theirs = swapped(theirs, "config", 1)
    sums, hub_sum = joined(sums, swapped(sums, "config", 1), hub_sum, hub_in)
    sums = [swapped(sums, "config", 2 * s) if s else sums for s in range(chips)]
    totals = call(
        tile_back,
        shape(slab, F32),
        (adj_t, w_back, mine, theirs),
        [VMEM] * 4,
        [pltpu.VMEM(by_core, BF)],
        name="tile_back",
    )
    while hub_sum.shape[0] > 2:
        keep = hub_sum.shape[0] // 2
        hub_sum = hub_sum[:keep] + swapped(hub_sum[keep:], "graph", keep)
    hub_in = swapped(hub_sum[1:], "graph", 1)
    count = sage_weight.shape[0] + attn_weight.shape[0]
    weights, summed = call(
        functools.partial(weights_out, 1.0 / math.sqrt(layouts * node_dev)),
        (shape((count * width, width), F32), token),
        sums,
        [VMEM] * chips,
        [pltpu.VMEM((chips, 2 * width, width), F32)],
        name="weights_out",
    )
    grad_features = call(
        finish,
        shape(slab),
        (hot, totals, hub_sum, hub_in, summed),
        [VMEM] * 4 + [ANY],
        [pltpu.VMEM(slab, BF), dma((layout_dev,))],
        outs_at=HBM,
        name="finish",
    )
    return (output, grad_features, weights.reshape(1, count, width, width))


def solution(mesh):
    return jax.shard_map(
        local,
        mesh=mesh,
        in_specs=(
            P("config", "graph", None),
            P(None, ("graph", "config"), None),
            P(),
            P(),
            P("graph", None, None),
            P("graph"),
            P("graph"),
            P("graph"),
            P("graph"),
            P("graph", None),
        ),
        out_specs=(
            P(None, ("graph", "config"), None),
            P("config", "graph", None),
            P("graph", None, None, None),
        ),
        check_vma=False,
    )
```

```python
import functools
import math

import jax
import jax.numpy as jnp
from jax import lax
from jax.experimental import pallas as pl
from jax.experimental.pallas import tpu as pltpu
from jax.sharding import PartitionSpec as P

HEADS = 4
CAP = 20.0
SUB = 8

BF = jnp.bfloat16
F32 = jnp.float32
VMEM = pl.BlockSpec(memory_space=pltpu.VMEM)
ANY = pl.BlockSpec(memory_space=pl.ANY)
HBM = pl.BlockSpec(memory_space=pltpu.HBM)
LIMIT = 24 * 1024 * 1024
WHOLE = 56 * 1024 * 1024


def dot(a, b):
    return jnp.dot(a, b, preferred_element_type=F32)


def dot_nt(a, b):
    return lax.dot_general(a, b, (((1,), (1,)), ((), ())), preferred_element_type=F32)


def dot_tn(a, b):
    return lax.dot_general(a, b, (((0,), (0,)), ((), ())), preferred_element_type=F32)


def shape(dims, kind=BF):
    return jax.ShapeDtypeStruct(dims, kind)


def call(kernel, outs, operands, specs, scratch=(), micros=1.0, limit=LIMIT, outs_at=VMEM, name=None):
    return pl.pallas_call(
        kernel,
        out_shape=outs,
        in_specs=specs,
        out_specs=jax.tree.map(lambda _: outs_at, outs),
        scratch_shapes=list(scratch),
        compiler_params=pltpu.CompilerParams(vmem_limit_bytes=limit),
        cost_estimate=pl.CostEstimate(
            flops=int(micros * 10**9), bytes_accessed=int(micros * 2**21), transcendentals=0
        ),
        name=name,
    )(*operands)


def fetch(pairs, sems):
    copies = [pltpu.make_async_copy(a, b, sems.at[i]) for i, (a, b) in enumerate(pairs)]
    for copy in copies:
        copy.start()
    return copies


def swapped(x, axis, mask):
    count = lax.axis_size(axis)
    return lax.ppermute(x, axis, [(i, i ^ mask) for i in range(count)])


def one_hot(ids, hubs, nodes):
    row = lax.broadcasted_iota(jnp.int32, (hubs, nodes), 0)
    col = lax.broadcasted_iota(jnp.int32, (hubs, nodes), 1)
    want = jnp.zeros((hubs, nodes), jnp.int32)
    for j in range(hubs):
        want = jnp.where(row == j, lax.rem(ids[j], nodes), want)
    return jnp.where(col == want, 1.0, 0.0).astype(BF)


def hub_pick(ids, feats, out, ids_s, feats_v, sems):
    layouts, nodes, _ = feats.shape
    copies = fetch([(ids, ids_s)] + [(feats.at[l], feats_v.at[l]) for l in range(layouts)], sems)
    copies[0].wait()
    hot = one_hot(ids_s, out.shape[1], nodes)
    for l in range(layouts):
        copies[1 + l].wait()
        out[l] = dot(hot, feats_v[l]).astype(BF)


def core_rows(ref, lead, core):
    block = ref[lead + (slice(None), pl.ds(core, 1))]
    return block.reshape(block.shape[0] * block.shape[2], block.shape[3])


def adjacency(first, ints, tiles, weight, feats, other, whole, summed, pre_self, chosen, mine, hot, ints_s, adj, dense, sems):
    copies = fetch([(ints, ints_s)], sems)
    slots, tile, _ = tiles.shape
    layouts, chips, cores, share, width = feats.shape
    nodes = chips * cores * share
    core = lax.rem(lax.axis_index("config"), 2)
    adj[...] = jnp.zeros(adj.shape, F32)
    for l in range(2 * layouts):
        chosen[l] = core_rows((feats, other)[l // layouts], (l % layouts,), core)
        pre_self[l] = dot(chosen[l], weight[0])
    copies[0].wait()
    for t in range(slots):

        @pl.when(t < ints_s[first + 2 * slots])
        def _():
            at = pl.ds(pl.multiple_of(ints_s[first + t] * tile, tile), tile)
            block = tiles[t].astype(F32)
            col = ints_s[first + slots + t]
            for s in range(nodes // tile):

                @pl.when(col == s)
                def _():
                    adj[at, pl.ds(s * tile, tile)] += block

    whole[...] = adj[...].astype(BF)
    dense[...] = whole[...].reshape(dense.shape)
    wide = [x[l].reshape(nodes, width) for x in (feats, other) for l in range(layouts)]
    summed[...] = dot(core_rows(dense, (), core), jnp.concatenate(wide, axis=1))
    hot[...] = one_hot(ints_s, mine.shape[1], nodes)
    for l in range(layouts):
        mine[l] = dot(hot[...], wide[l]).astype(BF)


def sage_out(*refs):
    hub_rows, (summed, pre_self, hub_weight, weight) = refs[:2], refs[2:6]
    blocks, (agg, pre, ready) = refs[6:-3], refs[-3:]
    layouts, nodes, width = pre_self.shape
    chips, groups, _, _ = ready.shape
    me = lax.axis_index("config")
    hub_all = jnp.concatenate([x[...] for x in hub_rows], axis=1)
    total = summed[...] + dot(core_rows(hub_weight, (), lax.rem(me, 2)), hub_all)
    acts = []
    for l in range(layouts):
        mine = total[:, l * width : (l + 1) * width].astype(BF)
        agg[l] = mine
        value = pre_self[l] + dot(mine, weight[1])
        pre[l] = value
        act = value / (1.0 + jnp.exp(-value))
        acts.append(act.reshape(chips, groups, SUB, width))
    ready[...] = jnp.concatenate(acts, axis=2).astype(BF)
    for s, block in enumerate(blocks):
        block[...] = ready[lax.bitwise_xor(me // 2, s)]


def prepare(cot, attn, weight, feats, agg, pre, adj, cot_g, gmix, slope, rows_t, w_back, adj_t):
    layouts, _, width = cot.shape
    groups = cot_g.shape[0]
    adj_t[...] = adj[...].T
    for l in range(feats.shape[0]):
        value = pre[l]
        sig = 1.0 / (1.0 + jnp.exp(-value))
        slope[l] = sig * (1.0 + value * (1.0 - sig))
        at = slice(l * feats.shape[1], (l + 1) * feats.shape[1])
        rows_t[0:width, at] = feats[l].T
        rows_t[width : 2 * width, at] = agg[l].T
    w_back[:, 0:width] = weight[0].T
    w_back[:, width : 2 * width] = weight[1].T
    for p in range(groups // 2):
        block = cot[:, 2 * SUB * p : 2 * SUB * (p + 1), :].astype(F32)
        for h in range(2):
            rows = block[:, SUB * h : SUB * (h + 1), :].reshape(layouts * SUB, width).astype(BF)
            cot_g[2 * p + h] = rows
            gmix[2 * p + h] = dot_nt(rows, attn[3]).astype(BF)


def attend(*refs):
    hidden, ready, grads, pieces = refs[-4:]
    groups, shares, depth, width = hidden.shape
    chips = shares // 2
    blocks, (cot_g, gmix, attn) = refs[:chips], refs[chips : chips + 3]
    outs, (hid_out, mixed_t) = refs[chips + 3 : -6], refs[-6:-4]
    me = lax.axis_index("config")
    rows = shares * depth
    head = width // HEADS
    scale = 1.0 / math.sqrt(head)
    for s, block in enumerate(blocks):
        for core in range(2):
            hidden[:, lax.bitwise_xor(me, 2 * s + core)] = block[:, core * depth : (core + 1) * depth]
    w_all = jnp.concatenate([attn[0], attn[1], attn[2]], axis=1)
    lane = lax.broadcasted_iota(jnp.int32, (rows, width), 1) // head
    r = lax.broadcasted_iota(jnp.int32, (rows, HEADS * rows), 0)
    c = lax.broadcasted_iota(jnp.int32, (rows, HEADS * rows), 1)
    same = (r % SUB) == (c % SUB)
    zero = jnp.zeros((rows, width), BF)
    gap = jnp.zeros((head, rows), BF)

    def by_head(x):
        return jnp.concatenate([jnp.where(lane == e, x, zero) for e in range(HEADS)], axis=0)

    flat = hidden[...].reshape(groups * rows, width)
    hid_out[...] = flat.reshape(groups, rows, width)
    qkv = dot(flat, w_all).astype(BF)
    inputs = []
    for g in range(groups):
        q, k, v = (qkv[g * rows : (g + 1) * rows, i * width : (i + 1) * width] for i in range(3))
        inputs.append((k, v, k.T, v.T, by_head(q), by_head(gmix[g])))
    products = [(dot_nt(k, qm), dot_nt(v, gm)) for k, v, _, _, qm, gm in inputs]
    weighted = []
    for scores, d_probs in products:
        t = jnp.tanh(scores * (scale / CAP))
        w = jnp.where(same, jnp.exp2(t * (CAP * math.log2(math.e))), 0.0)
        a = w * (1.0 / jnp.sum(w, axis=0, keepdims=True))
        z = a * d_probs
        zs = jnp.sum(z, axis=0, keepdims=True)
        weighted.append((a.astype(BF), ((z - a * zs) * (scale - scale * (t * t))).astype(BF)))
    d_all, mix_t = [], []
    for (k, v, k_t, v_t, qm, gm), (p, ds) in zip(inputs, weighted):
        mix, dq = [], []
        for e in range(HEADS):
            at, span = slice(e * head, (e + 1) * head), slice(e * rows, (e + 1) * rows)
            left = jnp.concatenate(
                [jnp.concatenate([v_t[at], gap], axis=1), jnp.concatenate([gap, k_t[at]], axis=1)], axis=0
            )
            both = dot(left, jnp.concatenate([p[:, span], ds[:, span]], axis=0))
            mix.append(both[:head])
            dq.append(both[head:])
        mix_t.append(jnp.concatenate(mix, axis=0).astype(BF))
        dq = jnp.concatenate(dq, axis=0).astype(BF).T
        d_all.append(jnp.concatenate([dq, dot(ds, qm).astype(BF), dot(p, gm).astype(BF)], axis=1))
    d_all = jnp.concatenate(d_all, axis=0)
    mix_t = jnp.concatenate(mix_t, axis=1)
    mixed_t[...] = mix_t
    cots = cot_g[...].reshape(groups * rows, width)
    back = (cots.astype(F32) + dot_nt(d_all, w_all)).astype(BF).reshape(groups, shares, depth, width)
    for g in range(groups):
        ready[:, g] = back[g]
    total = dot(flat.T, d_all)
    for i in range(3):
        grads[i] = total[:, i * width : (i + 1) * width].astype(BF)
    grads[3] = dot(mix_t, cots).astype(BF)
    shared = grads[...].reshape(chips, -1, width)
    pieces[...] = shared
    count = groups * 2 * depth
    for s, block in enumerate(outs):
        pair = [ready[lax.bitwise_xor(me, 2 * s + core)] for core in range(2)]
        block[0:count] = jnp.concatenate(pair, axis=1).reshape(count, width)
        block[count:] = pieces[lax.bitwise_xor(me // 2, s)]


def outputs(hidden, mixed_t, attn, _, out, done):
    done[...] = jnp.zeros(done.shape, F32)
    groups, rows, width = hidden.shape
    layouts = rows // SUB
    projected = dot_tn(mixed_t[...], attn[3])
    for p in range(groups // 2):
        pair = []
        for g in (2 * p, 2 * p + 1):
            both = hidden[g].astype(F32) + projected[g * rows : (g + 1) * rows]
            pair.append(both.reshape(layouts, SUB, width))
        out[:, 2 * SUB * p : 2 * SUB * (p + 1), :] = jnp.concatenate(pair, axis=1).astype(BF)


def sage_back(*refs):
    parts, hub_sum = refs[-2:]
    chips, _, layouts, _, width = parts.shape
    blocks, (slope, rows_t, w_back, hub_weight) = refs[:chips], refs[chips : chips + 4]
    mine, theirs, sums, hub_mine, hub_theirs = refs[chips + 5 : -2]
    me = lax.axis_index("config")
    nodes = slope.shape[1]
    count = parts.shape[1] * layouts * SUB
    for s, block in enumerate(blocks):
        parts[lax.bitwise_xor(me // 2, s)] = block[0:count].astype(F32).reshape(parts.shape[1:])
    sums[2 * width :] = sum(block[count:].astype(F32) for block in blocks).astype(BF)
    half = layouts // 2
    grad_pre, grad_agg = [], []
    for l in range(layouts):
        gpre = (parts[:, :, l].reshape(nodes, width) * slope[l]).astype(BF)
        (mine, theirs)[l // half][l % half] = gpre
        grad_pre.append(gpre)
        grad_agg.append(dot(gpre, w_back[:, width : 2 * width]).astype(BF))
    both = dot(rows_t[...], jnp.concatenate(grad_pre, axis=0))
    sums[0 : 2 * width] = both.astype(BF)
    hub_sum[...] = dot_tn(core_rows(hub_weight, (), lax.rem(me, 2)), jnp.concatenate(grad_agg, axis=1))
    slab = lax.axis_index("graph")
    ranks, _, hubs, _ = hub_mine.shape
    for s in range(ranks):
        at = pl.ds(pl.multiple_of(lax.bitwise_xor(slab, s) * hubs, hubs), hubs)
        for l in range(layouts):
            (hub_mine, hub_theirs)[l // half][s, l % half] = hub_sum[at, l * width : (l + 1) * width].astype(BF)


def tile_back(adj_t, w_back, mine, theirs, totals, whole):
    layouts, nodes, width = totals.shape
    core = lax.rem(lax.axis_index("config"), 2)
    for l in range(layouts):
        for part, at in ((mine, core), (theirs, 1 - core)):
            whole[l, :, pl.ds(at, 1)] = part[l].reshape(whole.shape[1], 1, whole.shape[3], width)
    grad_self, grad_agg = [], []
    for l in range(layouts):
        both = dot(whole[l].reshape(nodes, width), w_back[...]).astype(BF)
        grad_self.append(both[:, 0:width])
        grad_agg.append(both[:, width : 2 * width])
    back = dot(adj_t[...], jnp.concatenate(grad_agg, axis=1))
    for l in range(layouts):
        totals[l] = grad_self[l].astype(F32) + back[:, l * width : (l + 1) * width]


def add(a, b):
    return (a[...].astype(F32) + b[...].astype(F32)).astype(BF)


def join(*refs):
    pairs = len(refs) // 3
    for i in range(pairs):
        refs[2 * pairs + i][...] = add(refs[2 * i], refs[2 * i + 1])


def joined(*operands):
    return call(
        join,
        [shape(x.shape) for x in operands[::2]],
        operands,
        [VMEM] * len(operands),
        micros=0.1,
        name="join",
    )


def by_slab(*refs):
    pieces, (rows, work) = refs[:-2], refs[-2:]
    layouts, hubs, width = pieces[0].shape
    slab = lax.axis_index("graph")
    for s, piece in enumerate(pieces):
        at = pl.ds(pl.multiple_of(lax.bitwise_xor(slab, s) * hubs, hubs), hubs)
        for l in range(layouts):
            work[at, l * width : (l + 1) * width] = piece[l].astype(F32)
    rows[...] = work[...].astype(BF)


def finish(hot, totals, hub_own, hub_in, out, work, sems):
    layouts, nodes, width = totals.shape
    summed = [hub_own[0, l].astype(F32) + hub_in[0, l].astype(F32) for l in range(layouts)]
    upper = [x.astype(BF) for x in summed]
    lower = [(x - y.astype(F32)).astype(BF) for x, y in zip(summed, upper)]
    twice = jnp.concatenate([hot[...], hot[...]], axis=0)
    copies = []
    for l in range(layouts):
        added = dot_tn(twice, jnp.concatenate([upper[l], lower[l]], axis=0))
        work[l] = (totals[l] + added).astype(BF)
        copies.append(pltpu.make_async_copy(work.at[l], out.at[l], sems.at[l]))
        copies[l].start()
    for copy in copies:
        copy.wait()


def weights_out(scale, *refs):
    sums, (out, work) = refs[:-2], refs[-2:]
    width = out.shape[1]
    first = 2 * width
    share = sums[0].shape[0] - first
    chip = lax.axis_index("config") // 2
    for s, part in enumerate(sums):
        at = lax.bitwise_xor(chip, s)
        work[at] = part[0:first].astype(F32)
        out[pl.ds(pl.multiple_of(first + at * share, share), share)] = part[first:].astype(F32) * scale
    total = work[0]
    for s in range(1, len(sums)):
        total = total + work[s]
    out[0:first] = total * scale


def exchange(blocks):
    return [swapped(block, "config", 2 * s) if s else block for s, block in enumerate(blocks)]


def local(
    features,
    cotangent,
    sage_weight,
    attn_weight,
    tile_vals,
    tile_dst,
    tile_src,
    tile_count,
    hub_ids,
    hub_weight,
):
    layout_dev, node_dev, width = features.shape
    ranks = lax.axis_size("graph")
    shares = lax.axis_size("config")
    chips = shares // 2
    share = node_dev // shares
    groups = share // SUB
    layouts = layout_dev * shares
    rows = layouts * SUB
    depth = 2 * layout_dev * SUB
    hub_dev = hub_ids.shape[0]
    hubs = hub_weight.shape[1]
    slab = (layout_dev, node_dev, width)
    part = (2 * layout_dev, node_dev // 2, width)
    block = (groups, depth, width)
    dma = pltpu.SemaphoreType.DMA
    ints = jnp.concatenate([hub_ids, tile_dst, tile_src, tile_count])
    ints_s = pltpu.SMEM(ints.shape, jnp.int32)
    hub_weight = hub_weight.reshape(chips, 2, share, hubs)
    by_core = (layout_dev, chips, 2, share, width)

    mine = call(
        hub_pick,
        shape((layout_dev, hub_dev, width)),
        (hub_ids, features),
        [HBM] * 2,
        [pltpu.SMEM((hub_dev,), jnp.int32), pltpu.VMEM(slab, BF), dma((1 + layout_dev,))],
        limit=WHOLE,
        name="hub_pick",
    )
    pieces = [swapped(mine, "graph", s) for s in range(1, ranks)]
    other = swapped(features, "config", 1)

    adj, summed, pre_self, feats, mine, hot = call(
        functools.partial(adjacency, hub_dev),
        (
            shape((node_dev, node_dev)),
            shape((part[1], part[0] * width), F32),
            shape(part, F32),
            shape(part),
            shape(mine.shape),
            shape((hub_dev, node_dev)),
        ),
        (ints, tile_vals, sage_weight, features.reshape(by_core), other.reshape(by_core)),
        [VMEM] * 5,
        [
            ints_s,
            pltpu.VMEM((node_dev, node_dev), F32),
            pltpu.VMEM((chips, 2, share, node_dev), BF),
            dma((1,)),
        ],
        name="adjacency",
    )

    hub_rows = call(
        by_slab,
        shape((hubs, layout_dev * width)),
        (mine, *pieces),
        [VMEM] * ranks,
        [pltpu.VMEM((hubs, layout_dev * width), F32)],
        micros=0.1,
        name="by_slab",
    )
    hub_rows = (hub_rows, swapped(hub_rows, "config", 1))

    *blocks, agg, pre = call(
        sage_out,
        (*[shape(block)] * chips, shape(part), shape(part, F32)),
        (*hub_rows, summed, pre_self, hub_weight, sage_weight),
        [VMEM] * 6,
        [pltpu.VMEM((chips, *block), BF)],
        name="sage_out",
    )
    hidden_in = exchange(blocks)

    cot_g, gmix, slope, rows_t, w_back, adj_t = call(
        prepare,
        (
            shape((groups, rows, width)),
            shape((groups, rows, width)),
            shape(part, F32),
            shape((2 * width, part[0] * part[1])),
            shape((width, 2 * width)),
            shape((node_dev, node_dev)),
        ),
        (cotangent, attn_weight, sage_weight, feats, agg, pre, adj),
        [VMEM] * 7,
        name="prepare",
    )

    share_rows = attn_weight.shape[0] * width // chips
    back = (groups * depth + share_rows, width)
    *blocks, hidden, mixed_t = call(
        attend,
        (
            *[shape(back)] * chips,
            shape((groups, rows, width)),
            shape((width, groups * rows)),
        ),
        (*hidden_in, cot_g, gmix, attn_weight),
        [VMEM] * (len(hidden_in) + 3),
        [
            pltpu.VMEM((groups, shares, depth // 2, width), BF),
            pltpu.VMEM((shares, groups, depth // 2, width), BF),
            pltpu.VMEM(attn_weight.shape, BF),
            pltpu.VMEM((chips, share_rows, width), BF),
        ],
        micros=4.0,
        name="attend",
    )
    grad_in = exchange(blocks)
    token = shape((SUB, width), F32)
    output, shown = call(
        outputs,
        (shape((layouts, share, width)), token),
        (hidden, mixed_t, attn_weight, grad_in[1]),
        [VMEM] * 3 + [ANY],
        name="outputs",
    )

    hub_shape = (ranks, layout_dev, hub_dev, width)
    mine = (layout_dev, node_dev // 2, width)
    mine, theirs, sums, hub_sum, hub_theirs = call(
        sage_back,
        (shape(mine), shape(mine), shape((2 * width + share_rows, width)), shape(hub_shape), shape(hub_shape)),
        (*grad_in, slope, rows_t, w_back, hub_weight, shown),
        [VMEM] * (chips + 4) + [ANY],
        [
            pltpu.VMEM((chips, groups, 2 * layout_dev, SUB, width), F32),
            pltpu.VMEM((hubs, part[0] * width), F32),
        ],
        name="sage_back",
    )
    hub_in = swapped(hub_theirs, "config", 1)
    theirs = swapped(theirs, "config", 1)
    sums, hub_sum = joined(sums, swapped(sums, "config", 1), hub_sum, hub_in)
    sums = [swapped(sums, "config", 2 * s) if s else sums for s in range(chips)]
    totals = call(
        tile_back,
        shape(slab, F32),
        (adj_t, w_back, mine, theirs),
        [VMEM] * 4,
        [pltpu.VMEM(by_core, BF)],
        name="tile_back",
    )
    while hub_sum.shape[0] > 2:
        keep = hub_sum.shape[0] // 2
        hub_sum = hub_sum[:keep] + swapped(hub_sum[keep:], "graph", keep)
    hub_in = swapped(hub_sum[1:], "graph", 1)
    count = sage_weight.shape[0] + attn_weight.shape[0]
    weights = call(
        functools.partial(weights_out, 1.0 / math.sqrt(layouts * node_dev)),
        shape((count * width, width), F32),
        sums,
        [VMEM] * chips,
        [pltpu.VMEM((chips, 2 * width, width), F32)],
        name="weights_out",
    )
    grad_features = call(
        finish,
        shape(slab),
        (hot, totals, hub_sum, hub_in),
        [VMEM] * 4,
        [pltpu.VMEM(slab, BF), dma((layout_dev,))],
        outs_at=HBM,
        name="finish",
    )
    return (output, grad_features, weights.reshape(1, count, width, width))


def solution(mesh):
    return jax.shard_map(
        local,
        mesh=mesh,
        in_specs=(
            P("config", "graph", None),
            P(None, ("graph", "config"), None),
            P(),
            P(),
            P("graph", None, None),
            P("graph"),
            P("graph"),
            P("graph"),
            P("graph"),
            P("graph", None),
        ),
        out_specs=(
            P(None, ("graph", "config"), None),
            P("config", "graph", None),
            P("graph", None, None, None),
        ),
        check_vma=False,
    )
```

```python
import functools
import math

import jax
import jax.numpy as jnp
from jax import lax
from jax.experimental import pallas as pl
from jax.experimental.pallas import tpu as pltpu
from jax.sharding import PartitionSpec as P

HEADS = 4
CAP = 20.0
SUB = 8

BF = jnp.bfloat16
F32 = jnp.float32
VMEM = pl.BlockSpec(memory_space=pltpu.VMEM)
ANY = pl.BlockSpec(memory_space=pl.ANY)
HBM = pl.BlockSpec(memory_space=pltpu.HBM)
LIMIT = 24 * 1024 * 1024
WHOLE = 56 * 1024 * 1024


def dot(a, b):
    return jnp.dot(a, b, preferred_element_type=F32)


def dot_nt(a, b):
    return lax.dot_general(a, b, (((1,), (1,)), ((), ())), preferred_element_type=F32)


def dot_tn(a, b):
    return lax.dot_general(a, b, (((0,), (0,)), ((), ())), preferred_element_type=F32)


def shape(dims, kind=BF):
    return jax.ShapeDtypeStruct(dims, kind)


def call(kernel, outs, operands, specs, scratch=(), micros=1.0, limit=LIMIT, outs_at=VMEM, name=None):
    return pl.pallas_call(
        kernel,
        out_shape=outs,
        in_specs=specs,
        out_specs=jax.tree.map(lambda _: outs_at, outs),
        scratch_shapes=list(scratch),
        compiler_params=pltpu.CompilerParams(vmem_limit_bytes=limit),
        cost_estimate=pl.CostEstimate(
            flops=int(micros * 10**9), bytes_accessed=int(micros * 2**21), transcendentals=0
        ),
        name=name,
    )(*operands)


def fetch(pairs, sems):
    copies = [pltpu.make_async_copy(a, b, sems.at[i]) for i, (a, b) in enumerate(pairs)]
    for copy in copies:
        copy.start()
    return copies


def swapped(x, axis, mask):
    count = lax.axis_size(axis)
    return lax.ppermute(x, axis, [(i, i ^ mask) for i in range(count)])


def steps(count, first):
    return [0] + [s for s in first if s < count] + [s for s in range(1, count) if s not in first]


SLABS = (2, 3, 1)
CHIPS = (1, 2, 3)


def one_hot(ids, hubs, nodes):
    row = lax.broadcasted_iota(jnp.int32, (hubs, nodes), 0)
    col = lax.broadcasted_iota(jnp.int32, (hubs, nodes), 1)
    want = jnp.zeros((hubs, nodes), jnp.int32)
    for j in range(hubs):
        want = jnp.where(row == j, lax.rem(ids[j], nodes), want)
    return jnp.where(col == want, 1.0, 0.0).astype(BF)


def hub_pick(ids, feats, *refs):
    outs, (ids_s, feats_v, sems) = refs[:-3], refs[-3:]
    layouts, nodes, _ = feats.shape
    copies = fetch([(ids, ids_s)] + [(feats.at[l], feats_v.at[l]) for l in range(layouts)], sems)
    copies[0].wait()
    hot = one_hot(ids_s, outs[0].shape[1], nodes)
    for l in range(layouts):
        copies[1 + l].wait()
        picked = dot(hot, feats_v[l]).astype(BF)
        for out in outs:
            out[l] = picked


def core_rows(ref, lead, core):
    block = ref[lead + (slice(None), pl.ds(core, 1))]
    return block.reshape(block.shape[0] * block.shape[2], block.shape[3])


def adjacency(first, ints, tiles, weight, feats, other, whole, summed, pre_self, chosen, mine, hot, ints_s, adj, dense, sems):
    copies = fetch([(ints, ints_s)], sems)
    slots, tile, _ = tiles.shape
    layouts, chips, cores, share, width = feats.shape
    nodes = chips * cores * share
    core = lax.rem(lax.axis_index("config"), 2)
    adj[...] = jnp.zeros(adj.shape, F32)
    for l in range(2 * layouts):
        chosen[l] = core_rows((feats, other)[l // layouts], (l % layouts,), core)
        pre_self[l] = dot(chosen[l], weight[0])
    copies[0].wait()
    for t in range(slots):

        @pl.when(t < ints_s[first + 2 * slots])
        def _():
            at = pl.ds(pl.multiple_of(ints_s[first + t] * tile, tile), tile)
            block = tiles[t].astype(F32)
            col = ints_s[first + slots + t]
            for s in range(nodes // tile):

                @pl.when(col == s)
                def _():
                    adj[at, pl.ds(s * tile, tile)] += block

    whole[...] = adj[...].astype(BF)
    dense[...] = whole[...].reshape(dense.shape)
    wide = [x[l].reshape(nodes, width) for x in (feats, other) for l in range(layouts)]
    summed[...] = dot(core_rows(dense, (), core), jnp.concatenate(wide, axis=1))
    hot[...] = one_hot(ints_s, mine.shape[1], nodes)
    for l in range(layouts):
        mine[l] = dot(hot[...], wide[l]).astype(BF)


def sage_out(*refs):
    hub_rows, (summed, pre_self, hub_weight, weight) = refs[:2], refs[2:6]
    blocks, (agg, pre, ready) = refs[6:-3], refs[-3:]
    layouts, nodes, width = pre_self.shape
    chips, groups, _, _ = ready.shape
    me = lax.axis_index("config")
    hub_all = jnp.concatenate([x[...] for x in hub_rows], axis=1)
    total = summed[...] + dot(core_rows(hub_weight, (), lax.rem(me, 2)), hub_all)
    acts = []
    for l in range(layouts):
        mine = total[:, l * width : (l + 1) * width].astype(BF)
        agg[l] = mine
        value = pre_self[l] + dot(mine, weight[1])
        pre[l] = value
        act = value / (1.0 + jnp.exp(-value))
        acts.append(act.reshape(chips, groups, SUB, width))
    ready[...] = jnp.concatenate(acts, axis=2).astype(BF)
    for s, block in zip(steps(chips, CHIPS), blocks):
        block[...] = ready[lax.bitwise_xor(me // 2, s)]


def prepare(cot, attn, weight, feats, agg, pre, adj, cot_g, gmix, slope, rows_t, w_back, adj_t):
    layouts, _, width = cot.shape
    groups = cot_g.shape[0]
    adj_t[...] = adj[...].T
    for l in range(feats.shape[0]):
        value = pre[l]
        sig = 1.0 / (1.0 + jnp.exp(-value))
        slope[l] = sig * (1.0 + value * (1.0 - sig))
        at = slice(l * feats.shape[1], (l + 1) * feats.shape[1])
        rows_t[0:width, at] = feats[l].T
        rows_t[width : 2 * width, at] = agg[l].T
    w_back[:, 0:width] = weight[0].T
    w_back[:, width : 2 * width] = weight[1].T
    for p in range(groups // 2):
        block = cot[:, 2 * SUB * p : 2 * SUB * (p + 1), :].astype(F32)
        for h in range(2):
            rows = block[:, SUB * h : SUB * (h + 1), :].reshape(layouts * SUB, width).astype(BF)
            cot_g[2 * p + h] = rows
            gmix[2 * p + h] = dot_nt(rows, attn[3]).astype(BF)


def attend(*refs):
    hidden, ready, grads, pieces = refs[-4:]
    groups, shares, depth, width = hidden.shape
    chips = shares // 2
    blocks, (cot_g, gmix, attn) = refs[:chips], refs[chips : chips + 3]
    outs, (hid_out, mixed_t) = refs[chips + 3 : -6], refs[-6:-4]
    me = lax.axis_index("config")
    rows = shares * depth
    head = width // HEADS
    scale = 1.0 / math.sqrt(head)
    for s, block in zip(steps(chips, CHIPS), blocks):
        for core in range(2):
            hidden[:, lax.bitwise_xor(me, 2 * s + core)] = block[:, core * depth : (core + 1) * depth]
    w_all = jnp.concatenate([attn[0], attn[1], attn[2]], axis=1)
    lane = lax.broadcasted_iota(jnp.int32, (rows, width), 1) // head
    r = lax.broadcasted_iota(jnp.int32, (rows, HEADS * rows), 0)
    c = lax.broadcasted_iota(jnp.int32, (rows, HEADS * rows), 1)
    same = (r % SUB) == (c % SUB)
    zero = jnp.zeros((rows, width), BF)
    gap = jnp.zeros((head, rows), BF)

    def by_head(x):
        return jnp.concatenate([jnp.where(lane == e, x, zero) for e in range(HEADS)], axis=0)

    flat = hidden[...].reshape(groups * rows, width)
    hid_out[...] = flat.reshape(groups, rows, width)
    qkv = dot(flat, w_all).astype(BF)
    inputs = []
    for g in range(groups):
        q, k, v = (qkv[g * rows : (g + 1) * rows, i * width : (i + 1) * width] for i in range(3))
        inputs.append((k, v, k.T, v.T, by_head(q), by_head(gmix[g])))
    products = [(dot_nt(k, qm), dot_nt(v, gm)) for k, v, _, _, qm, gm in inputs]
    weighted = []
    for scores, d_probs in products:
        t = jnp.tanh(scores * (scale / CAP))
        w = jnp.where(same, jnp.exp2(t * (CAP * math.log2(math.e))), 0.0)
        a = w * (1.0 / jnp.sum(w, axis=0, keepdims=True))
        z = a * d_probs
        zs = jnp.sum(z, axis=0, keepdims=True)
        weighted.append((a.astype(BF), ((z - a * zs) * (scale - scale * (t * t))).astype(BF)))
    d_all, mix_t = [], []
    for (k, v, k_t, v_t, qm, gm), (p, ds) in zip(inputs, weighted):
        mix, dq = [], []
        for e in range(HEADS):
            at, span = slice(e * head, (e + 1) * head), slice(e * rows, (e + 1) * rows)
            left = jnp.concatenate(
                [jnp.concatenate([v_t[at], gap], axis=1), jnp.concatenate([gap, k_t[at]], axis=1)], axis=0
            )
            both = dot(left, jnp.concatenate([p[:, span], ds[:, span]], axis=0))
            mix.append(both[:head])
            dq.append(both[head:])
        mix_t.append(jnp.concatenate(mix, axis=0).astype(BF))
        dq = jnp.concatenate(dq, axis=0).astype(BF).T
        d_all.append(jnp.concatenate([dq, dot(ds, qm).astype(BF), dot(p, gm).astype(BF)], axis=1))
    d_all = jnp.concatenate(d_all, axis=0)
    mix_t = jnp.concatenate(mix_t, axis=1)
    mixed_t[...] = mix_t
    cots = cot_g[...].reshape(groups * rows, width)
    back = (cots.astype(F32) + dot_nt(d_all, w_all)).astype(BF).reshape(groups, shares, depth, width)
    for g in range(groups):
        ready[:, g] = back[g]
    total = dot(flat.T, d_all)
    for i in range(3):
        grads[i] = total[:, i * width : (i + 1) * width].astype(BF)
    grads[3] = dot(mix_t, cots).astype(BF)
    shared = grads[...].reshape(chips, -1, width)
    pieces[...] = shared
    count = groups * 2 * depth
    for s, block in zip(steps(chips, CHIPS), outs):
        pair = [ready[lax.bitwise_xor(me, 2 * s + core)] for core in range(2)]
        block[0:count] = jnp.concatenate(pair, axis=1).reshape(count, width)
        block[count:] = pieces[lax.bitwise_xor(me // 2, s)]


def outputs(hidden, mixed_t, attn, _, out, done):
    done[...] = jnp.zeros(done.shape, F32)
    groups, rows, width = hidden.shape
    layouts = rows // SUB
    projected = dot_tn(mixed_t[...], attn[3])
    for p in range(groups // 2):
        pair = []
        for g in (2 * p, 2 * p + 1):
            both = hidden[g].astype(F32) + projected[g * rows : (g + 1) * rows]
            pair.append(both.reshape(layouts, SUB, width))
        out[:, 2 * SUB * p : 2 * SUB * (p + 1), :] = jnp.concatenate(pair, axis=1).astype(BF)


def sage_back(*refs):
    parts, hub_sum = refs[-2:]
    chips, _, layouts, _, width = parts.shape
    blocks, (slope, rows_t, w_back, hub_weight) = refs[:chips], refs[chips : chips + 4]
    mine, theirs, sums, hub_mine, hub_theirs = refs[chips + 5 : -2]
    me = lax.axis_index("config")
    nodes = slope.shape[1]
    count = parts.shape[1] * layouts * SUB
    for s, block in zip(steps(chips, CHIPS), blocks):
        parts[lax.bitwise_xor(me // 2, s)] = block[0:count].astype(F32).reshape(parts.shape[1:])
    sums[2 * width :] = sum(block[count:].astype(F32) for block in blocks).astype(BF)
    half = layouts // 2
    grad_pre, grad_agg = [], []
    for l in range(layouts):
        gpre = (parts[:, :, l].reshape(nodes, width) * slope[l]).astype(BF)
        (mine, theirs)[l // half][l % half] = gpre
        grad_pre.append(gpre)
        grad_agg.append(dot(gpre, w_back[:, width : 2 * width]).astype(BF))
    both = dot(rows_t[...], jnp.concatenate(grad_pre, axis=0))
    sums[0 : 2 * width] = both.astype(BF)
    hub_sum[...] = dot_tn(core_rows(hub_weight, (), lax.rem(me, 2)), jnp.concatenate(grad_agg, axis=1))
    slab = lax.axis_index("graph")
    ranks, _, hubs, _ = hub_mine.shape
    for s in range(ranks):
        at = pl.ds(pl.multiple_of(lax.bitwise_xor(slab, s) * hubs, hubs), hubs)
        for l in range(layouts):
            (hub_mine, hub_theirs)[l // half][s, l % half] = hub_sum[at, l * width : (l + 1) * width].astype(BF)


def tile_back(adj_t, w_back, mine, theirs, totals, whole):
    layouts, nodes, width = totals.shape
    core = lax.rem(lax.axis_index("config"), 2)
    for l in range(layouts):
        for part, at in ((mine, core), (theirs, 1 - core)):
            whole[l, :, pl.ds(at, 1)] = part[l].reshape(whole.shape[1], 1, whole.shape[3], width)
    grad_self, grad_agg = [], []
    for l in range(layouts):
        both = dot(whole[l].reshape(nodes, width), w_back[...]).astype(BF)
        grad_self.append(both[:, 0:width])
        grad_agg.append(both[:, width : 2 * width])
    back = dot(adj_t[...], jnp.concatenate(grad_agg, axis=1))
    for l in range(layouts):
        totals[l] = grad_self[l].astype(F32) + back[:, l * width : (l + 1) * width]


def add(a, b):
    return (a[...].astype(F32) + b[...].astype(F32)).astype(BF)


def join(*refs):
    pairs = len(refs) // 3
    for i in range(pairs):
        refs[2 * pairs + i][...] = add(refs[2 * i], refs[2 * i + 1])


def joined(*operands):
    return call(
        join,
        [shape(x.shape) for x in operands[::2]],
        operands,
        [VMEM] * len(operands),
        micros=0.1,
        name="join",
    )


def by_slab(*refs):
    pieces, (rows, work) = refs[:-2], refs[-2:]
    layouts, hubs, width = pieces[0].shape
    slab = lax.axis_index("graph")
    for s, piece in zip(steps(len(pieces), SLABS), pieces):
        at = pl.ds(pl.multiple_of(lax.bitwise_xor(slab, s) * hubs, hubs), hubs)
        for l in range(layouts):
            work[at, l * width : (l + 1) * width] = piece[l].astype(F32)
    rows[...] = work[...].astype(BF)


def finish(hot, totals, hub_own, hub_in, out, work, sems):
    layouts, nodes, width = totals.shape
    summed = [hub_own[0, l].astype(F32) + hub_in[0, l].astype(F32) for l in range(layouts)]
    upper = [x.astype(BF) for x in summed]
    lower = [(x - y.astype(F32)).astype(BF) for x, y in zip(summed, upper)]
    twice = jnp.concatenate([hot[...], hot[...]], axis=0)
    copies = []
    for l in range(layouts):
        added = dot_tn(twice, jnp.concatenate([upper[l], lower[l]], axis=0))
        work[l] = (totals[l] + added).astype(BF)
        copies.append(pltpu.make_async_copy(work.at[l], out.at[l], sems.at[l]))
        copies[l].start()
    for copy in copies:
        copy.wait()


def weights_out(scale, *refs):
    sums, (out, work) = refs[:-2], refs[-2:]
    width = out.shape[1]
    first = 2 * width
    share = sums[0].shape[0] - first
    chip = lax.axis_index("config") // 2
    for s, part in zip(steps(len(sums), CHIPS), sums):
        at = lax.bitwise_xor(chip, s)
        work[at] = part[0:first].astype(F32)
        out[pl.ds(pl.multiple_of(first + at * share, share), share)] = part[first:].astype(F32) * scale
    total = work[0]
    for s in range(1, len(sums)):
        total = total + work[s]
    out[0:first] = total * scale


def exchange(blocks):
    masks = steps(len(blocks), CHIPS)
    return [swapped(block, "config", 2 * s) if s else block for s, block in zip(masks, blocks)]


def local(
    features,
    cotangent,
    sage_weight,
    attn_weight,
    tile_vals,
    tile_dst,
    tile_src,
    tile_count,
    hub_ids,
    hub_weight,
):
    layout_dev, node_dev, width = features.shape
    ranks = lax.axis_size("graph")
    shares = lax.axis_size("config")
    chips = shares // 2
    share = node_dev // shares
    groups = share // SUB
    layouts = layout_dev * shares
    rows = layouts * SUB
    depth = 2 * layout_dev * SUB
    hub_dev = hub_ids.shape[0]
    hubs = hub_weight.shape[1]
    slab = (layout_dev, node_dev, width)
    part = (2 * layout_dev, node_dev // 2, width)
    block = (groups, depth, width)
    dma = pltpu.SemaphoreType.DMA
    ints = jnp.concatenate([hub_ids, tile_dst, tile_src, tile_count])
    ints_s = pltpu.SMEM(ints.shape, jnp.int32)
    hub_weight = hub_weight.reshape(chips, 2, share, hubs)
    by_core = (layout_dev, chips, 2, share, width)

    picked_shape = (layout_dev, hub_dev, width)
    picked = call(
        hub_pick,
        [shape(picked_shape)] * (ranks - 1),
        (hub_ids, features),
        [HBM] * 2,
        [pltpu.SMEM((hub_dev,), jnp.int32), pltpu.VMEM(slab, BF), dma((1 + layout_dev,))],
        limit=WHOLE,
        name="hub_pick",
    )
    pieces = [swapped(x, "graph", s) for s, x in zip(steps(ranks, SLABS)[1:], picked)]
    other = swapped(features, "config", 1)

    adj, summed, pre_self, feats, mine, hot = call(
        functools.partial(adjacency, hub_dev),
        (
            shape((node_dev, node_dev)),
            shape((part[1], part[0] * width), F32),
            shape(part, F32),
            shape(part),
            shape(picked_shape),
            shape((hub_dev, node_dev)),
        ),
        (ints, tile_vals, sage_weight, features.reshape(by_core), other.reshape(by_core)),
        [VMEM] * 5,
        [
            ints_s,
            pltpu.VMEM((node_dev, node_dev), F32),
            pltpu.VMEM((chips, 2, share, node_dev), BF),
            dma((1,)),
        ],
        name="adjacency",
    )

    hub_rows = call(
        by_slab,
        shape((hubs, layout_dev * width)),
        (mine, *pieces),
        [VMEM] * ranks,
        [pltpu.VMEM((hubs, layout_dev * width), F32)],
        micros=0.1,
        name="by_slab",
    )
    hub_rows = (hub_rows, swapped(hub_rows, "config", 1))

    *blocks, agg, pre = call(
        sage_out,
        (*[shape(block)] * chips, shape(part), shape(part, F32)),
        (*hub_rows, summed, pre_self, hub_weight, sage_weight),
        [VMEM] * 6,
        [pltpu.VMEM((chips, *block), BF)],
        name="sage_out",
    )
    hidden_in = exchange(blocks)

    cot_g, gmix, slope, rows_t, w_back, adj_t = call(
        prepare,
        (
            shape((groups, rows, width)),
            shape((groups, rows, width)),
            shape(part, F32),
            shape((2 * width, part[0] * part[1])),
            shape((width, 2 * width)),
            shape((node_dev, node_dev)),
        ),
        (cotangent, attn_weight, sage_weight, feats, agg, pre, adj),
        [VMEM] * 7,
        name="prepare",
    )

    share_rows = attn_weight.shape[0] * width // chips
    back = (groups * depth + share_rows, width)
    *blocks, hidden, mixed_t = call(
        attend,
        (
            *[shape(back)] * chips,
            shape((groups, rows, width)),
            shape((width, groups * rows)),
        ),
        (*hidden_in, cot_g, gmix, attn_weight),
        [VMEM] * (len(hidden_in) + 3),
        [
            pltpu.VMEM((groups, shares, depth // 2, width), BF),
            pltpu.VMEM((shares, groups, depth // 2, width), BF),
            pltpu.VMEM(attn_weight.shape, BF),
            pltpu.VMEM((chips, share_rows, width), BF),
        ],
        micros=4.0,
        name="attend",
    )
    grad_in = exchange(blocks)
    token = shape((SUB, width), F32)
    output, shown = call(
        outputs,
        (shape((layouts, share, width)), token),
        (hidden, mixed_t, attn_weight, grad_in[1]),
        [VMEM] * 3 + [ANY],
        name="outputs",
    )

    hub_shape = (ranks, layout_dev, hub_dev, width)
    mine = (layout_dev, node_dev // 2, width)
    mine, theirs, sums, hub_sum, hub_theirs = call(
        sage_back,
        (shape(mine), shape(mine), shape((2 * width + share_rows, width)), shape(hub_shape), shape(hub_shape)),
        (*grad_in, slope, rows_t, w_back, hub_weight, shown),
        [VMEM] * (chips + 4) + [ANY],
        [
            pltpu.VMEM((chips, groups, 2 * layout_dev, SUB, width), F32),
            pltpu.VMEM((hubs, part[0] * width), F32),
        ],
        name="sage_back",
    )
    hub_in = swapped(hub_theirs, "config", 1)
    theirs = swapped(theirs, "config", 1)
    sums, hub_sum = joined(sums, swapped(sums, "config", 1), hub_sum, hub_in)
    sums = exchange([sums] * chips)
    totals = call(
        tile_back,
        shape(slab, F32),
        (adj_t, w_back, mine, theirs),
        [VMEM] * 4,
        [pltpu.VMEM(by_core, BF)],
        name="tile_back",
    )
    while hub_sum.shape[0] > 2:
        keep = hub_sum.shape[0] // 2
        hub_sum = hub_sum[:keep] + swapped(hub_sum[keep:], "graph", keep)
    hub_in = swapped(hub_sum[1:], "graph", 1)
    count = sage_weight.shape[0] + attn_weight.shape[0]
    weights = call(
        functools.partial(weights_out, 1.0 / math.sqrt(layouts * node_dev)),
        shape((count * width, width), F32),
        sums,
        [VMEM] * chips,
        [pltpu.VMEM((chips, 2 * width, width), F32)],
        name="weights_out",
    )
    grad_features = call(
        finish,
        shape(slab),
        (hot, totals, hub_sum, hub_in),
        [VMEM] * 4,
        [pltpu.VMEM(slab, BF), dma((layout_dev,))],
        outs_at=HBM,
        name="finish",
    )
    return (output, grad_features, weights.reshape(1, count, width, width))


def solution(mesh):
    return jax.shard_map(
        local,
        mesh=mesh,
        in_specs=(
            P("config", "graph", None),
            P(None, ("graph", "config"), None),
            P(),
            P(),
            P("graph", None, None),
            P("graph"),
            P("graph"),
            P("graph"),
            P("graph"),
            P("graph", None),
        ),
        out_specs=(
            P(None, ("graph", "config"), None),
            P("config", "graph", None),
            P("graph", None, None, None),
        ),
        check_vma=False,
    )
```

```python
import functools
import math

import jax
import jax.numpy as jnp
from jax import lax
from jax.experimental import pallas as pl
from jax.experimental.pallas import tpu as pltpu
from jax.sharding import PartitionSpec as P

HEADS = 4
CAP = 20.0
SUB = 8

BF = jnp.bfloat16
F32 = jnp.float32
VMEM = pl.BlockSpec(memory_space=pltpu.VMEM)
ANY = pl.BlockSpec(memory_space=pl.ANY)
HBM = pl.BlockSpec(memory_space=pltpu.HBM)
LIMIT = 24 * 1024 * 1024
WHOLE = 56 * 1024 * 1024


def dot(a, b):
    return jnp.dot(a, b, preferred_element_type=F32)


def dot_nt(a, b):
    return lax.dot_general(a, b, (((1,), (1,)), ((), ())), preferred_element_type=F32)


def dot_tn(a, b):
    return lax.dot_general(a, b, (((0,), (0,)), ((), ())), preferred_element_type=F32)


def shape(dims, kind=BF):
    return jax.ShapeDtypeStruct(dims, kind)


def call(kernel, outs, operands, specs, scratch=(), micros=1.0, limit=LIMIT, outs_at=VMEM, name=None):
    return pl.pallas_call(
        kernel,
        out_shape=outs,
        in_specs=specs,
        out_specs=jax.tree.map(lambda _: outs_at, outs),
        scratch_shapes=list(scratch),
        compiler_params=pltpu.CompilerParams(vmem_limit_bytes=limit),
        cost_estimate=pl.CostEstimate(
            flops=int(micros * 10**9), bytes_accessed=int(micros * 2**21), transcendentals=0
        ),
        name=name,
    )(*operands)


def fetch(pairs, sems):
    copies = [pltpu.make_async_copy(a, b, sems.at[i]) for i, (a, b) in enumerate(pairs)]
    for copy in copies:
        copy.start()
    return copies


def swapped(x, axis, mask):
    count = lax.axis_size(axis)
    return lax.ppermute(x, axis, [(i, i ^ mask) for i in range(count)])


def steps(count, first):
    return [0] + [s for s in first if s < count] + [s for s in range(1, count) if s not in first]


SLABS = (2, 3, 1)
CHIPS = (1, 2, 3)


def one_hot(ids, hubs, nodes):
    row = lax.broadcasted_iota(jnp.int32, (hubs, nodes), 0)
    col = lax.broadcasted_iota(jnp.int32, (hubs, nodes), 1)
    want = jnp.zeros((hubs, nodes), jnp.int32)
    for j in range(hubs):
        want = jnp.where(row == j, lax.rem(ids[j], nodes), want)
    return jnp.where(col == want, 1.0, 0.0).astype(BF)


def hub_pick(ids, feats, *refs):
    outs, (ids_s, feats_v, sems) = refs[:-3], refs[-3:]
    layouts, nodes, _ = feats.shape
    copies = fetch([(ids, ids_s)] + [(feats.at[l], feats_v.at[l]) for l in range(layouts)], sems)
    copies[0].wait()
    hot = one_hot(ids_s, outs[0].shape[1], nodes)
    for l in range(layouts):
        copies[1 + l].wait()
        picked = dot(hot, feats_v[l]).astype(BF)
        for out in outs:
            out[l] = picked


def core_rows(ref, lead, core):
    block = ref[lead + (slice(None), pl.ds(core, 1))]
    return block.reshape(block.shape[0] * block.shape[2], block.shape[3])


def adjacency(first, ints, tiles, weight, feats, other, whole, summed, pre_self, chosen, mine, hot, ints_s, adj, dense, sems):
    copies = fetch([(ints, ints_s)], sems)
    slots, tile, _ = tiles.shape
    layouts, chips, cores, share, width = feats.shape
    nodes = chips * cores * share
    core = lax.rem(lax.axis_index("config"), 2)
    adj[...] = jnp.zeros(adj.shape, F32)
    for l in range(2 * layouts):
        chosen[l] = core_rows((feats, other)[l // layouts], (l % layouts,), core)
        pre_self[l] = dot(chosen[l], weight[0])
    copies[0].wait()
    for t in range(slots):

        @pl.when(t < ints_s[first + 2 * slots])
        def _():
            at = pl.ds(pl.multiple_of(ints_s[first + t] * tile, tile), tile)
            block = tiles[t].astype(F32)
            col = ints_s[first + slots + t]
            for s in range(nodes // tile):

                @pl.when(col == s)
                def _():
                    adj[at, pl.ds(s * tile, tile)] += block

    whole[...] = adj[...].astype(BF)
    dense[...] = whole[...].reshape(dense.shape)
    wide = [x[l].reshape(nodes, width) for x in (feats, other) for l in range(layouts)]
    summed[...] = dot(core_rows(dense, (), core), jnp.concatenate(wide, axis=1))
    hot[...] = one_hot(ints_s, mine.shape[1], nodes)
    for l in range(layouts):
        mine[l] = dot(hot[...], wide[l]).astype(BF)


def sage_out(*refs):
    hub_rows, (summed, pre_self, hub_weight, weight) = refs[:2], refs[2:6]
    blocks, (agg, pre, ready) = refs[6:-3], refs[-3:]
    layouts, nodes, width = pre_self.shape
    chips, groups, _, _ = ready.shape
    me = lax.axis_index("config")
    hub_all = jnp.concatenate([x[...] for x in hub_rows], axis=1)
    total = summed[...] + dot(core_rows(hub_weight, (), lax.rem(me, 2)), hub_all)
    acts = []
    for l in range(layouts):
        mine = total[:, l * width : (l + 1) * width].astype(BF)
        agg[l] = mine
        value = pre_self[l] + dot(mine, weight[1])
        pre[l] = value
        act = value / (1.0 + jnp.exp(-value))
        acts.append(act.reshape(chips, groups, SUB, width))
    ready[...] = jnp.concatenate(acts, axis=2).astype(BF)
    for s, block in zip(steps(chips, CHIPS), blocks):
        block[...] = ready[lax.bitwise_xor(me // 2, s)]


def prepare(cot, attn, weight, feats, agg, pre, adj, cot_g, gmix, slope, rows_t, w_back, adj_t):
    layouts, _, width = cot.shape
    groups = cot_g.shape[0]
    adj_t[...] = adj[...].T
    for l in range(feats.shape[0]):
        value = pre[l]
        sig = 1.0 / (1.0 + jnp.exp(-value))
        slope[l] = sig * (1.0 + value * (1.0 - sig))
        at = slice(l * feats.shape[1], (l + 1) * feats.shape[1])
        rows_t[0:width, at] = feats[l].T
        rows_t[width : 2 * width, at] = agg[l].T
    w_back[:, 0:width] = weight[0].T
    w_back[:, width : 2 * width] = weight[1].T
    for p in range(groups // 2):
        block = cot[:, 2 * SUB * p : 2 * SUB * (p + 1), :].astype(F32)
        for h in range(2):
            rows = block[:, SUB * h : SUB * (h + 1), :].reshape(layouts * SUB, width).astype(BF)
            cot_g[2 * p + h] = rows
            gmix[2 * p + h] = dot_nt(rows, attn[3]).astype(BF)


def attend(*refs):
    hidden, ready, grads, pieces = refs[-4:]
    groups, shares, depth, width = hidden.shape
    chips = shares // 2
    blocks, (cot_g, gmix, attn) = refs[:chips], refs[chips : chips + 3]
    outs, (hid_out, mixed_t) = refs[chips + 3 : -6], refs[-6:-4]
    me = lax.axis_index("config")
    rows = shares * depth
    head = width // HEADS
    scale = 1.0 / math.sqrt(head)
    for s, block in zip(steps(chips, CHIPS), blocks):
        for core in range(2):
            hidden[:, lax.bitwise_xor(me, 2 * s + core)] = block[:, core * depth : (core + 1) * depth]
    w_all = jnp.concatenate([attn[0], attn[1], attn[2]], axis=1)
    lane = lax.broadcasted_iota(jnp.int32, (rows, width), 1) // head
    r = lax.broadcasted_iota(jnp.int32, (rows, HEADS * rows), 0)
    c = lax.broadcasted_iota(jnp.int32, (rows, HEADS * rows), 1)
    same = (r % SUB) == (c % SUB)
    zero = jnp.zeros((rows, width), BF)
    gap = jnp.zeros((head, rows), BF)

    def by_head(x):
        return jnp.concatenate([jnp.where(lane == e, x, zero) for e in range(HEADS)], axis=0)

    flat = hidden[...].reshape(groups * rows, width)
    hid_out[...] = flat.reshape(groups, rows, width)
    qkv = dot(flat, w_all).astype(BF)
    inputs = []
    for g in range(groups):
        q, k, v = (qkv[g * rows : (g + 1) * rows, i * width : (i + 1) * width] for i in range(3))
        inputs.append((k, v, k.T, v.T, by_head(q), by_head(gmix[g])))
    products = [(dot_nt(k, qm), dot_nt(v, gm)) for k, v, _, _, qm, gm in inputs]
    weighted = []
    for scores, d_probs in products:
        t = jnp.tanh(scores * (scale / CAP))
        w = jnp.where(same, jnp.exp2(t * (CAP * math.log2(math.e))), 0.0)
        a = w * (1.0 / jnp.sum(w, axis=0, keepdims=True))
        z = a * d_probs
        zs = jnp.sum(z, axis=0, keepdims=True)
        weighted.append((a.astype(BF), ((z - a * zs) * (scale - scale * (t * t))).astype(BF)))
    d_all, mix_t = [], []
    for (k, v, k_t, v_t, qm, gm), (p, ds) in zip(inputs, weighted):
        mix, dq = [], []
        for e in range(HEADS):
            at, span = slice(e * head, (e + 1) * head), slice(e * rows, (e + 1) * rows)
            left = jnp.concatenate(
                [jnp.concatenate([v_t[at], gap], axis=1), jnp.concatenate([gap, k_t[at]], axis=1)], axis=0
            )
            both = dot(left, jnp.concatenate([p[:, span], ds[:, span]], axis=0))
            mix.append(both[:head])
            dq.append(both[head:])
        mix_t.append(jnp.concatenate(mix, axis=0).astype(BF))
        dq = jnp.concatenate(dq, axis=0).astype(BF).T
        d_all.append(jnp.concatenate([dq, dot(ds, qm).astype(BF), dot(p, gm).astype(BF)], axis=1))
    d_all = jnp.concatenate(d_all, axis=0)
    mix_t = jnp.concatenate(mix_t, axis=1)
    mixed_t[...] = mix_t
    cots = cot_g[...].reshape(groups * rows, width)
    back = (cots.astype(F32) + dot_nt(d_all, w_all)).astype(BF).reshape(groups, shares, depth, width)
    for g in range(groups):
        ready[:, g] = back[g]
    total = dot(flat.T, d_all)
    for i in range(3):
        grads[i] = total[:, i * width : (i + 1) * width].astype(BF)
    grads[3] = dot(mix_t, cots).astype(BF)
    shared = grads[...].reshape(chips, -1, width)
    pieces[...] = shared
    count = groups * 2 * depth
    for s, block in zip(steps(chips, CHIPS), outs):
        pair = [ready[lax.bitwise_xor(me, 2 * s + core)] for core in range(2)]
        block[0:count] = jnp.concatenate(pair, axis=1).reshape(count, width)
        block[count:] = pieces[lax.bitwise_xor(me // 2, s)]


def outputs(hidden, mixed_t, attn, _, out, done):
    done[...] = jnp.zeros(done.shape, F32)
    groups, rows, width = hidden.shape
    layouts = rows // SUB
    projected = dot_tn(mixed_t[...], attn[3])
    for p in range(groups // 2):
        pair = []
        for g in (2 * p, 2 * p + 1):
            both = hidden[g].astype(F32) + projected[g * rows : (g + 1) * rows]
            pair.append(both.reshape(layouts, SUB, width))
        out[:, 2 * SUB * p : 2 * SUB * (p + 1), :] = jnp.concatenate(pair, axis=1).astype(BF)


def sage_back(*refs):
    parts, hub_sum = refs[-2:]
    chips, _, layouts, _, width = parts.shape
    blocks, (slope, rows_t, w_back, hub_weight) = refs[:chips], refs[chips : chips + 4]
    mine, theirs, sums, hub_mine = refs[chips + 5 : -2]
    me = lax.axis_index("config")
    nodes = slope.shape[1]
    count = parts.shape[1] * layouts * SUB
    for s, block in zip(steps(chips, CHIPS), blocks):
        parts[lax.bitwise_xor(me // 2, s)] = block[0:count].astype(F32).reshape(parts.shape[1:])
    share = blocks[0].shape[0] - count
    sums[2 * width : 2 * width + share] = sum(block[count:].astype(F32) for block in blocks).astype(BF)
    half = layouts // 2
    grad_pre, grad_agg = [], []
    for l in range(layouts):
        gpre = (parts[:, :, l].reshape(nodes, width) * slope[l]).astype(BF)
        (mine, theirs)[l // half][l % half] = gpre
        grad_pre.append(gpre)
        grad_agg.append(dot(gpre, w_back[:, width : 2 * width]).astype(BF))
    both = dot(rows_t[...], jnp.concatenate(grad_pre, axis=0))
    sums[0 : 2 * width] = both.astype(BF)
    hub_sum[...] = dot_tn(core_rows(hub_weight, (), lax.rem(me, 2)), jnp.concatenate(grad_agg, axis=1))
    slab = lax.axis_index("graph")
    ranks, _, hubs, _ = hub_mine.shape
    pieces = []
    for s in range(ranks):
        at = pl.ds(pl.multiple_of(lax.bitwise_xor(slab, s) * hubs, hubs), hubs)
        for l in range(layouts):
            piece = hub_sum[at, l * width : (l + 1) * width]
            if l < half:
                hub_mine[s, l] = piece.astype(BF)
            else:
                pieces.append(piece)
    sums[2 * width + share :] = jnp.concatenate(pieces, axis=0).astype(BF)


def tile_back(adj_t, w_back, mine, theirs, totals, whole):
    layouts, nodes, width = totals.shape
    core = lax.rem(lax.axis_index("config"), 2)
    for l in range(layouts):
        for part, at in ((mine, core), (theirs, 1 - core)):
            whole[l, :, pl.ds(at, 1)] = part[l].reshape(whole.shape[1], 1, whole.shape[3], width)
    grad_self, grad_agg = [], []
    for l in range(layouts):
        both = dot(whole[l].reshape(nodes, width), w_back[...]).astype(BF)
        grad_self.append(both[:, 0:width])
        grad_agg.append(both[:, width : 2 * width])
    back = dot(adj_t[...], jnp.concatenate(grad_agg, axis=1))
    for l in range(layouts):
        totals[l] = grad_self[l].astype(F32) + back[:, l * width : (l + 1) * width]


def add(a, b):
    return (a[...].astype(F32) + b[...].astype(F32)).astype(BF)


def join(sums, sums_in, hub_mine, sums_out, hub_out):
    count = sums_out.shape[0]
    sums_out[...] = (sums[0:count].astype(F32) + sums_in[0:count].astype(F32)).astype(BF)
    received = sums_in[count:].astype(F32).reshape(hub_out.shape)
    hub_out[...] = (hub_mine[...].astype(F32) + received).astype(BF)


def by_slab(*refs):
    pieces, (rows, work) = refs[:-2], refs[-2:]
    layouts, hubs, width = pieces[0].shape
    slab = lax.axis_index("graph")
    for s, piece in zip(steps(len(pieces), SLABS), pieces):
        at = pl.ds(pl.multiple_of(lax.bitwise_xor(slab, s) * hubs, hubs), hubs)
        for l in range(layouts):
            work[at, l * width : (l + 1) * width] = piece[l].astype(F32)
    rows[...] = work[...].astype(BF)


def finish(hot, totals, hub_own, hub_in, out, work, sems):
    layouts, nodes, width = totals.shape
    summed = [hub_own[0, l].astype(F32) + hub_in[0, l].astype(F32) for l in range(layouts)]
    upper = [x.astype(BF) for x in summed]
    lower = [(x - y.astype(F32)).astype(BF) for x, y in zip(summed, upper)]
    twice = jnp.concatenate([hot[...], hot[...]], axis=0)
    copies = []
    for l in range(layouts):
        added = dot_tn(twice, jnp.concatenate([upper[l], lower[l]], axis=0))
        work[l] = (totals[l] + added).astype(BF)
        copies.append(pltpu.make_async_copy(work.at[l], out.at[l], sems.at[l]))
        copies[l].start()
    for copy in copies:
        copy.wait()


def weights_out(scale, *refs):
    sums, (out, work) = refs[:-2], refs[-2:]
    width = out.shape[1]
    first = 2 * width
    share = sums[0].shape[0] - first
    chip = lax.axis_index("config") // 2
    for s, part in zip(steps(len(sums), CHIPS), sums):
        at = lax.bitwise_xor(chip, s)
        work[at] = part[0:first].astype(F32)
        out[pl.ds(pl.multiple_of(first + at * share, share), share)] = part[first:].astype(F32) * scale
    total = work[0]
    for s in range(1, len(sums)):
        total = total + work[s]
    out[0:first] = total * scale


def exchange(blocks):
    masks = steps(len(blocks), CHIPS)
    return [swapped(block, "config", 2 * s) if s else block for s, block in zip(masks, blocks)]


def local(
    features,
    cotangent,
    sage_weight,
    attn_weight,
    tile_vals,
    tile_dst,
    tile_src,
    tile_count,
    hub_ids,
    hub_weight,
):
    layout_dev, node_dev, width = features.shape
    ranks = lax.axis_size("graph")
    shares = lax.axis_size("config")
    chips = shares // 2
    share = node_dev // shares
    groups = share // SUB
    layouts = layout_dev * shares
    rows = layouts * SUB
    depth = 2 * layout_dev * SUB
    hub_dev = hub_ids.shape[0]
    hubs = hub_weight.shape[1]
    slab = (layout_dev, node_dev, width)
    part = (2 * layout_dev, node_dev // 2, width)
    block = (groups, depth, width)
    dma = pltpu.SemaphoreType.DMA
    ints = jnp.concatenate([hub_ids, tile_dst, tile_src, tile_count])
    ints_s = pltpu.SMEM(ints.shape, jnp.int32)
    hub_weight = hub_weight.reshape(chips, 2, share, hubs)
    by_core = (layout_dev, chips, 2, share, width)

    picked_shape = (layout_dev, hub_dev, width)
    picked = call(
        hub_pick,
        [shape(picked_shape)] * (ranks - 1),
        (hub_ids, features),
        [HBM] * 2,
        [pltpu.SMEM((hub_dev,), jnp.int32), pltpu.VMEM(slab, BF), dma((1 + layout_dev,))],
        limit=WHOLE,
        name="hub_pick",
    )
    pieces = [swapped(x, "graph", s) for s, x in zip(steps(ranks, SLABS)[1:], picked)]
    other = swapped(features, "config", 1)

    adj, summed, pre_self, feats, mine, hot = call(
        functools.partial(adjacency, hub_dev),
        (
            shape((node_dev, node_dev)),
            shape((part[1], part[0] * width), F32),
            shape(part, F32),
            shape(part),
            shape(picked_shape),
            shape((hub_dev, node_dev)),
        ),
        (ints, tile_vals, sage_weight, features.reshape(by_core), other.reshape(by_core)),
        [VMEM] * 5,
        [
            ints_s,
            pltpu.VMEM((node_dev, node_dev), F32),
            pltpu.VMEM((chips, 2, share, node_dev), BF),
            dma((1,)),
        ],
        name="adjacency",
    )

    hub_rows = call(
        by_slab,
        shape((hubs, layout_dev * width)),
        (mine, *pieces),
        [VMEM] * ranks,
        [pltpu.VMEM((hubs, layout_dev * width), F32)],
        micros=0.1,
        name="by_slab",
    )
    hub_rows = (hub_rows, swapped(hub_rows, "config", 1))

    *blocks, agg, pre = call(
        sage_out,
        (*[shape(block)] * chips, shape(part), shape(part, F32)),
        (*hub_rows, summed, pre_self, hub_weight, sage_weight),
        [VMEM] * 6,
        [pltpu.VMEM((chips, *block), BF)],
        name="sage_out",
    )
    hidden_in = exchange(blocks)

    cot_g, gmix, slope, rows_t, w_back, adj_t = call(
        prepare,
        (
            shape((groups, rows, width)),
            shape((groups, rows, width)),
            shape(part, F32),
            shape((2 * width, part[0] * part[1])),
            shape((width, 2 * width)),
            shape((node_dev, node_dev)),
        ),
        (cotangent, attn_weight, sage_weight, feats, agg, pre, adj),
        [VMEM] * 7,
        name="prepare",
    )

    share_rows = attn_weight.shape[0] * width // chips
    back = (groups * depth + share_rows, width)
    *blocks, hidden, mixed_t = call(
        attend,
        (
            *[shape(back)] * chips,
            shape((groups, rows, width)),
            shape((width, groups * rows)),
        ),
        (*hidden_in, cot_g, gmix, attn_weight),
        [VMEM] * (len(hidden_in) + 3),
        [
            pltpu.VMEM((groups, shares, depth // 2, width), BF),
            pltpu.VMEM((shares, groups, depth // 2, width), BF),
            pltpu.VMEM(attn_weight.shape, BF),
            pltpu.VMEM((chips, share_rows, width), BF),
        ],
        micros=4.0,
        name="attend",
    )
    grad_in = exchange(blocks)
    token = shape((SUB, width), F32)
    output, shown = call(
        outputs,
        (shape((layouts, share, width)), token),
        (hidden, mixed_t, attn_weight, grad_in[1]),
        [VMEM] * 3 + [ANY],
        name="outputs",
    )

    hub_shape = (ranks, layout_dev, hub_dev, width)
    mine = (layout_dev, node_dev // 2, width)
    hub_rows = ranks * layout_dev * hub_dev
    mine, theirs, sums, hub_sum = call(
        sage_back,
        (
            shape(mine),
            shape(mine),
            shape((2 * width + share_rows + hub_rows, width)),
            shape(hub_shape),
        ),
        (*grad_in, slope, rows_t, w_back, hub_weight, shown),
        [VMEM] * (chips + 4) + [ANY],
        [
            pltpu.VMEM((chips, groups, 2 * layout_dev, SUB, width), F32),
            pltpu.VMEM((hubs, part[0] * width), F32),
        ],
        name="sage_back",
    )
    theirs = swapped(theirs, "config", 1)
    sums, hub_sum = call(
        join,
        (shape((2 * width + share_rows, width)), shape(hub_shape)),
        (sums, swapped(sums, "config", 1), hub_sum),
        [VMEM] * 3,
        micros=0.1,
        name="join",
    )
    sums = exchange([sums] * chips)
    totals = call(
        tile_back,
        shape(slab, F32),
        (adj_t, w_back, mine, theirs),
        [VMEM] * 4,
        [pltpu.VMEM(by_core, BF)],
        name="tile_back",
    )
    while hub_sum.shape[0] > 2:
        keep = hub_sum.shape[0] // 2
        hub_sum = hub_sum[:keep] + swapped(hub_sum[keep:], "graph", keep)
    hub_in = swapped(hub_sum[1:], "graph", 1)
    count = sage_weight.shape[0] + attn_weight.shape[0]
    weights = call(
        functools.partial(weights_out, 1.0 / math.sqrt(layouts * node_dev)),
        shape((count * width, width), F32),
        sums,
        [VMEM] * chips,
        [pltpu.VMEM((chips, 2 * width, width), F32)],
        name="weights_out",
    )
    grad_features = call(
        finish,
        shape(slab),
        (hot, totals, hub_sum, hub_in),
        [VMEM] * 4,
        [pltpu.VMEM(slab, BF), dma((layout_dev,))],
        outs_at=HBM,
        name="finish",
    )
    return (output, grad_features, weights.reshape(1, count, width, width))


def solution(mesh):
    return jax.shard_map(
        local,
        mesh=mesh,
        in_specs=(
            P("config", "graph", None),
            P(None, ("graph", "config"), None),
            P(),
            P(),
            P("graph", None, None),
            P("graph"),
            P("graph"),
            P("graph"),
            P("graph"),
            P("graph", None),
        ),
        out_specs=(
            P(None, ("graph", "config"), None),
            P("config", "graph", None),
            P("graph", None, None, None),
        ),
        check_vma=False,
    )
```

```python
import functools
import math

import jax
import jax.numpy as jnp
from jax import lax
from jax.experimental import pallas as pl
from jax.experimental.pallas import tpu as pltpu
from jax.sharding import PartitionSpec as P

HEADS = 4
CAP = 20.0
SUB = 8

BF = jnp.bfloat16
F32 = jnp.float32
VMEM = pl.BlockSpec(memory_space=pltpu.VMEM)
ANY = pl.BlockSpec(memory_space=pl.ANY)
HBM = pl.BlockSpec(memory_space=pltpu.HBM)
LIMIT = 24 * 1024 * 1024
WHOLE = 56 * 1024 * 1024


def dot(a, b):
    return jnp.dot(a, b, preferred_element_type=F32)


def dot_nt(a, b):
    return lax.dot_general(a, b, (((1,), (1,)), ((), ())), preferred_element_type=F32)


def dot_tn(a, b):
    return lax.dot_general(a, b, (((0,), (0,)), ((), ())), preferred_element_type=F32)


def shape(dims, kind=BF):
    return jax.ShapeDtypeStruct(dims, kind)


def call(kernel, outs, operands, specs, scratch=(), micros=1.0, limit=LIMIT, outs_at=VMEM, name=None):
    return pl.pallas_call(
        kernel,
        out_shape=outs,
        in_specs=specs,
        out_specs=jax.tree.map(lambda _: outs_at, outs),
        scratch_shapes=list(scratch),
        compiler_params=pltpu.CompilerParams(vmem_limit_bytes=limit),
        cost_estimate=pl.CostEstimate(
            flops=int(micros * 10**9), bytes_accessed=int(micros * 2**21), transcendentals=0
        ),
        name=name,
    )(*operands)


def fetch(pairs, sems):
    copies = [pltpu.make_async_copy(a, b, sems.at[i]) for i, (a, b) in enumerate(pairs)]
    for copy in copies:
        copy.start()
    return copies


def swapped(x, axis, mask):
    count = lax.axis_size(axis)
    return lax.ppermute(x, axis, [(i, i ^ mask) for i in range(count)])


def steps(count, first):
    return [0] + [s for s in first if s < count] + [s for s in range(1, count) if s not in first]


def turned(s):
    return s if s % 4 in (0, 3) else s ^ 3


def met(s, core):
    return s + core * (turned(s) - s)


SLABS = (2, 3, 1)
CHIPS = (1, 2, 3)


def one_hot(ids, hubs, nodes):
    row = lax.broadcasted_iota(jnp.int32, (hubs, nodes), 0)
    col = lax.broadcasted_iota(jnp.int32, (hubs, nodes), 1)
    want = jnp.zeros((hubs, nodes), jnp.int32)
    for j in range(hubs):
        want = jnp.where(row == j, lax.rem(ids[j], nodes), want)
    return jnp.where(col == want, 1.0, 0.0).astype(BF)


def hub_pick(ids, feats, *refs):
    outs, (ids_s, feats_v, sems) = refs[:-3], refs[-3:]
    layouts, nodes, _ = feats.shape
    copies = fetch([(ids, ids_s)] + [(feats.at[l], feats_v.at[l]) for l in range(layouts)], sems)
    copies[0].wait()
    hot = one_hot(ids_s, outs[0].shape[1], nodes)
    for l in range(layouts):
        copies[1 + l].wait()
        picked = dot(hot, feats_v[l]).astype(BF)
        for out in outs:
            out[l] = picked


def core_rows(ref, lead, core):
    block = ref[lead + (slice(None), pl.ds(core, 1))]
    return block.reshape(block.shape[0] * block.shape[2], block.shape[3])


def adjacency(first, ints, tiles, weight, feats, other, whole, summed, pre_self, chosen, mine, hot, ints_s, adj, dense, sems):
    copies = fetch([(ints, ints_s)], sems)
    slots, tile, _ = tiles.shape
    layouts, chips, cores, share, width = feats.shape
    nodes = chips * cores * share
    core = lax.rem(lax.axis_index("config"), 2)
    adj[...] = jnp.zeros(adj.shape, F32)
    for l in range(2 * layouts):
        chosen[l] = core_rows((feats, other)[l // layouts], (l % layouts,), core)
        pre_self[l] = dot(chosen[l], weight[0])
    copies[0].wait()
    for t in range(slots):

        @pl.when(t < ints_s[first + 2 * slots])
        def _():
            at = pl.ds(pl.multiple_of(ints_s[first + t] * tile, tile), tile)
            block = tiles[t].astype(F32)
            col = ints_s[first + slots + t]
            for s in range(nodes // tile):

                @pl.when(col == s)
                def _():
                    adj[at, pl.ds(s * tile, tile)] += block

    whole[...] = adj[...].astype(BF)
    dense[...] = whole[...].reshape(dense.shape)
    wide = [x[l].reshape(nodes, width) for x in (feats, other) for l in range(layouts)]
    summed[...] = dot(core_rows(dense, (), core), jnp.concatenate(wide, axis=1))
    hot[...] = one_hot(ints_s, mine.shape[1], nodes)
    for l in range(layouts):
        mine[l] = dot(hot[...], wide[l]).astype(BF)


def sage_out(*refs):
    hub_rows, (summed, pre_self, hub_weight, weight) = refs[:2], refs[2:6]
    blocks, (agg, pre, ready) = refs[6:-3], refs[-3:]
    layouts, nodes, width = pre_self.shape
    chips, groups, _, _ = ready.shape
    me = lax.axis_index("config")
    hub_all = jnp.concatenate([x[...] for x in hub_rows], axis=1)
    total = summed[...] + dot(core_rows(hub_weight, (), lax.rem(me, 2)), hub_all)
    acts = []
    for l in range(layouts):
        mine = total[:, l * width : (l + 1) * width].astype(BF)
        agg[l] = mine
        value = pre_self[l] + dot(mine, weight[1])
        pre[l] = value
        act = value / (1.0 + jnp.exp(-value))
        acts.append(act.reshape(chips, groups, SUB, width))
    ready[...] = jnp.concatenate(acts, axis=2).astype(BF)
    for s, block in zip(steps(chips, CHIPS), blocks):
        block[...] = ready[lax.bitwise_xor(me // 2, s)]


def prepare(cot, attn, weight, feats, agg, pre, adj, cot_g, gmix, slope, rows_t, w_back, adj_t):
    layouts, _, width = cot.shape
    groups = cot_g.shape[0]
    adj_t[...] = adj[...].T
    for l in range(feats.shape[0]):
        value = pre[l]
        sig = 1.0 / (1.0 + jnp.exp(-value))
        slope[l] = sig * (1.0 + value * (1.0 - sig))
        at = slice(l * feats.shape[1], (l + 1) * feats.shape[1])
        rows_t[0:width, at] = feats[l].T
        rows_t[width : 2 * width, at] = agg[l].T
    w_back[:, 0:width] = weight[0].T
    w_back[:, width : 2 * width] = weight[1].T
    for p in range(groups // 2):
        block = cot[:, 2 * SUB * p : 2 * SUB * (p + 1), :].astype(F32)
        for h in range(2):
            rows = block[:, SUB * h : SUB * (h + 1), :].reshape(layouts * SUB, width).astype(BF)
            cot_g[2 * p + h] = rows
            gmix[2 * p + h] = dot_nt(rows, attn[3]).astype(BF)


def attend(*refs):
    hidden, ready, grads, pieces = refs[-4:]
    groups, shares, depth, width = hidden.shape
    chips = shares // 2
    blocks, (cot_g, gmix, attn) = refs[:chips], refs[chips : chips + 3]
    outs, (hid_out, mixed_t) = refs[chips + 3 : -6], refs[-6:-4]
    me = lax.axis_index("config")
    rows = shares * depth
    head = width // HEADS
    scale = 1.0 / math.sqrt(head)
    for s, block in zip(steps(chips, CHIPS), blocks):
        for core in range(2):
            hidden[:, lax.bitwise_xor(me, 2 * s + core)] = block[:, core * depth : (core + 1) * depth]
    w_all = jnp.concatenate([attn[0], attn[1], attn[2]], axis=1)
    lane = lax.broadcasted_iota(jnp.int32, (rows, width), 1) // head
    r = lax.broadcasted_iota(jnp.int32, (rows, HEADS * rows), 0)
    c = lax.broadcasted_iota(jnp.int32, (rows, HEADS * rows), 1)
    same = (r % SUB) == (c % SUB)
    zero = jnp.zeros((rows, width), BF)
    gap = jnp.zeros((head, rows), BF)

    def by_head(x):
        return jnp.concatenate([jnp.where(lane == e, x, zero) for e in range(HEADS)], axis=0)

    flat = hidden[...].reshape(groups * rows, width)
    hid_out[...] = flat.reshape(groups, rows, width)
    qkv = dot(flat, w_all).astype(BF)
    inputs = []
    for g in range(groups):
        q, k, v = (qkv[g * rows : (g + 1) * rows, i * width : (i + 1) * width] for i in range(3))
        inputs.append((k, v, k.T, v.T, by_head(q), by_head(gmix[g])))
    products = [(dot_nt(k, qm), dot_nt(v, gm)) for k, v, _, _, qm, gm in inputs]
    weighted = []
    for scores, d_probs in products:
        t = jnp.tanh(scores * (scale / CAP))
        w = jnp.where(same, jnp.exp2(t * (CAP * math.log2(math.e))), 0.0)
        a = w * (1.0 / jnp.sum(w, axis=0, keepdims=True))
        z = a * d_probs
        zs = jnp.sum(z, axis=0, keepdims=True)
        weighted.append((a.astype(BF), ((z - a * zs) * (scale - scale * (t * t))).astype(BF)))
    d_all, mix_t = [], []
    for (k, v, k_t, v_t, qm, gm), (p, ds) in zip(inputs, weighted):
        mix, dq = [], []
        for e in range(HEADS):
            at, span = slice(e * head, (e + 1) * head), slice(e * rows, (e + 1) * rows)
            left = jnp.concatenate(
                [jnp.concatenate([v_t[at], gap], axis=1), jnp.concatenate([gap, k_t[at]], axis=1)], axis=0
            )
            both = dot(left, jnp.concatenate([p[:, span], ds[:, span]], axis=0))
            mix.append(both[:head])
            dq.append(both[head:])
        mix_t.append(jnp.concatenate(mix, axis=0).astype(BF))
        dq = jnp.concatenate(dq, axis=0).astype(BF).T
        d_all.append(jnp.concatenate([dq, dot(ds, qm).astype(BF), dot(p, gm).astype(BF)], axis=1))
    d_all = jnp.concatenate(d_all, axis=0)
    mix_t = jnp.concatenate(mix_t, axis=1)
    mixed_t[...] = mix_t
    cots = cot_g[...].reshape(groups * rows, width)
    back = (cots.astype(F32) + dot_nt(d_all, w_all)).astype(BF).reshape(groups, shares, depth, width)
    for g in range(groups):
        ready[:, g] = back[g]
    total = dot(flat.T, d_all)
    for i in range(3):
        grads[i] = total[:, i * width : (i + 1) * width].astype(BF)
    grads[3] = dot(mix_t, cots).astype(BF)
    shared = grads[...].reshape(chips, -1, width)
    pieces[...] = shared
    count = groups * 2 * depth
    for s, block in zip(steps(chips, CHIPS), outs):
        pair = [ready[lax.bitwise_xor(me, 2 * s + core)] for core in range(2)]
        block[0:count] = jnp.concatenate(pair, axis=1).reshape(count, width)
        block[count:] = pieces[lax.bitwise_xor(me // 2, s)]


def outputs(hidden, mixed_t, attn, _, out, done):
    done[...] = jnp.zeros(done.shape, F32)
    groups, rows, width = hidden.shape
    layouts = rows // SUB
    projected = dot_tn(mixed_t[...], attn[3])
    for p in range(groups // 2):
        pair = []
        for g in (2 * p, 2 * p + 1):
            both = hidden[g].astype(F32) + projected[g * rows : (g + 1) * rows]
            pair.append(both.reshape(layouts, SUB, width))
        out[:, 2 * SUB * p : 2 * SUB * (p + 1), :] = jnp.concatenate(pair, axis=1).astype(BF)


def sage_back(*refs):
    parts, hub_sum = refs[-2:]
    chips, _, layouts, _, width = parts.shape
    blocks, (slope, rows_t, w_back, hub_weight) = refs[:chips], refs[chips : chips + 4]
    mine, theirs, sums, hub_mine, hub_theirs = refs[chips + 5 : -2]
    me = lax.axis_index("config")
    nodes = slope.shape[1]
    count = parts.shape[1] * layouts * SUB
    for s, block in zip(steps(chips, CHIPS), blocks):
        parts[lax.bitwise_xor(me // 2, s)] = block[0:count].astype(F32).reshape(parts.shape[1:])
    sums[2 * width :] = sum(block[count:].astype(F32) for block in blocks).astype(BF)
    half = layouts // 2
    grad_pre, grad_agg = [], []
    for l in range(layouts):
        gpre = (parts[:, :, l].reshape(nodes, width) * slope[l]).astype(BF)
        (mine, theirs)[l // half][l % half] = gpre
        grad_pre.append(gpre)
        grad_agg.append(dot(gpre, w_back[:, width : 2 * width]).astype(BF))
    both = dot(rows_t[...], jnp.concatenate(grad_pre, axis=0))
    sums[0 : 2 * width] = both.astype(BF)
    hub_sum[...] = dot_tn(core_rows(hub_weight, (), lax.rem(me, 2)), jnp.concatenate(grad_agg, axis=1))
    slab = lax.axis_index("graph")
    ranks, _, hubs, _ = hub_mine.shape
    for s in range(ranks):
        at = pl.ds(pl.multiple_of(lax.bitwise_xor(slab, s) * hubs, hubs), hubs)
        for l in range(layouts):
            (hub_mine, hub_theirs)[l // half][s, l % half] = hub_sum[at, l * width : (l + 1) * width].astype(BF)


def tile_back(adj_t, w_back, mine, theirs, totals, whole):
    layouts, nodes, width = totals.shape
    core = lax.rem(lax.axis_index("config"), 2)
    for l in range(layouts):
        for part, at in ((mine, core), (theirs, 1 - core)):
            whole[l, :, pl.ds(at, 1)] = part[l].reshape(whole.shape[1], 1, whole.shape[3], width)
    grad_self, grad_agg = [], []
    for l in range(layouts):
        both = dot(whole[l].reshape(nodes, width), w_back[...]).astype(BF)
        grad_self.append(both[:, 0:width])
        grad_agg.append(both[:, width : 2 * width])
    back = dot(adj_t[...], jnp.concatenate(grad_agg, axis=1))
    for l in range(layouts):
        totals[l] = grad_self[l].astype(F32) + back[:, l * width : (l + 1) * width]


def add(a, b):
    return (a[...].astype(F32) + b[...].astype(F32)).astype(BF)


def join(*refs):
    pairs = len(refs) // 3
    for i in range(pairs):
        refs[2 * pairs + i][...] = add(refs[2 * i], refs[2 * i + 1])


def joined(*operands):
    return call(
        join,
        [shape(x.shape) for x in operands[::2]],
        operands,
        [VMEM] * len(operands),
        micros=0.1,
        name="join",
    )


def by_slab(*refs):
    pieces, (rows, work) = refs[:-2], refs[-2:]
    layouts, hubs, width = pieces[0].shape
    slab = lax.axis_index("graph")
    for s, piece in zip(steps(len(pieces), SLABS), pieces):
        at = pl.ds(pl.multiple_of(lax.bitwise_xor(slab, s) * hubs, hubs), hubs)
        for l in range(layouts):
            work[at, l * width : (l + 1) * width] = piece[l].astype(F32)
    rows[...] = work[...].astype(BF)


def finish(hot, totals, hub_own, hub_in, out, work, sems):
    layouts, nodes, width = totals.shape
    summed = [hub_own[0, l].astype(F32) + hub_in[0, l].astype(F32) for l in range(layouts)]
    upper = [x.astype(BF) for x in summed]
    lower = [(x - y.astype(F32)).astype(BF) for x, y in zip(summed, upper)]
    twice = jnp.concatenate([hot[...], hot[...]], axis=0)
    copies = []
    for l in range(layouts):
        added = dot_tn(twice, jnp.concatenate([upper[l], lower[l]], axis=0))
        work[l] = (totals[l] + added).astype(BF)
        copies.append(pltpu.make_async_copy(work.at[l], out.at[l], sems.at[l]))
        copies[l].start()
    for copy in copies:
        copy.wait()


def weights_out(scale, *refs):
    sums, (out, work) = refs[:-2], refs[-2:]
    width = out.shape[1]
    first = 2 * width
    share = sums[0].shape[0] - first
    chip = lax.axis_index("config") // 2
    for s, part in zip(steps(len(sums), CHIPS), sums):
        at = lax.bitwise_xor(chip, met(s, lax.rem(lax.axis_index("config"), 2)))
        work[at] = part[0:first].astype(F32)
        out[pl.ds(pl.multiple_of(first + at * share, share), share)] = part[first:].astype(F32) * scale
    total = work[0]
    for s in range(1, len(sums)):
        total = total + work[s]
    out[0:first] = total * scale


def exchange(blocks, apart=False):
    masks = steps(len(blocks), CHIPS)
    if not apart or len(blocks) < 4:
        return [swapped(block, "config", 2 * s) if s else block for s, block in zip(masks, blocks)]
    count = lax.axis_size("config")
    return [
        lax.ppermute(block, "config", [(i, i ^ 2 * (turned(s) if i % 2 else s)) for i in range(count)]) if s else block
        for s, block in zip(masks, blocks)
    ]


def local(
    features,
    cotangent,
    sage_weight,
    attn_weight,
    tile_vals,
    tile_dst,
    tile_src,
    tile_count,
    hub_ids,
    hub_weight,
):
    layout_dev, node_dev, width = features.shape
    ranks = lax.axis_size("graph")
    shares = lax.axis_size("config")
    chips = shares // 2
    share = node_dev // shares
    groups = share // SUB
    layouts = layout_dev * shares
    rows = layouts * SUB
    depth = 2 * layout_dev * SUB
    hub_dev = hub_ids.shape[0]
    hubs = hub_weight.shape[1]
    slab = (layout_dev, node_dev, width)
    part = (2 * layout_dev, node_dev // 2, width)
    block = (groups, depth, width)
    dma = pltpu.SemaphoreType.DMA
    ints = jnp.concatenate([hub_ids, tile_dst, tile_src, tile_count])
    ints_s = pltpu.SMEM(ints.shape, jnp.int32)
    hub_weight = hub_weight.reshape(chips, 2, share, hubs)
    by_core = (layout_dev, chips, 2, share, width)

    picked_shape = (layout_dev, hub_dev, width)
    picked = call(
        hub_pick,
        [shape(picked_shape)] * (ranks - 1),
        (hub_ids, features),
        [HBM] * 2,
        [pltpu.SMEM((hub_dev,), jnp.int32), pltpu.VMEM(slab, BF), dma((1 + layout_dev,))],
        limit=WHOLE,
        name="hub_pick",
    )
    pieces = [swapped(x, "graph", s) for s, x in zip(steps(ranks, SLABS)[1:], picked)]
    other = swapped(features, "config", 1)

    adj, summed, pre_self, feats, mine, hot = call(
        functools.partial(adjacency, hub_dev),
        (
            shape((node_dev, node_dev)),
            shape((part[1], part[0] * width), F32),
            shape(part, F32),
            shape(part),
            shape(picked_shape),
            shape((hub_dev, node_dev)),
        ),
        (ints, tile_vals, sage_weight, features.reshape(by_core), other.reshape(by_core)),
        [VMEM] * 5,
        [
            ints_s,
            pltpu.VMEM((node_dev, node_dev), F32),
            pltpu.VMEM((chips, 2, share, node_dev), BF),
            dma((1,)),
        ],
        name="adjacency",
    )

    hub_rows = call(
        by_slab,
        shape((hubs, layout_dev * width)),
        (mine, *pieces),
        [VMEM] * ranks,
        [pltpu.VMEM((hubs, layout_dev * width), F32)],
        micros=0.1,
        name="by_slab",
    )
    hub_rows = (hub_rows, swapped(hub_rows, "config", 1))

    *blocks, agg, pre = call(
        sage_out,
        (*[shape(block)] * chips, shape(part), shape(part, F32)),
        (*hub_rows, summed, pre_self, hub_weight, sage_weight),
        [VMEM] * 6,
        [pltpu.VMEM((chips, *block), BF)],
        name="sage_out",
    )
    hidden_in = exchange(blocks)

    cot_g, gmix, slope, rows_t, w_back, adj_t = call(
        prepare,
        (
            shape((groups, rows, width)),
            shape((groups, rows, width)),
            shape(part, F32),
            shape((2 * width, part[0] * part[1])),
            shape((width, 2 * width)),
            shape((node_dev, node_dev)),
        ),
        (cotangent, attn_weight, sage_weight, feats, agg, pre, adj),
        [VMEM] * 7,
        name="prepare",
    )

    share_rows = attn_weight.shape[0] * width // chips
    back = (groups * depth + share_rows, width)
    *blocks, hidden, mixed_t = call(
        attend,
        (
            *[shape(back)] * chips,
            shape((groups, rows, width)),
            shape((width, groups * rows)),
        ),
        (*hidden_in, cot_g, gmix, attn_weight),
        [VMEM] * (len(hidden_in) + 3),
        [
            pltpu.VMEM((groups, shares, depth // 2, width), BF),
            pltpu.VMEM((shares, groups, depth // 2, width), BF),
            pltpu.VMEM(attn_weight.shape, BF),
            pltpu.VMEM((chips, share_rows, width), BF),
        ],
        micros=4.0,
        name="attend",
    )
    grad_in = exchange(blocks)
    token = shape((SUB, width), F32)
    output, shown = call(
        outputs,
        (shape((layouts, share, width)), token),
        (hidden, mixed_t, attn_weight, grad_in[1]),
        [VMEM] * 3 + [ANY],
        name="outputs",
    )

    hub_shape = (ranks, layout_dev, hub_dev, width)
    mine = (layout_dev, node_dev // 2, width)
    mine, theirs, sums, hub_sum, hub_theirs = call(
        sage_back,
        (shape(mine), shape(mine), shape((2 * width + share_rows, width)), shape(hub_shape), shape(hub_shape)),
        (*grad_in, slope, rows_t, w_back, hub_weight, shown),
        [VMEM] * (chips + 4) + [ANY],
        [
            pltpu.VMEM((chips, groups, 2 * layout_dev, SUB, width), F32),
            pltpu.VMEM((hubs, part[0] * width), F32),
        ],
        name="sage_back",
    )
    hub_in = swapped(hub_theirs, "config", 1)
    theirs = swapped(theirs, "config", 1)
    sums, hub_sum = joined(sums, swapped(sums, "config", 1), hub_sum, hub_in)
    sums = exchange([sums] * chips, apart=True)
    totals = call(
        tile_back,
        shape(slab, F32),
        (adj_t, w_back, mine, theirs),
        [VMEM] * 4,
        [pltpu.VMEM(by_core, BF)],
        name="tile_back",
    )
    while hub_sum.shape[0] > 2:
        keep = hub_sum.shape[0] // 2
        hub_sum = hub_sum[:keep] + swapped(hub_sum[keep:], "graph", keep)
    hub_in = swapped(hub_sum[1:], "graph", 1)
    count = sage_weight.shape[0] + attn_weight.shape[0]
    weights = call(
        functools.partial(weights_out, 1.0 / math.sqrt(layouts * node_dev)),
        shape((count * width, width), F32),
        sums,
        [VMEM] * chips,
        [pltpu.VMEM((chips, 2 * width, width), F32)],
        name="weights_out",
    )
    grad_features = call(
        finish,
        shape(slab),
        (hot, totals, hub_sum, hub_in),
        [VMEM] * 4,
        [pltpu.VMEM(slab, BF), dma((layout_dev,))],
        outs_at=HBM,
        name="finish",
    )
    return (output, grad_features, weights.reshape(1, count, width, width))


def solution(mesh):
    return jax.shard_map(
        local,
        mesh=mesh,
        in_specs=(
            P("config", "graph", None),
            P(None, ("graph", "config"), None),
            P(),
            P(),
            P("graph", None, None),
            P("graph"),
            P("graph"),
            P("graph"),
            P("graph"),
            P("graph", None),
        ),
        out_specs=(
            P(None, ("graph", "config"), None),
            P("config", "graph", None),
            P("graph", None, None, None),
        ),
        check_vma=False,
    )
```
